128 devices in a mesh: range: 128 (over z, x, y, core).
Axes of the slice: x: 4, y: 4, z: 4, core: 2. Of those that a mesh axis runs over, the one named last changes fastest.
Arguments:
- raw: bfloat16 [2, 64, 32, 32768], P(None, None, None, 'range'), may hold values from -40 to 40
- replica: bfloat16 [2, 128], replicated, may hold values from -1 to 1
- det_bin: int32 [16384], P('range'), may hold values from 0 to 31
- det_block: int32 [16384], P('range'), may hold values from 0 to 1
- det_beam: int32 [16384], P('range'), may hold values from 0 to 7
- det_owner: int32 [16384, 1], P('range'), may hold values from 0 to 127; in each aligned block of 128 rows (0 to 127, 128 to 255, ...) at most 2 rows name the same one
Outputs:
- tracked: float32 [32768, 256], P('range')
The draws below stay inside these ranges and needn't reach their ends.
Inputs may be any that keep to these rules, and one draw needn't show every extreme that they name: `det_owner`: in each slab's detections no owner appears more than 2 times; some owner appears exactly 2 times.
All inputs are finite; a program needn't handle non-finite values.
Results may differ from the reference program's by a relative error of at most 0.025.
Values may be sent and summed in bfloat16 or wider, within the bound.
A program may use at most 256 MiB of HBM per device.

```python
import math
import jax
import jax.numpy as jnp
import numpy as np
from jax import lax

C = 64
P_SIZE = 32
TAPS = 128
BLOCK = 128
G_DEV = 256
BEAMS = 8
CAP = 2
DET_DEV = 128
NDET = 16384
NG = 32768
N_RANGE = 128


def draw_raw(key, part):
    keys = jax.random.split(jax.random.fold_in(key, 17), 4)
    slabs = NG // G_DEV
    slab_of = jnp.arange(NG).astype(jnp.int32) // G_DEV
    phases = jax.random.uniform(keys[0], (slabs,), minval=-1.0, maxval=1.0)
    freqs = jax.random.uniform(keys[1], (slabs,), minval=0.0, maxval=float(P_SIZE))
    gain = jax.random.truncated_normal(keys[2], -4.0, 4.0, (2, NG))
    noise = jax.random.truncated_normal(keys[3], -6.0, 6.0, (2, C, P_SIZE, NG))
    chan = jnp.arange(C).astype(jnp.float32)[:, None, None]
    pulse = jnp.arange(P_SIZE).astype(jnp.float32)[None, :, None]
    angle = math.pi * phases[slab_of][None, None, :] * chan + 2.0 * math.pi / P_SIZE * freqs[slab_of][None, None, :] * pulse
    cosine = jnp.cos(angle)
    sine = jnp.sin(angle)
    real_part = 4.0 * (gain[0] * cosine - gain[1] * sine)
    imag_part = 4.0 * (gain[0] * sine + gain[1] * cosine)
    return (noise + jnp.stack([real_part, imag_part], 0)).astype(jnp.bfloat16)


def plant(result, key, least, top_value):
    spot = [jax.random.randint(jax.random.fold_in(key, axis), (), 0, length) for axis, length in enumerate(result.shape)]
    widest = result.shape.index(max(result.shape))
    beside = spot[:widest] + [(spot[widest] + 1) % result.shape[widest]] + spot[widest + 1:]
    return result.at[tuple(spot)].set(least).at[tuple(beside)].set(top_value)


def assign_block(key, own, number, rows, count, top, limit, slope):
    ranking = jax.random.permutation(key, count)
    packed, usual = shares(count, rows * top, limit, slope, True), shares(count, rows * top, limit, slope, False)
    places = jnp.arange(count)

    def named(sizes, turn):
        used = int((sizes > 0).sum())
        fixed = max(1, used // 4)
        passed = fixed + (places - fixed + turn * (used - fixed)) % max(1, count - fixed)
        return jnp.zeros((count,), jnp.int32).at[ranking[jnp.where(places < fixed, places, passed)]].set(jnp.asarray(sizes, jnp.int32))

    sizes = jnp.where(number % 4 == 0, named(packed, number // 4), named(usual, number - number // 4 - 1))
    mixed = jax.random.permutation(jax.random.fold_in(own, 3), count)
    donor, taker = mixed[0:count // 2 * 2:2], mixed[1:count // 2 * 2:2]
    slack = jnp.minimum(sizes[donor] - 1, limit - sizes[taker]) // 2
    slack = jnp.where((donor == ranking[0]) | (taker == ranking[0]) | (sizes[taker] == 0), 0, jnp.maximum(slack, 0))
    passed = jax.random.randint(jax.random.fold_in(own, 4), (count // 2,), 0, 1 << 20) % (slack + 1)
    sizes = sizes.at[donor].add(-passed).at[taker].add(passed)
    items = jnp.searchsorted(jnp.cumsum(sizes), jnp.arange(rows * top), side="right").astype(jnp.int32)
    table = items.reshape(top, rows).T
    table = table[jax.random.permutation(jax.random.fold_in(own, 1), rows)]
    turn = jax.random.randint(jax.random.fold_in(own, 2), (rows, 1), 0, top)
    return jnp.take_along_axis(table, (jnp.arange(top)[None, :] + turn) % top, axis=1)


def shares(number_of, total, limit, skew, full):
    loads = [(1 << 20) // math.isqrt(grade ** skew) + 1 for grade in range(1, number_of + 1)]
    largest = limit if full else min(limit, max(-(-total // number_of), total * loads[0] // sum(loads)))
    least = 1 if total - largest >= number_of - 1 else 0
    holding, rest = [largest] + [least] * (number_of - 1), total - largest - least * (number_of - 1)
    while rest > 0:
        candidates = [i for i in range(1, number_of) if holding[i] < largest] or [i for i in range(1, number_of) if holding[i] < limit]
        whole, budget = sum([loads[i] for i in candidates]), rest
        for i in candidates:
            more = min(limit - holding[i], max(1, budget * loads[i] // whole), rest)
            holding[i] = holding[i] + more
            rest = rest - more
    return np.array(holding)


def scatter_about(stream_key, extent, width, limit, kind=jnp.bfloat16):
    values = width * jax.random.normal(stream_key, extent, jnp.float32)
    return jnp.clip(values, min=-limit, max=limit).astype(kind)


def setup_inputs(seed: int = 0) -> dict:
    arg_keys = jax.random.split(jax.random.key(seed), 7)
    raw = draw_raw(jax.random.fold_in(arg_keys[6], 71), 0)
    replica = scatter_about(arg_keys[1], (2, TAPS), ((2 * TAPS) ** -0.5), 1.0)
    det_bin = plant(jax.random.randint(arg_keys[2], (NDET,), 0, P_SIZE), jax.random.fold_in(arg_keys[2], 1), 0, P_SIZE - 1).astype(jnp.int32)
    det_block = plant(jax.random.randint(arg_keys[3], (NDET,), 0, G_DEV // BLOCK), jax.random.fold_in(arg_keys[3], 1), 0, (G_DEV // BLOCK) - 1).astype(jnp.int32)
    det_beam = plant(jax.random.randint(arg_keys[4], (NDET,), 0, BEAMS), jax.random.fold_in(arg_keys[4], 1), 0, BEAMS - 1).astype(jnp.int32)
    det_owner_keys = jax.random.split(jax.random.fold_in(arg_keys[5], 1), NDET // DET_DEV)
    det_owner_turns = jax.random.permutation(jax.random.fold_in(arg_keys[5], 3), NDET // DET_DEV)
    det_owner = jax.vmap(lambda own, number: assign_block(jax.random.fold_in(arg_keys[5], 2), own, number, DET_DEV, N_RANGE, 1, CAP, 2))(det_owner_keys, det_owner_turns).reshape((NDET, 1))
    return {"raw": raw, "replica": replica, "det_bin": det_bin, "det_block": det_block, "det_beam": det_beam, "det_owner": det_owner}


def toeplitz(replica):
    taps = replica.shape[1]
    zero = jnp.zeros((2, taps), replica.dtype)
    padded = jnp.concatenate([zero, replica, zero], axis=1)

    def column(shift):
        return lax.dynamic_slice_in_dim(padded, (taps - shift).astype(jnp.int32), 2 * taps, 1)
    cols = jax.vmap(column)(jnp.arange(taps).astype(jnp.int32))
    real_part = cols[:, 0, :].T
    imag_part = cols[:, 1, :].T
    return jnp.stack([jnp.stack([real_part, -imag_part], 1), jnp.stack([imag_part, real_part], 1)], 0)

def dft_table(pulses):
    index = jnp.arange(pulses).astype(jnp.int32)
    angle = 2.0 * math.pi / pulses * (index[:, None] * index[None, :] % pulses).astype(jnp.float32)
    cosine = jnp.cos(angle)
    sine = jnp.sin(angle)
    table = jnp.stack([jnp.stack([cosine, -sine], 1), jnp.stack([sine, cosine], 1)], 0)
    return (table * pulses ** (-0.5)).astype(jnp.bfloat16)

def compress(extended, replica):
    taps = replica.shape[1]
    gates = extended.shape[3] - taps
    shape = extended.shape[:3] + (gates // taps, taps)
    current = extended[..., :gates].reshape(shape)
    following = extended[..., taps:].reshape(shape)
    paired = jnp.concatenate([current, following], axis=4).astype(jnp.float32)
    kernel = toeplitz(replica).astype(jnp.float32)
    out = jnp.einsum('icpbn,inom->ocpbm', paired, kernel, precision=lax.Precision.HIGHEST)
    return out.reshape(extended.shape[:3] + (gates,)).astype(jnp.bfloat16)

def doppler(compressed):
    table = dft_table(compressed.shape[2]).astype(jnp.float32)
    out = jnp.einsum('icpg,ipod->docg', compressed.astype(jnp.float32), table, precision=lax.Precision.HIGHEST)
    return out.astype(jnp.bfloat16)

def cross_blocks(spectra):
    bins, _, chans, gates = spectra.shape
    flat = spectra.reshape(bins, 2 * chans, gates).astype(jnp.float32)
    parts = []
    for delta in range(3):
        parts.append(jnp.einsum('erg,esg->ers', flat, jnp.roll(flat, -delta, 0), precision=lax.Precision.HIGHEST))
    return jnp.stack(parts, 0)

def to_complex(blocks):
    bins = blocks.shape[1]
    chans = blocks.shape[2] // 2
    split = blocks.reshape(3, bins, 2, chans, 2, chans)
    real_part = split[:, :, 0, :, 0, :] + split[:, :, 1, :, 1, :]
    imag_part = split[:, :, 1, :, 0, :] - split[:, :, 0, :, 1, :]
    return jnp.stack([real_part, imag_part], 2)

def weights(cross, total, beams, chosen):
    cross = cross / jnp.float32(total)
    bins = cross.shape[1]
    chans = cross.shape[3]
    count = chosen.shape[0]
    rows_real = []
    rows_imag = []
    for left in range(3):
        row_real = []
        row_imag = []
        for right in range(3):
            if right >= left:
                picked = cross[right - left][(chosen - 1 + left) % bins]
                row_real.append(picked[:, 0])
                row_imag.append(picked[:, 1])
            else:
                picked = cross[left - right][(chosen - 1 + right) % bins]
                row_real.append(jnp.swapaxes(picked[:, 0], 1, 2))
                row_imag.append(-jnp.swapaxes(picked[:, 1], 1, 2))
        rows_real.append(jnp.concatenate(row_real, 2))
        rows_imag.append(jnp.concatenate(row_imag, 2))
    cov_real = jnp.concatenate(rows_real, 1)
    cov_imag = jnp.concatenate(rows_imag, 1)
    embedded = jnp.concatenate([jnp.concatenate([cov_real, -cov_imag], 2), jnp.concatenate([cov_imag, cov_real], 2)], 1)
    lower = jnp.linalg.cholesky(embedded)
    chan_index = jnp.arange(chans).astype(jnp.float32)
    sines = -0.8 + 1.6 * jnp.arange(beams).astype(jnp.float32) / (beams - 1)
    angle = math.pi * chan_index[:, None] * sines[None, :]
    empty = jnp.zeros((chans, beams), jnp.float32)
    steer = jnp.concatenate([empty, jnp.cos(angle), empty, empty, jnp.sin(angle), empty], 0)
    steer = jnp.broadcast_to(steer, (count,) + steer.shape)
    middle = lax.linalg.triangular_solve(lower, steer, left_side=True, lower=True)
    solved = lax.linalg.triangular_solve(lower, middle, left_side=True, lower=True, transpose_a=True)
    quad = lax.optimization_barrier(jnp.sum(steer * solved, axis=1))
    return (solved / jnp.sqrt(quad)[:, None, :]).astype(jnp.bfloat16)

def beam_blocks(spectra, weight, det_bin, det_block, det_beam, block):
    bins, _, chans, _ = spectra.shape

    def single(bin_id, block_id, beam_id):
        start = (block_id * block).astype(jnp.int32)
        zero = jnp.int32(0)
        pieces = []
        for offset in range(3):
            band = ((bin_id - 1 + offset) % bins).astype(jnp.int32)
            pieces.append(lax.dynamic_slice(spectra, (band, zero, zero, start), (1, 2, chans, block)))
        window = jnp.concatenate(pieces, 0).astype(jnp.float32)
        vector = weight[bin_id, :, beam_id].reshape(2, 3, chans).astype(jnp.float32)
        hp = lax.Precision.HIGHEST
        real_out = jnp.einsum('oc,ocg->g', vector[0], window[:, 0], precision=hp) + jnp.einsum('oc,ocg->g', vector[1], window[:, 1], precision=hp)
        imag_out = jnp.einsum('oc,ocg->g', vector[0], window[:, 1], precision=hp) - jnp.einsum('oc,ocg->g', vector[1], window[:, 0], precision=hp)
        return jnp.concatenate([real_out, imag_out], 0)
    return jax.vmap(single)(det_bin, det_block, det_beam)

def reference(raw, replica, det_bin, det_block, det_beam, det_owner):
    slabs = N_RANGE
    padded = jnp.concatenate([raw, jnp.zeros((2, C, P_SIZE, TAPS), raw.dtype)], axis=3)

    def advance(total, slab):
        extended = lax.dynamic_slice_in_dim(padded, slab * G_DEV, G_DEV + TAPS, 3)
        spectra = doppler(compress(extended, replica))
        return (total + cross_blocks(spectra), spectra)
    start = jnp.zeros((3, P_SIZE, 2 * C, 2 * C), jnp.float32)
    blocks, spectra_all = lax.scan(advance, start, jnp.arange(slabs).astype(jnp.int32))
    weight = weights(to_complex(blocks), NG, BEAMS, jnp.arange(P_SIZE).astype(jnp.int32))
    beams = jax.vmap(lambda s, a, b, c: beam_blocks(s, weight, a, b, c, BLOCK))(spectra_all, det_bin.reshape(slabs, -1), det_block.reshape(slabs, -1), det_beam.reshape(slabs, -1))
    owners = det_owner[:, 0].reshape(slabs, -1)
    index = jnp.arange(owners.shape[1]).astype(jnp.int32)
    earlier = (owners[:, None, :] == owners[:, :, None]) & (index[None, None, :] < index[None, :, None])
    ranks = lax.optimization_barrier(jnp.sum(earlier.astype(jnp.int32), axis=2))
    source = jnp.arange(slabs).astype(jnp.int32)[:, None]
    target = owners * (owners.shape[1] * CAP) + source * CAP + ranks
    tracked = jnp.zeros((NDET * CAP, 2 * BLOCK), jnp.float32)
    return tracked.at[target.reshape(-1)].set(beams.reshape(-1, 2 * BLOCK))
```

```python
import functools
import math

import jax
import jax.numpy as jnp
import numpy as np
from jax import lax
from jax.experimental import pallas as pl
from jax.experimental.pallas import tpu as pltpu
from jax.sharding import PartitionSpec as P

C = 64
PULSES = 32
TAPS = 128
GATES = 256
BEAMS = 8
F32 = jnp.float32
BF16 = jnp.bfloat16
MESH = pl.DeviceIdType.MESH
VMEM = pl.BlockSpec(memory_space=pltpu.VMEM)
NT = (((1,), (1,)), ((), ()))
LIMIT = 48 * 1024 * 1024


def dft_matrix():
    index = np.arange(PULSES)
    angle = 2.0 * math.pi / PULSES * (index[:, None] * index[None, :] % PULSES)
    scale = PULSES**-0.5
    real = np.cos(angle) * scale
    imag = -np.sin(angle) * scale
    eye = np.eye(8)
    kr = np.einsum("pd,ab->dabp", real, eye).reshape(256, 256)
    ki = np.einsum("pd,ab->dabp", imag, eye).reshape(256, 256)
    full = np.concatenate([np.concatenate([kr, -ki], 1), np.concatenate([ki, kr], 1)], 0)
    return full.astype(jnp.bfloat16)


def steer_rows():
    sines = -0.8 + 1.6 * np.arange(BEAMS, dtype=np.float32) / np.float32(BEAMS - 1)
    angle = (math.pi * np.arange(C, dtype=np.float32)[None, :] * sines[:, None]).astype(np.float32)
    return np.concatenate([np.cos(angle), -np.sin(angle)], 1).astype(np.float32)


def front_kernel(raw_ref, halo_ref, rep_ref, dft_ref, s_ref, p_ref, tz):
    def band(v):
        wide = jnp.concatenate(
            [jnp.broadcast_to(v, (TAPS, TAPS)), jnp.zeros((TAPS, TAPS), F32)], axis=1
        )
        return pltpu.roll(wide, 0, 1, stride=1, stride_axis=0).T

    rep = rep_ref[...].astype(F32)
    tr = band(rep[0:1])
    ti = band(rep[1:2])
    tz[0:256, 0:128] = tr.astype(BF16)
    tz[0:256, 128:256] = (-ti).astype(BF16)
    tz[256:512, 0:128] = ti.astype(BF16)
    tz[256:512, 128:256] = tr.astype(BF16)

    def group(first):
        at = pl.ds(first, 8)
        xr = raw_ref[0, at].reshape(256, 256)
        xi = raw_ref[1, at].reshape(256, 256)
        hr = halo_ref[0, at].reshape(256, 128)
        hi = halo_ref[1, at].reshape(256, 128)
        l0 = jnp.concatenate([xr, xi], axis=1)
        l1 = jnp.concatenate([xr[:, 128:], hr, xi[:, 128:], hi], axis=1)
        y0 = jnp.dot(l0, tz[...], preferred_element_type=F32).astype(BF16)
        y1 = jnp.dot(l1, tz[...], preferred_element_type=F32).astype(BF16)
        y = jnp.concatenate(
            [
                jnp.concatenate([y0[:, :128], y1[:, :128]], axis=1),
                jnp.concatenate([y0[:, 128:], y1[:, 128:]], axis=1),
            ],
            axis=0,
        )
        out = jnp.dot(dft_ref[...], y, preferred_element_type=F32)
        return out[:256].reshape(32, 8, 256), out[256:].reshape(32, 8, 256)

    def pair(i, carry):
        first = pl.multiple_of(i * 16, 16)
        ar, ai = group(first)
        br, bi = group(first + 8)
        s_ref[2:34, pl.ds(first, 16), 0:256] = jnp.concatenate([ar, br], axis=1).astype(BF16)
        s_ref[2:34, pl.ds(first, 16), 256:512] = jnp.concatenate([ai, bi], axis=1).astype(BF16)
        return carry

    lax.fori_loop(0, 4, pair, 0)
    s_ref[0:2] = s_ref[32:34]
    s_ref[34] = s_ref[2]

    lane = lax.broadcasted_iota(jnp.int32, (32, 128), 1)
    row = lax.broadcasted_iota(jnp.int32, (32, 128), 0)
    low = lane < 64

    def cross(f, carry):
        lhs = s_ref[pl.ds(f, 3)].reshape(192, 512)
        cur = s_ref[f + 2]
        rot = jnp.concatenate([-cur[:, 256:], cur[:, :256]], axis=1)
        rhs = jnp.concatenate([cur, rot], axis=0)
        prod = lax.dot_general(lhs, rhs, NT, preferred_element_type=F32)
        d0 = prod[128:192]
        sw = pltpu.roll(d0, 64, 1)
        top = jnp.where(row >= lane, d0[:32], sw[:32])
        bottom = jnp.where(row + 32 >= lane - 64, sw[32:], d0[32:])
        packed = jnp.where(low, top, bottom)
        other = (f // 2) % 4 * 8 + f // 8 * 2 + f % 2
        for h in range(2):
            pos = f if h == 0 else other
            for q in range(2):
                a = 32 * h + 16 * q
                p_ref[h, pos, 40 * q : 40 * q + 16] = prod[a : a + 16]
                p_ref[h, pos, 40 * q + 16 : 40 * q + 32] = prod[64 + a : 80 + a]
                p_ref[h, pos, 40 * q + 32 : 40 * q + 40] = packed[a // 2 : a // 2 + 8]
        return carry

    lax.fori_loop(0, 32, cross, 0)


def front(raw, halo, replica):
    return pl.pallas_call(
        front_kernel,
        out_shape=(
            jax.ShapeDtypeStruct((35, 64, 512), BF16),
            jax.ShapeDtypeStruct((2, 32, 80, 128), F32),
        ),
        in_specs=[VMEM] * 4,
        out_specs=(VMEM, VMEM),
        scratch_shapes=[pltpu.VMEM((512, 256), BF16)],
        compiler_params=pltpu.CompilerParams(vmem_limit_bytes=LIMIT),
        name="front",
    )(raw, halo, replica, jnp.asarray(dft_matrix()))


def remote(src, dst, send, recv, to):
    return pltpu.make_async_remote_copy(
        src_ref=src, dst_ref=dst, send_sem=send, recv_sem=recv, device_id=(to,), device_id_type=MESH
    )


def greet(partners):
    barrier = pltpu.get_barrier_semaphore()
    for to in partners:
        pl.semaphore_signal(barrier, inc=1, device_id=(to,), device_id_type=MESH)
    pl.semaphore_wait(barrier, len(partners))


def reduce_kernel(
    p_ref, out_ref, r1, a1, r2, a2, r3, a3, r4, gath,
    s1, t1, s2, t2, s3, t3, s4, t4, s5, t5,
):
    me = lax.axis_index("range")
    core = me % 2
    sib = me + 1 - 2 * core
    sa = 32 - 24 * core
    sb = 8 + 24 * core
    a = me // sa % 4
    b = me // sb % 4
    y = me // 2 % 4
    bin_ = me // 4
    member = me % 4
    oa = me // sb % 4

    def along(stride, coord, j):
        return me + ((coord + j) % 4 - coord) * stride

    near = []
    for delta in (-1, 0, 1):
        for j in range(4):
            if delta == 0 and j == 0:
                continue
            near.append((delta, j, (bin_ + delta + 32) % 32 * 4 + (member + j) % 4))
    partners = [sib]
    for stride, coord in ((sa, a), (sb, b), (2, y)):
        partners += [along(stride, coord, j) for j in (1, 2, 3)]
    partners += [to for _, _, to in near]
    greet(partners)

    order = (2, 1, 3, 0)
    first = []
    for j in order:
        at = pl.ds((oa + j) % 4 * 8, 8)
        copy = remote(p_ref.at[1 - core, at], r1.at[at], s1.at[j], t1.at[j], sib)
        copy.start()
        first.append(copy)
    second = []
    for n, j in enumerate(order):
        at = pl.ds((a + j) % 4 * 8, 8)
        remote(p_ref.at[core, at], r1.at[at], s1.at[j], t1.at[j], sib).wait_recv()
        a1[at] = p_ref[core, at] + r1[at]
        if j:
            copy = remote(a1.at[at], r2.at[j - 1], s2.at[j - 1], t2.at[j - 1], along(sa, a, j))
            copy.start()
            second.append(copy)
    for copy in second:
        copy.wait_recv()
    third = []
    for j in order:
        at = pl.ds((b + j) % 4 * 2, 2)
        src = pl.ds(a * 8 + (b + j) % 4 * 2, 2)
        a2[at] = (a1[src] + r2[0, at]) + (r2[1, at] + r2[2, at])
        if j:
            copy = remote(a2.at[at], r3.at[j - 1], s3.at[j - 1], t3.at[j - 1], along(sb, b, j))
            copy.start()
            third.append(copy)
    for copy in third:
        copy.wait_recv()
    a3[...] = (a2[pl.ds(b * 2, 2)] + r3[0]) + (r3[1] + r3[2])
    fourth = []
    for j in (2, 1, 3):
        to = (y + j) % 4
        src = a3.at[to // 2, pl.ds(pl.multiple_of(to % 2 * 40, 8), 40)]
        copy = remote(src, r4.at[j - 1], s4.at[j - 1], t4.at[j - 1], along(2, y, j))
        copy.start()
        fourth.append(copy)
    for copy in fourth:
        copy.wait_recv()
    mine = (a3[y // 2, pl.ds(pl.multiple_of(y % 2 * 40, 8), 40)] + r4[0]) + (r4[1] + r4[2])
    gath[1, member] = mine
    fifth = []
    for n, (delta, j, to) in enumerate(near):
        rows = {-1: pl.ds(0, 40), 0: pl.ds(16, 24), 1: pl.ds(32, 8)}[delta]
        copy = remote(
            gath.at[1, member, rows], gath.at[1 - delta, member, rows], s5.at[n],
            t5.at[1 - delta, member], to,
        )
        copy.start()
        fifth.append(copy)
    for delta in (-1, 0, 1):
        for j in range(4):
            if delta == 0 and j == 0:
                continue
            rows = {-1: pl.ds(0, 40), 0: pl.ds(16, 24), 1: pl.ds(32, 8)}[delta]
            m = (member + j) % 4
            remote(
                gath.at[1, member, rows], gath.at[1 - delta, m, rows], s5.at[0],
                t5.at[1 - delta, m], sib,
            ).wait_recv()
    for copy in first + second + third + fourth + fifth:
        copy.wait_send()
    out_ref[0, :, 32:40] = gath[0, :, 32:40]
    out_ref[1, :, 16:40] = gath[1, :, 16:40]
    out_ref[2] = gath[2]


def reduce(p):
    dma = pltpu.SemaphoreType.DMA
    return pl.pallas_call(
        reduce_kernel,
        out_shape=jax.ShapeDtypeStruct((3, 4, 40, 128), F32),
        in_specs=[VMEM],
        out_specs=VMEM,
        scratch_shapes=[
            pltpu.VMEM((32, 80, 128), F32),
            pltpu.VMEM((32, 80, 128), F32),
            pltpu.VMEM((3, 8, 80, 128), F32),
            pltpu.VMEM((8, 80, 128), F32),
            pltpu.VMEM((3, 2, 80, 128), F32),
            pltpu.VMEM((2, 80, 128), F32),
            pltpu.VMEM((3, 40, 128), F32),
            pltpu.VMEM((3, 4, 40, 128), F32),
            dma((4,)), dma((4,)), dma((3,)), dma((3,)), dma((3,)), dma((3,)),
            dma((3,)), dma((3,)), dma((11,)), dma((3, 4)),
        ],
        compiler_params=pltpu.CompilerParams(
            collective_id=0, has_side_effects=True, vmem_limit_bytes=LIMIT
        ),
        name="reduce",
    )(p)


def times_i(m):
    return jnp.concatenate([-m[:, 64:], m[:, :64]], axis=1)


def cdot(x, y):
    return jnp.dot(
        x, jnp.concatenate([y, times_i(y)], axis=0),
        preferred_element_type=F32, precision=lax.Precision.HIGHEST,
    )


def adjoint(m):
    t = m.T
    return jnp.concatenate([t[:64], -t[64:]], axis=1)


def hermitian_inverse(m):
    lane = lax.broadcasted_iota(jnp.int32, (8, 128), 1)
    sub = lax.broadcasted_iota(jnp.int32, (8, 128), 0)
    n = times_i(m)
    ms = [m[8 * t : 8 * t + 8] for t in range(8)]
    ns = [n[8 * t : 8 * t + 8] for t in range(8)]
    for k in range(64):
        t0, r0 = divmod(k, 8)
        is_re = lane == k
        is_im = lane == 64 + k
        hit = is_re | is_im
        inv = 1.0 / jnp.broadcast_to(ms[t0][r0 : r0 + 1, k : k + 1], (8, 128))
        row = jnp.broadcast_to(ms[t0][r0 : r0 + 1], (8, 128)) * inv
        rowi = jnp.broadcast_to(ns[t0][r0 : r0 + 1], (8, 128)) * inv
        row = jnp.where(is_re, inv, jnp.where(is_im, 0.0, row))
        rowi = jnp.where(is_im, inv, jnp.where(is_re, 0.0, rowi))
        for t in range(8):
            cr = jnp.broadcast_to(ms[t][:, k : k + 1], (8, 128))
            ci = jnp.broadcast_to(ms[t][:, 64 + k : 65 + k], (8, 128))
            mt = jnp.where(hit, 0.0, ms[t]) - cr * row - ci * rowi
            nt = jnp.where(hit, 0.0, ns[t]) - cr * rowi + ci * row
            if t == t0:
                mt = jnp.where(sub == r0, row, mt)
                nt = jnp.where(sub == r0, rowi, nt)
            ms[t] = mt
            ns[t] = nt
    return jnp.concatenate(ms, axis=0)


def solve_kernel(g_ref, steer_ref, w_ref):
    scale = 1.0 / 32768.0
    order = (0, 2, 1, 3)
    r64 = lax.broadcasted_iota(jnp.int32, (64, 64), 0)
    c64 = lax.broadcasted_iota(jnp.int32, (64, 64), 1)

    def block(g, rows):
        return jnp.concatenate([g_ref[g, m, rows] for m in order], axis=0) * scale

    def diagonal(g):
        pk = block(g, slice(32, 40))
        k = jnp.concatenate([pk[:, :64], pk[:, 64:]], axis=0)
        kt = k.T
        real = jnp.where(r64 >= c64, k, kt)
        imag = jnp.where(r64 < c64, k, jnp.where(r64 == c64, 0.0, -kt))
        return jnp.concatenate([real, imag], axis=1)

    a11 = diagonal(0)
    a33 = diagonal(1)
    a22 = diagonal(2)
    a12 = block(2, slice(0, 16))
    a13 = block(1, slice(16, 32))
    a32 = block(2, slice(16, 32))
    p = hermitian_inverse(a11)
    v21 = cdot(adjoint(a12), p)
    v31 = cdot(adjoint(a13), p)
    s22 = a22 - cdot(v21, a12)
    s32 = a32 - cdot(v31, a12)
    s33 = a33 - cdot(v31, a13)
    q = hermitian_inverse(s22)
    v32 = cdot(s32, q)
    s33 = s33 - cdot(v32, adjoint(s32))
    r = hermitian_inverse(s33)
    t = steer_ref[...]
    y3 = cdot(t, r)
    y2 = -cdot(y3, v32)
    y1 = -cdot(y2, v21) - cdot(y3, v31)
    norm = lax.rsqrt(jnp.sum(t * y3, axis=1, keepdims=True))
    real = [(v[:, :64] * norm) for v in (y1, y3, y2)]
    imag = [(v[:, 64:] * -norm) for v in (y1, y3, y2)]
    rows = jnp.concatenate(
        [jnp.concatenate(real, axis=1), jnp.concatenate(imag, axis=1)], axis=0
    )
    zero = jnp.zeros((16, 64), F32)
    even = jnp.concatenate([rows, zero], axis=1)
    odd = jnp.concatenate([zero, rows], axis=1)
    parity = lax.axis_index("range") // 4 % 2
    w_ref[...] = jnp.where(parity == 0, even, odd).astype(BF16)


def solve(gathered):
    return pl.pallas_call(
        solve_kernel,
        out_shape=jax.ShapeDtypeStruct((16, 256), BF16),
        in_specs=[VMEM] * 2,
        out_specs=VMEM,
        compiler_params=pltpu.CompilerParams(vmem_limit_bytes=LIMIT),
        name="solve",
    )(gathered, jnp.asarray(steer_rows()))


def back_kernel(
    w_ref, s_ref, bin_ref, block_ref, beam_ref, owner_ref, out_ref,
    wall, table, slots, r1, r2, mid,
    s1, t1, s2, t2, s3, t3, s4, t4, s5, t5,
):
    me = lax.axis_index("range")
    core = me % 2
    y = me // 2 % 4
    x = me // 8 % 4
    z = me // 32
    zx = me // 8
    yc = me % 8
    bin_ = me // 4

    across = me + ((y + 2) % 4 - y) * 2
    xs = [me + ((x + j) % 4 - x) * 8 for j in (1, 2, 3)]
    zs = [me + ((z + j) % 4 - z) * 32 for j in (1, 2, 3)]
    planes = [((z + j // 4) % 4 * 4 + (x + j % 4) % 4) for j in range(1, 16)]
    froms = [((z + 4 - j // 4) % 4 * 4 + (x + 4 - j % 4) % 4) for j in range(1, 16)]
    posts = [(yc + j) % 8 for j in range(1, 8)]
    partners = [across] + xs + zs + [q * 8 + yc for q in planes] + [zx * 8 + q for q in posts]
    greet(partners)

    wall[bin_] = w_ref[...]
    copies = []
    one = remote(w_ref, wall.at[bin_], s1, t1, across)
    one.start()
    copies.append(one)

    s_iota = lax.broadcasted_iota(jnp.int32, (256, 128), 0)
    named = (s_iota // 2 == owner_ref[...]).astype(F32)
    before = (
        lax.broadcasted_iota(jnp.int32, (128, 128), 0) < lax.broadcasted_iota(jnp.int32, (128, 128), 1)
    ).astype(F32)
    earlier = jnp.dot(named.astype(BF16), before.astype(BF16), preferred_element_type=F32)
    pick = jnp.where(earlier == (s_iota % 2).astype(F32), named, 0.0).astype(BF16)
    wanted = block_ref[...] * 256 + bin_ref[...] * 8 + beam_ref[...]
    t_iota = lax.broadcasted_iota(jnp.int32, (512, 128), 0)
    holds = (t_iota == wanted).astype(F32).astype(BF16)
    select = lax.dot_general(pick, holds, NT, preferred_element_type=F32).astype(BF16)

    one.wait_recv()
    for j, to in enumerate(xs):
        at = pl.ds(zx * 2, 2)
        copy = remote(wall.at[at], wall.at[at], s2.at[j], t2.at[j], to)
        copy.start()
        copies.append(copy)
    for j in range(3):
        src = z * 4 + (x + 3 - j) % 4
        at = pl.ds(src * 2, 2)
        remote(wall.at[at], wall.at[at], s2.at[j], t2.at[j], xs[j]).wait_recv()
    for j, to in enumerate(zs):
        at = pl.ds(z * 8, 8)
        copy = remote(wall.at[at], wall.at[at], s3.at[j], t3.at[j], to)
        copy.start()
        copies.append(copy)

    for j in (3, 0, 2, 1):
        src = (z + 3 - j) % 4 if j < 3 else z
        if j < 3:
            at = pl.ds(src * 8, 8)
            remote(wall.at[at], wall.at[at], s3.at[j], t3.at[j], zs[j]).wait_recv()
        for k in range(4):
            first = src * 8 + 2 * k
            lhs = wall[pl.ds(first, 2)].reshape(32, 256)
            rhs = s_ref[pl.ds(first + 1, 4)].reshape(256, 512)
            prod = jnp.dot(lhs, rhs, preferred_element_type=F32)
            reals, imags = [], []
            for i in range(2):
                top = prod[16 * i : 16 * i + 8]
                low = prod[16 * i + 8 : 16 * i + 16]
                reals.append(top[:, :256] + low[:, 256:])
                imags.append(top[:, 256:] - low[:, :256])
            real = jnp.concatenate(reals, axis=0).astype(BF16)
            imag = jnp.concatenate(imags, axis=0).astype(BF16)
            for i in range(2):
                rows = pl.ds(pl.multiple_of(i * 256 + first * 8, 16), 16)
                table[rows, 0:128] = real[:, 128 * i : 128 * i + 128]
                table[rows, 128:256] = imag[:, 128 * i : 128 * i + 128]

    slots[...] = (
        jnp.dot(select, table[...], preferred_element_type=F32).astype(BF16).reshape(16, 16, 256)
    )
    for j, q in enumerate(planes):
        copy = remote(slots.at[q], r1.at[zx], s4.at[j], t4.at[j], q * 8 + yc)
        copy.start()
        copies.append(copy)
    r1[zx] = slots[zx]
    for j, q in enumerate(froms):
        remote(slots.at[q], r1.at[q], s4.at[j], t4.at[j], across).wait_recv()
    o = lax.broadcasted_iota(jnp.int32, (256, 256), 0)
    i = lax.broadcasted_iota(jnp.int32, (256, 256), 1)
    turn = (i == o % 32 // 2 * 16 + o // 32 * 2 + o % 2).astype(F32).astype(BF16)
    mid[...] = (
        jnp.dot(turn, r1[...].reshape(256, 256), preferred_element_type=F32)
        .astype(BF16)
        .reshape(8, 32, 256)
    )
    for j, q in enumerate(posts):
        copy = remote(mid.at[q], r2.at[yc], s5.at[j], t5.at[j], zx * 8 + q)
        copy.start()
        copies.append(copy)
    r2[yc] = mid[yc]
    back = (i == o % 16 // 2 * 32 + o // 16 * 2 + o % 2).astype(F32).astype(BF16)
    for j in range(7):
        q = (yc + 7 - j) % 8
        remote(mid.at[q], r2.at[q], s5.at[j], t5.at[j], across).wait_recv()
    out_ref[...] = jnp.dot(back, r2[...].reshape(256, 256), preferred_element_type=F32)
    for copy in copies:
        copy.wait_send()


def back(weight, spectra, det_bin, det_block, det_beam, owner):
    dma = pltpu.SemaphoreType.DMA
    return pl.pallas_call(
        back_kernel,
        out_shape=jax.ShapeDtypeStruct((256, 256), F32),
        in_specs=[VMEM] * 6,
        out_specs=VMEM,
        scratch_shapes=[
            pltpu.VMEM((32, 16, 256), BF16),
            pltpu.VMEM((512, 256), BF16),
            pltpu.VMEM((16, 16, 256), BF16),
            pltpu.VMEM((16, 16, 256), BF16),
            pltpu.VMEM((8, 32, 256), BF16),
            pltpu.VMEM((8, 32, 256), BF16),
            dma(()), dma(()), dma((3,)), dma((3,)), dma((3,)), dma((3,)),
            dma((15,)), dma((15,)), dma((7,)), dma((7,)),
        ],
        compiler_params=pltpu.CompilerParams(
            collective_id=1, has_side_effects=True, vmem_limit_bytes=LIMIT
        ),
        name="back",
    )(weight, spectra, det_bin, det_block, det_beam, owner)


def on_device(raw, replica, det_bin, det_block, det_beam, det_owner):
    count = lax.axis_size("range")
    halo = lax.ppermute(raw[..., :TAPS], "range", [(i + 1, i) for i in range(count - 1)])
    spectra, partial = front(raw, halo, replica)
    weight = solve(reduce(partial))
    rows = [v.reshape(1, 128) for v in (det_bin, det_block, det_beam, det_owner)]
    return back(weight, spectra, *rows)


def solution(mesh):
    in_specs = (
        P(None, None, None, "range"),
        P(),
        P("range"),
        P("range"),
        P("range"),
        P("range", None),
    )
    return jax.shard_map(
        on_device, mesh=mesh, in_specs=in_specs, out_specs=P("range", None), check_vma=False
    )
```

```python
import functools
import math

import jax
import jax.numpy as jnp
import numpy as np
from jax import lax
from jax.experimental import pallas as pl
from jax.experimental.pallas import tpu as pltpu
from jax.sharding import PartitionSpec as P

C = 64
PULSES = 32
TAPS = 128
BEAMS = 8
F32 = jnp.float32
BF16 = jnp.bfloat16
MESH = pl.DeviceIdType.MESH
VMEM = pl.BlockSpec(memory_space=pltpu.VMEM)
ANY = pl.BlockSpec(memory_space=pl.ANY)
NT = (((1,), (1,)), ((), ()))
LIMIT = 48 * 1024 * 1024


def dft_matrix():
    index = np.arange(PULSES)
    angle = 2.0 * math.pi / PULSES * (index[:, None] * index[None, :] % PULSES)
    scale = PULSES**-0.5
    real = np.cos(angle) * scale
    imag = -np.sin(angle) * scale
    eye = np.eye(8)
    kr = np.einsum("pd,ab->dabp", real, eye).reshape(256, 256)
    ki = np.einsum("pd,ab->dabp", imag, eye).reshape(256, 256)
    full = np.concatenate([np.concatenate([kr, -ki], 1), np.concatenate([ki, kr], 1)], 0)
    return full.astype(jnp.bfloat16)


def steer_rows():
    sines = -0.8 + 1.6 * np.arange(BEAMS, dtype=np.float32) / np.float32(BEAMS - 1)
    angle = (math.pi * np.arange(C, dtype=np.float32)[None, :] * sines[:, None]).astype(np.float32)
    return np.concatenate([np.cos(angle), -np.sin(angle)], 1).astype(np.float32)


def remote(src, dst, send, recv, to):
    return pltpu.make_async_remote_copy(
        src_ref=src, dst_ref=dst, send_sem=send, recv_sem=recv, device_id=(to,), device_id_type=MESH
    )


def build_toeplitz(rep_ref, tz):
    def band(v):
        wide = jnp.concatenate(
            [jnp.broadcast_to(v, (TAPS, TAPS)), jnp.zeros((TAPS, TAPS), F32)], axis=1
        )
        return pltpu.roll(wide, 0, 1, stride=1, stride_axis=0).T

    rep = rep_ref[...].astype(F32)
    tr = band(rep[0:1])
    ti = band(rep[1:2])
    tz[0:256, 0:128] = tr.astype(BF16)
    tz[0:256, 128:256] = (-ti).astype(BF16)
    tz[256:512, 0:128] = ti.astype(BF16)
    tz[256:512, 128:256] = tr.astype(BF16)


def spectra_part(b, i, raw, halo, dft_ref, s, tz):
    def compressed(first):
        at = pl.ds(first, 8)
        xr = raw[0, at].reshape(256, 256)
        xi = raw[1, at].reshape(256, 256)
        if b == 0:
            window = jnp.concatenate([xr, xi], axis=1)
        else:
            hr = halo[0, at].reshape(256, 128)
            hi = halo[1, at].reshape(256, 128)
            window = jnp.concatenate([xr[:, 128:], hr, xi[:, 128:], hi], axis=1)
        return jnp.dot(window, tz[...], preferred_element_type=F32).astype(BF16)

    first = 16 * i
    ya = compressed(first)
    yb = compressed(first + 8)
    y = jnp.concatenate(
        [
            jnp.concatenate([ya[:, :128], yb[:, :128]], axis=1),
            jnp.concatenate([ya[:, 128:], yb[:, 128:]], axis=1),
        ],
        axis=0,
    )
    out = jnp.dot(dft_ref[...], y, preferred_element_type=F32)
    for p in range(2):
        h = out[256 * p : 256 * p + 256]
        v = jnp.concatenate(
            [h[:, :128].reshape(32, 8, 128), h[:, 128:].reshape(32, 8, 128)], axis=1
        )
        lanes = 256 * b + 128 * p
        s[2:34, first : first + 16, lanes : lanes + 128] = v.astype(BF16)


def store_products(p, f, two, one, zero):
    lane = lax.broadcasted_iota(jnp.int32, (32, 128), 1)
    row = lax.broadcasted_iota(jnp.int32, (32, 128), 0)
    swapped = pltpu.roll(zero, 64, 1)
    top = jnp.where(row >= lane, zero[:32], swapped[:32])
    bottom = jnp.where(row + 32 >= lane - 64, swapped[32:], zero[32:])
    packed = jnp.where(lane < 64, top, bottom)
    other = (f // 2) % 4 * 8 + f // 8 * 2 + f % 2
    for h in range(2):
        pos = f if h == 0 else other
        for q in range(2):
            a = 32 * h + 16 * q
            p[h, pos, 40 * q : 40 * q + 16] = two[a : a + 16]
            p[h, pos, 40 * q + 16 : 40 * q + 32] = one[a : a + 16]
            p[h, pos, 40 * q + 32 : 40 * q + 40] = packed[a // 2 : a // 2 + 8]


def cross_products(s, p):
    def step(i, carry):
        f = 2 * i
        lhs = s[pl.ds(f, 4)].reshape(256, 512)
        rhs = []
        for n in range(2):
            v = s[f + 2 + n]
            turned = [-v[:, 128:256], v[:, :128], -v[:, 384:], v[:, 256:384]]
            rhs += [v, jnp.concatenate(turned, axis=1)]
        prod = lax.dot_general(
            lhs, jnp.concatenate(rhs, axis=0), NT, preferred_element_type=F32
        )
        store_products(p, f, prod[:64, :128], prod[64:128, :128], prod[128:192, :128])
        store_products(p, f + 1, prod[64:128, 128:], prod[128:192, 128:], prod[192:, 128:])
        return carry

    lax.fori_loop(0, 16, step, 0, unroll=UNROLL)


UNROLL = 4


def times_i(m):
    return jnp.concatenate([-m[:, 64:], m[:, :64]], axis=1)


def cdot(x, y):
    return jnp.dot(
        x, jnp.concatenate([y, times_i(y)], axis=0),
        preferred_element_type=F32, precision=lax.Precision.HIGHEST,
    )


def adjoint(m):
    t = m.T
    return jnp.concatenate([t[:64], -t[64:]], axis=1)


def lane_of(v, k):
    return jnp.broadcast_to(v[:, k : k + 1], (8, 128))


def row_of(v, r):
    return jnp.broadcast_to(v[r : r + 1], (8, 128))


def cmul(x, y):
    return (x[0] * y[0] - x[1] * y[1], x[0] * y[1] + x[1] * y[0])


def cmulc(x, y):
    return (x[0] * y[0] + x[1] * y[1], x[1] * y[0] - x[0] * y[1])


def cadd(x, y):
    return (x[0] + y[0], x[1] + y[1])


def csub(x, y):
    return (x[0] - y[0], x[1] - y[1])


def cscale(x, c):
    return (x * c[0], x * c[1])


def conj(x):
    return (x[0], -x[1])


def size2(x):
    return x[0] * x[0] + x[1] * x[1]


def rdot(x, y):
    return x[0] * y[0] + x[1] * y[1]


def cm(c, row):
    v, w = row
    return (c[0] * v + c[1] * w, c[0] * w - c[1] * v)


def hermitian_inverse(m):
    lane = lax.broadcasted_iota(jnp.int32, (8, 128), 1)
    sub = lax.broadcasted_iota(jnp.int32, (8, 128), 0)
    ms = [m[8 * t : 8 * t + 8] for t in range(8)]
    for k in range(0, 64, 4):
        t0, r0 = divmod(k, 8)
        w = ms[t0]
        wi = times_i(w)
        cr = [[lane_of(v, k + j) for v in ms] for j in range(4)]
        ci = [[lane_of(v, 64 + k + j) for v in ms] for j in range(4)]

        def entry(i, j):
            return (row_of(cr[j][t0], r0 + i), row_of(ci[j][t0], r0 + i))

        a, d, b = entry(0, 0)[0], entry(1, 1)[0], entry(0, 1)
        p, s, q = entry(2, 2)[0], entry(3, 3)[0], entry(2, 3)
        bb = [[entry(0, 2), entry(0, 3)], [entry(1, 2), entry(1, 3)]]
        det = 1.0 / (a * d - size2(b))
        ia, id_, ib = d * det, a * det, cscale(-det, b)
        ww = [
            [cadd(cscale(ia, bb[0][j]), cmul(ib, bb[1][j])) for j in range(2)],
            [cadd(cmul(conj(ib), bb[0][j]), cscale(id_, bb[1][j])) for j in range(2)],
        ]
        s00 = p - (rdot(bb[0][0], ww[0][0]) + rdot(bb[1][0], ww[1][0]))
        s11 = s - (rdot(bb[0][1], ww[0][1]) + rdot(bb[1][1], ww[1][1]))
        s01 = csub(q, cadd(cmulc(ww[0][1], bb[0][0]), cmulc(ww[1][1], bb[1][0])))
        dets = 1.0 / (s00 * s11 - size2(s01))
        j00, j11, j01 = s11 * dets, s00 * dets, cscale(-dets, s01)
        hit = ((lane >= k) & (lane < k + 4)) | ((lane >= 64 + k) & (lane < 68 + k))
        rows = []
        for j in range(4):
            real = jnp.where(hit, jnp.where(lane == k + j, 1.0, 0.0), row_of(w, r0 + j))
            imag = jnp.where(hit, jnp.where(lane == 64 + k + j, 1.0, 0.0), row_of(wi, r0 + j))
            rows.append((real, imag))
        t2 = csub(rows[2], cadd(cm(conj(ww[0][0]), rows[0]), cm(conj(ww[1][0]), rows[1])))
        t3 = csub(rows[3], cadd(cm(conj(ww[0][1]), rows[0]), cm(conj(ww[1][1]), rows[1])))
        x2 = cadd(cscale(j00, t2), cm(j01, t3))
        x3 = cadd(cscale(j11, t3), cm(conj(j01), t2))
        u0 = cadd(cscale(ia, rows[0]), cm(ib, rows[1]))
        u1 = cadd(cscale(id_, rows[1]), cm(conj(ib), rows[0]))
        x0 = csub(u0, cadd(cm(ww[0][0], x2), cm(ww[0][1], x3)))
        x1 = csub(u1, cadd(cm(ww[1][0], x2), cm(ww[1][1], x3)))
        g = [x0, x1, x2, x3]
        for t in range(8):
            terms = [cr[j][t] * g[j][0] + ci[j][t] * g[j][1] for j in range(4)]
            mt = jnp.where(hit, 0.0, ms[t]) - ((terms[0] + terms[1]) + (terms[2] + terms[3]))
            if t == t0:
                for j in range(4):
                    mt = jnp.where(sub == r0 + j, g[j][0], mt)
            ms[t] = mt
    return jnp.concatenate(ms, axis=0)


def solve(g_ref, steer_ref, parity):
    scale = 1.0 / 32768.0
    order = (0, 2, 1, 3)
    r64 = lax.broadcasted_iota(jnp.int32, (64, 64), 0)
    c64 = lax.broadcasted_iota(jnp.int32, (64, 64), 1)

    def block(g, rows):
        return jnp.concatenate([g_ref[g, m, rows] for m in order], axis=0) * scale

    def diagonal(g):
        pk = block(g, slice(32, 40))
        k = jnp.concatenate([pk[:, :64], pk[:, 64:]], axis=0)
        kt = k.T
        real = jnp.where(r64 >= c64, k, kt)
        imag = jnp.where(r64 < c64, k, jnp.where(r64 == c64, 0.0, -kt))
        return jnp.concatenate([real, imag], axis=1)

    a11 = diagonal(0)
    a33 = diagonal(1)
    a22 = diagonal(2)
    a12 = block(2, slice(0, 16))
    a13 = block(1, slice(16, 32))
    a32 = block(2, slice(16, 32))
    p = hermitian_inverse(a11)
    v21 = cdot(adjoint(a12), p)
    v31 = cdot(adjoint(a13), p)
    s22 = a22 - cdot(v21, a12)
    s32 = a32 - cdot(v31, a12)
    s33 = a33 - cdot(v31, a13)
    q = hermitian_inverse(s22)
    v32 = cdot(s32, q)
    s33 = s33 - cdot(v32, adjoint(s32))
    r = hermitian_inverse(s33)
    t = steer_ref[...]
    y3 = cdot(t, r)
    y2 = -cdot(y3, v32)
    y1 = -cdot(y2, v21) - cdot(y3, v31)
    norm = lax.rsqrt(jnp.sum(t * y3, axis=1, keepdims=True))
    real = [(v[:, :64] * norm) for v in (y1, y3, y2)]
    imag = [(v[:, 64:] * -norm) for v in (y1, y3, y2)]
    rows = jnp.concatenate(
        [jnp.concatenate(real, axis=1), jnp.concatenate(imag, axis=1)], axis=0
    )
    zero = jnp.zeros((16, 64), F32)
    even = jnp.concatenate([rows, zero], axis=1)
    odd = jnp.concatenate([zero, rows], axis=1)
    return jnp.where(parity == 0, even, odd).astype(BF16)


def selection(bin_ref, block_ref, beam_ref, owner_ref, select, turn, back):
    s_iota = lax.broadcasted_iota(jnp.int32, (256, 128), 0)
    named = (s_iota // 2 == owner_ref[...]).astype(F32)
    before = (
        lax.broadcasted_iota(jnp.int32, (128, 128), 0)
        < lax.broadcasted_iota(jnp.int32, (128, 128), 1)
    ).astype(F32)
    earlier = jnp.dot(named.astype(BF16), before.astype(BF16), preferred_element_type=F32)
    pick = jnp.where(earlier == (s_iota % 2).astype(F32), named, 0.0).astype(BF16)
    wanted = block_ref[...] * 256 + bin_ref[...] * 8 + beam_ref[...]
    t_iota = lax.broadcasted_iota(jnp.int32, (512, 128), 0)
    holds = (t_iota == wanted).astype(F32).astype(BF16)
    select[...] = lax.dot_general(pick, holds, NT, preferred_element_type=F32).astype(BF16)
    o = lax.broadcasted_iota(jnp.int32, (256, 256), 0)
    i = lax.broadcasted_iota(jnp.int32, (256, 256), 1)
    turn[...] = (i == o % 32 // 2 * 16 + o // 32 * 2 + o % 2).astype(F32).astype(BF16)
    back[...] = (i == o % 16 // 2 * 32 + o // 16 * 2 + o % 2).astype(F32).astype(BF16)


def kernel(
    stop,
    raw_ref, rep_ref, dft_ref, steer_ref, bin_ref, block_ref, beam_ref, owner_ref,
    out_ref,
    raw, halo, tz, s, p, r1, a1, rp, rm, a2, r3, a3, r4, gath, wall, table, select, turn, back,
    slots, d1, mid, d2,
    ls, hs, ht, s1, t1, s2, t2, s3, t3, s4, t4, s5, t5, s6, t6, s7, t7, s8, t8,
):
    me = lax.axis_index("range")
    core = me % 2
    y = me // 2 % 4
    x = me // 8 % 4
    z = me // 32
    zx = me // 8
    yc = me % 8
    bin_ = me // 4
    member = me % 4
    sib = me + 1 - 2 * core
    sa = 32 - 24 * core
    sb = 8 + 24 * core
    a = me // sa % 4
    b = me // sb % 4
    left = (me + 127) % 128
    right = (me + 1) % 128

    def along(stride, coord, j):
        return me + ((coord + j) % 4 - coord) * stride

    near = []
    for delta in (-1, 0, 1):
        for j in range(4):
            if delta or j:
                near.append((delta, j, (bin_ + delta + 32) % 32 * 4 + (member + j) % 4))
    bins = [(bin_ + j) % 32 for j in range(1, 32)]
    planes = [(z + j // 4) % 4 * 4 + (x + j % 4) % 4 for j in range(1, 16)]
    froms = [(z + 4 - j // 4) % 4 * 4 + (x + 4 - j % 4) % 4 for j in range(1, 16)]
    posts = [(yc + j) % 8 for j in range(1, 8)]
    partners = [left, right, sib, along(sa, a, 1), along(sa, a, 3)]
    partners += [along(sb, b, j) for j in (1, 2, 3)] + [along(2, y, j) for j in (1, 2, 3)]
    partners += [to for _, _, to in near] + [q * 4 + member for q in bins]
    partners += [q * 8 + yc for q in planes] + [zx * 8 + q for q in posts]

    loads = []
    for i in range(4):
        at = pl.ds(16 * i, 16)
        copy = pltpu.make_async_copy(raw_ref.at[:, at], raw.at[:, at], ls.at[i])
        copy.start()
        loads.append(copy)
    barrier = pltpu.get_barrier_semaphore()
    for to in partners:
        pl.semaphore_signal(barrier, inc=1, device_id=(to,), device_id_type=MESH)
    build_toeplitz(rep_ref, tz)
    pl.semaphore_wait(barrier, len(partners))

    def halo_copy(i):
        at = pl.ds(16 * i, 16)
        return remote(
            raw_ref.at[:, at, :, pl.ds(0, TAPS)], halo.at[:, at], hs.at[i], ht.at[i], left
        )

    @pl.when(me > 0)
    def _():
        for i in range(4):
            halo_copy(i).start()

    @pl.when(me == 127)
    def _():
        halo[...] = jnp.zeros_like(halo)

    for i in range(4):
        loads[i].wait()
        spectra_part(0, i, raw, halo, dft_ref, s, tz)
    selection(bin_ref, block_ref, beam_ref, owner_ref, select, turn, back)
    for i in range(4):

        @pl.when(me < 127)
        def _():
            halo_copy(i).wait_recv()

        spectra_part(1, i, raw, halo, dft_ref, s, tz)

    @pl.when(me > 0)
    def _():
        for i in range(4):
            halo_copy(i).wait_send()

    s[0:2] = s[32:34]
    s[34] = s[2]
    copies = []

    def finish():
        for copy in copies:
            copy.wait_send()

    if stop < 1:
        out_ref[...] = s[0, :1, :256].astype(F32)
        return finish()
    cross_products(s, p)
    if stop < 2:
        out_ref[...] = p[0, 0, :1] [:, :1] + jnp.zeros((256, 256), F32)
        return finish()

    order = (2, 1, 3, 0)
    for j in order:
        at = pl.ds(b_like(me, sb, j) * 8, 8)
        copy = remote(p.at[1 - core, at], r1.at[at], s1.at[j], t1.at[j], sib)
        copy.start()
        copies.append(copy)
    rings = []

    def ring(src, dst, n, to):
        copy = remote(src, dst, s2.at[n], t2.at[n], to)
        copy.start()
        copies.append(copy)
        rings.append(copy)

    ahead, behind = along(sa, a, 1), along(sa, a, 3)
    base = {j: (a + j) % 4 * 8 for j in range(4)}
    for j in order:
        at = pl.ds(base[j], 8)
        remote(p.at[core, at], r1.at[at], s1.at[j], t1.at[j], sib).wait_recv()
        a1[at] = p[core, at] + r1[at]
        if j == 2:
            ring(a1.at[pl.ds(base[2], 4)], rp.at[0], 0, ahead)
            ring(a1.at[pl.ds(base[2] + 4, 4)], rm.at[0], 1, behind)
        elif j == 1:
            ring(a1.at[pl.ds(base[1] + 4, 4)], rp.at[1], 2, ahead)
        elif j == 3:
            ring(a1.at[pl.ds(base[3], 4)], rm.at[1], 3, behind)
    rings[0].wait_recv()
    at = pl.ds(base[1], 4)
    a1[at] = a1[at] + rp[0]
    ring(a1.at[at], rp.at[2], 4, ahead)
    rings[1].wait_recv()
    at = pl.ds(base[3] + 4, 4)
    a1[at] = a1[at] + rm[0]
    ring(a1.at[at], rm.at[2], 5, behind)
    for n in (2, 3):
        rings[n].wait_recv()
    at = pl.ds(base[0] + 4, 4)
    a2[4:8] = a1[at] + rp[1]
    at = pl.ds(base[0], 4)
    a2[0:4] = a1[at] + rm[1]
    rings[4].wait_recv()
    a2[0:4] = a2[0:4] + rp[2]
    rings[5].wait_recv()
    a2[4:8] = a2[4:8] + rm[2]
    if stop < 3:
        out_ref[...] = a2[0, :1, :1] + jnp.zeros((256, 256), F32)
        return finish()

    third = []
    for j in (2, 1, 3):
        src = a2.at[pl.ds((b + j) % 4 * 2, 2)]
        copy = remote(src, r3.at[j - 1], s3.at[j - 1], t3.at[j - 1], along(sb, b, j))
        copy.start()
        third.append(copy)
    for copy in third:
        copy.wait_recv()
    copies += third
    a3[...] = (a2[pl.ds(b * 2, 2)] + r3[0]) + (r3[1] + r3[2])
    fourth = []
    for j in (2, 1, 3):
        to = (y + j) % 4
        src = a3.at[to // 2, pl.ds(pl.multiple_of(to % 2 * 40, 8), 40)]
        copy = remote(src, r4.at[j - 1], s4.at[j - 1], t4.at[j - 1], along(2, y, j))
        copy.start()
        fourth.append(copy)
    for copy in fourth:
        copy.wait_recv()
    copies += fourth
    mine = (a3[y // 2, pl.ds(pl.multiple_of(y % 2 * 40, 8), 40)] + r4[0]) + (r4[1] + r4[2])
    gath[1, member] = mine
    if stop < 4:
        out_ref[...] = mine[:1, :1] + jnp.zeros((256, 256), F32)
        return finish()
    needs = {-1: pl.ds(0, 40), 0: pl.ds(16, 24), 1: pl.ds(32, 8)}
    for n, (delta, j, to) in enumerate(near):
        rows = needs[delta]
        copy = remote(
            gath.at[1, member, rows], gath.at[1 - delta, member, rows], s5.at[n],
            t5.at[1 - delta, member], to,
        )
        copy.start()
        copies.append(copy)
    for delta, j, _ in near:
        rows = needs[delta]
        m = (member + j) % 4
        remote(
            gath.at[1, member, rows], gath.at[1 - delta, m, rows], s5.at[0],
            t5.at[1 - delta, m], sib,
        ).wait_recv()
    if stop < 5:
        out_ref[...] = gath[2, 0, :1, :1] + jnp.zeros((256, 256), F32)
        return finish()

    wall[bin_] = solve(gath, steer_ref, bin_ % 2)
    if stop < 6:
        out_ref[...] = wall[bin_, :1].astype(F32) + jnp.zeros((256, 256), F32)
        return finish()
    for n, to in enumerate(bins):
        copy = remote(wall.at[bin_], wall.at[bin_], s6.at[n], t6.at[bin_], to * 4 + member)
        copy.start()
        copies.append(copy)

    for n in range(16):
        duo = (bin_ // 2 + 16 - n) % 16
        first = duo * 2
        waits = (first, first + 1) if n else (bin_ + 1 - 2 * (bin_ % 2),)
        for q in waits:
            remote(wall.at[q], wall.at[q], s6.at[0], t6.at[q], sib).wait_recv()
        lhs = wall[pl.ds(first, 2)].reshape(32, 256)
        rhs = s[pl.ds(first + 1, 4)].reshape(256, 512)
        prod = jnp.dot(lhs, rhs, preferred_element_type=F32)
        for i in range(2):
            at = 256 * i
            tops = [prod[16 * e : 16 * e + 8, at : at + 256] for e in range(2)]
            lows = [prod[16 * e + 8 : 16 * e + 16, at : at + 256] for e in range(2)]
            top = jnp.concatenate(tops, axis=0)
            low = jnp.concatenate(lows, axis=0)
            rows = pl.ds(pl.multiple_of(256 * i + first * 8, 16), 16)
            table[rows, 0:128] = (top[:, :128] + low[:, 128:]).astype(BF16)
            table[rows, 128:256] = (top[:, 128:] - low[:, :128]).astype(BF16)
    if stop < 7:
        out_ref[...] = table[0:256].astype(F32)
        return finish()

    slots[...] = (
        jnp.dot(select[...], table[...], preferred_element_type=F32)
        .astype(BF16)
        .reshape(16, 16, 256)
    )
    for j, q in enumerate(planes):
        copy = remote(slots.at[q], d1.at[zx], s7.at[j], t7.at[j], q * 8 + yc)
        copy.start()
        copies.append(copy)
    d1[zx] = slots[zx]
    for j, q in enumerate(froms):
        remote(slots.at[q], d1.at[q], s7.at[j], t7.at[j], sib).wait_recv()
    mid[...] = (
        jnp.dot(turn[...], d1[...].reshape(256, 256), preferred_element_type=F32)
        .astype(BF16)
        .reshape(8, 32, 256)
    )
    if stop < 8:
        out_ref[...] = mid[...].reshape(256, 256).astype(F32)
        return finish()
    for j, q in enumerate(posts):
        copy = remote(mid.at[q], d2.at[yc], s8.at[j], t8.at[j], zx * 8 + q)
        copy.start()
        copies.append(copy)
    d2[yc] = mid[yc]
    for j in range(7):
        q = (yc + 7 - j) % 8
        remote(mid.at[q], d2.at[q], s8.at[j], t8.at[j], sib).wait_recv()
    out_ref[...] = jnp.dot(back[...], d2[...].reshape(256, 256), preferred_element_type=F32)
    finish()


def b_like(me, stride, j):
    return (me // stride % 4 + j) % 4


def program(raw, replica, det_bin, det_block, det_beam, owner, stop=9):
    dma = pltpu.SemaphoreType.DMA
    vm = pltpu.VMEM
    return pl.pallas_call(
        functools.partial(kernel, stop),
        out_shape=jax.ShapeDtypeStruct((256, 256), F32),
        in_specs=[ANY] + [VMEM] * 7,
        out_specs=VMEM,
        scratch_shapes=[
            vm((2, 64, 32, 256), BF16),
            vm((2, 64, 32, 128), BF16),
            vm((512, 256), BF16),
            vm((35, 64, 512), BF16),
            vm((2, 32, 80, 128), F32),
            vm((32, 80, 128), F32),
            vm((32, 80, 128), F32),
            vm((3, 4, 80, 128), F32),
            vm((3, 4, 80, 128), F32),
            vm((8, 80, 128), F32),
            vm((3, 2, 80, 128), F32),
            vm((2, 80, 128), F32),
            vm((3, 40, 128), F32),
            vm((3, 4, 40, 128), F32),
            vm((32, 16, 256), BF16),
            vm((512, 256), BF16),
            vm((256, 512), BF16),
            vm((256, 256), BF16),
            vm((256, 256), BF16),
            vm((16, 16, 256), BF16),
            vm((16, 16, 256), BF16),
            vm((8, 32, 256), BF16),
            vm((8, 32, 256), BF16),
            dma((4,)), dma((4,)), dma((4,)),
            dma((4,)), dma((4,)), dma((6,)), dma((6,)), dma((3,)), dma((3,)),
            dma((3,)), dma((3,)), dma((11,)), dma((3, 4)), dma((31,)), dma((32,)),
            dma((15,)), dma((15,)), dma((7,)), dma((7,)),
        ],
        compiler_params=pltpu.CompilerParams(
            collective_id=0, has_side_effects=True, vmem_limit_bytes=LIMIT
        ),
        name="stap",
    )(
        raw, replica, jnp.asarray(dft_matrix()), jnp.asarray(steer_rows()),
        det_bin, det_block, det_beam, owner,
    )


def on_device(stop, raw, replica, det_bin, det_block, det_beam, det_owner):
    rows = [v.reshape(1, 128) for v in (det_bin, det_block, det_beam, det_owner)]
    return program(raw, replica, *rows, stop=stop)


def solution(mesh, stop=9):
    in_specs = (
        P(None, None, None, "range"),
        P(),
        P("range"),
        P("range"),
        P("range"),
        P("range", None),
    )
    return jax.shard_map(
        functools.partial(on_device, stop),
        mesh=mesh,
        in_specs=in_specs,
        out_specs=P("range", None),
        check_vma=False,
    )
```

```python
import functools
import math

import jax
import jax.numpy as jnp
import numpy as np
from jax import lax
from jax.experimental import pallas as pl
from jax.experimental.pallas import tpu as pltpu
from jax.sharding import PartitionSpec as P

C = 64
PULSES = 32
TAPS = 128
BEAMS = 8
F32 = jnp.float32
BF16 = jnp.bfloat16
MESH = pl.DeviceIdType.MESH
VMEM = pl.BlockSpec(memory_space=pltpu.VMEM)
HBM = pl.BlockSpec(memory_space=pltpu.HBM)
NT = (((1,), (1,)), ((), ()))
LIMIT = 48 * 1024 * 1024


def dft_matrix():
    index = np.arange(PULSES)
    angle = 2.0 * math.pi / PULSES * (index[:, None] * index[None, :] % PULSES)
    scale = PULSES**-0.5
    eye = np.eye(8)
    parts = [
        np.einsum("pd,ab->dabp", v * scale, eye).reshape(256, 256)
        for v in (np.cos(angle), -np.sin(angle))
    ]
    return np.concatenate(parts, 0).astype(jnp.bfloat16)


def steer_rows():
    sines = -0.8 + 1.6 * np.arange(BEAMS, dtype=np.float32) / np.float32(BEAMS - 1)
    angle = (math.pi * np.arange(C, dtype=np.float32)[None, :] * sines[:, None]).astype(np.float32)
    return np.concatenate([np.cos(angle), -np.sin(angle)], 1).astype(np.float32)


def remote(src, dst, send, recv, to):
    return pltpu.make_async_remote_copy(
        src_ref=src, dst_ref=dst, send_sem=send, recv_sem=recv, device_id=(to,), device_id_type=MESH
    )


def build_toeplitz(rep_ref, keep, tza, tzb):
    def band(v):
        wide = jnp.concatenate(
            [jnp.broadcast_to(v, (TAPS, TAPS)), jnp.zeros((TAPS, TAPS), F32)], axis=1
        )
        return pltpu.roll(wide, 0, 1, stride=1, stride_axis=0).T

    rep = rep_ref[...].astype(F32)
    tr = band(rep[0:1])
    ti = band(rep[1:2])
    re = jnp.concatenate([tr[:, :64], -ti[:, :64], tr[:, 64:], -ti[:, 64:]], axis=1)
    im = jnp.concatenate([ti[:, :64], tr[:, :64], ti[:, 64:], tr[:, 64:]], axis=1)
    zero = jnp.zeros((64, 256), F32)
    inner = jnp.concatenate([re[64:256], zero, im[64:256], zero], axis=0)
    tza[0:64] = re[0:64].astype(BF16)
    tza[64:128] = im[0:64].astype(BF16)
    tza[128:640, 0:128] = (inner[:, :128] * keep).astype(BF16)
    tza[128:640, 128:256] = inner[:, 128:].astype(BF16)
    tzb[0:512] = jnp.concatenate([zero, re[0:192], zero, im[0:192]], axis=0).astype(BF16)
    tzb[512:576] = re[192:256].astype(BF16)
    tzb[576:640] = im[192:256].astype(BF16)


def turned(v):
    lane = lax.broadcasted_iota(jnp.int32, (v.shape[0], 128), 1)
    parts = []
    for n in range(v.shape[1] // 128):
        r = pltpu.roll(v[:, 128 * n : 128 * n + 128], 64, 1)
        parts.append(jnp.where(lane < 64, -r, r))
    return jnp.concatenate(parts, axis=1)


def spectra_part(i, raw, hl, hr, dft_ref, s, tza, tzb):
    first = 16 * i
    for b in range(2):
        outs = []
        for n in range(2):
            at = pl.ds(first + 8 * n, 8)
            xr = raw[0, at].reshape(256, 256)
            xi = raw[1, at].reshape(256, 256)
            if b == 0:
                window, tz = [hl[at].reshape(256, 128), xr, xi], tza
            else:
                window, tz = [xr, xi, hr[at].reshape(256, 128)], tzb
            y = jnp.dot(jnp.concatenate(window, axis=1), tz[...], preferred_element_type=F32)
            uv = jnp.dot(dft_ref[...], y.astype(BF16), preferred_element_type=F32)
            outs.append((uv[:256] + turned(uv[256:])).reshape(32, 8, 256))
        s[2:34, first : first + 16, 256 * b : 256 * b + 256] = jnp.concatenate(
            outs, axis=1
        ).astype(BF16)


def store_products(p, f, two, one, zero):
    lane = lax.broadcasted_iota(jnp.int32, (32, 128), 1)
    row = lax.broadcasted_iota(jnp.int32, (32, 128), 0)
    swapped = pltpu.roll(zero, 64, 1)
    top = jnp.where(row >= lane, zero[:32], swapped[:32])
    bottom = jnp.where(row + 32 >= lane - 64, swapped[32:], zero[32:])
    packed = jnp.where(lane < 64, top, bottom)
    other = (f // 2) % 4 * 8 + f // 8 * 2 + f % 2
    for h in range(2):
        pos = f if h == 0 else other
        for q in range(2):
            a = 32 * h + 16 * q
            p[h, pos, 40 * q : 40 * q + 16] = two[a : a + 16]
            p[h, pos, 40 * q + 16 : 40 * q + 32] = one[a : a + 16]
            p[h, pos, 40 * q + 32 : 40 * q + 40] = packed[a // 2 : a // 2 + 8]


def cross_products(i, s, p):
    f = 2 * i
    lhs = s[pl.ds(f, 4)].reshape(256, 512)
    rhs = []
    for n in range(2):
        v = s[f + 2 + n]
        rhs += [v, turned(v.astype(F32)).astype(BF16)]
    prod = lax.dot_general(lhs, jnp.concatenate(rhs, axis=0), NT, preferred_element_type=F32)
    store_products(p, f, prod[:64, :128], prod[64:128, :128], prod[128:192, :128])
    store_products(p, f + 1, prod[64:128, 128:], prod[128:192, 128:], prod[192:, 128:])


def times_i(m):
    return jnp.concatenate([-m[:, 64:], m[:, :64]], axis=1)


def cdot(x, y):
    return jnp.dot(
        x, jnp.concatenate([y, times_i(y)], axis=0),
        preferred_element_type=F32, precision=lax.Precision.HIGHEST,
    )


def adjoint(m):
    t = m.T
    return jnp.concatenate([t[:64], -t[64:]], axis=1)


def lane_of(v, k):
    return jnp.broadcast_to(v[:, k : k + 1], (8, 128))


def row_of(v, r):
    return jnp.broadcast_to(v[r : r + 1], (8, 128))


def cmul(x, y):
    return (x[0] * y[0] - x[1] * y[1], x[0] * y[1] + x[1] * y[0])


def cmulc(x, y):
    return (x[0] * y[0] + x[1] * y[1], x[1] * y[0] - x[0] * y[1])


def cadd(x, y):
    return (x[0] + y[0], x[1] + y[1])


def csub(x, y):
    return (x[0] - y[0], x[1] - y[1])


def cscale(x, c):
    return (x * c[0], x * c[1])


def conj(x):
    return (x[0], -x[1])


def size2(x):
    return x[0] * x[0] + x[1] * x[1]


def rdot(x, y):
    return x[0] * y[0] + x[1] * y[1]


def cm(c, row):
    v, w = row
    return (c[0] * v + c[1] * w, c[0] * w - c[1] * v)


def hermitian_inverse(m):
    lane = lax.broadcasted_iota(jnp.int32, (8, 128), 1)
    sub = lax.broadcasted_iota(jnp.int32, (8, 128), 0)
    ms = [m[8 * t : 8 * t + 8] for t in range(8)]
    for k in range(0, 64, 4):
        t0, r0 = divmod(k, 8)
        w = ms[t0]
        wi = times_i(w)
        cr = [[lane_of(v, k + j) for v in ms] for j in range(4)]
        ci = [[lane_of(v, 64 + k + j) for v in ms] for j in range(4)]

        def entry(i, j):
            return (row_of(cr[j][t0], r0 + i), row_of(ci[j][t0], r0 + i))

        a, d, b = entry(0, 0)[0], entry(1, 1)[0], entry(0, 1)
        p, s, q = entry(2, 2)[0], entry(3, 3)[0], entry(2, 3)
        bb = [[entry(0, 2), entry(0, 3)], [entry(1, 2), entry(1, 3)]]
        det = 1.0 / (a * d - size2(b))
        ia, id_, ib = d * det, a * det, cscale(-det, b)
        ww = [
            [cadd(cscale(ia, bb[0][j]), cmul(ib, bb[1][j])) for j in range(2)],
            [cadd(cmul(conj(ib), bb[0][j]), cscale(id_, bb[1][j])) for j in range(2)],
        ]
        s00 = p - (rdot(bb[0][0], ww[0][0]) + rdot(bb[1][0], ww[1][0]))
        s11 = s - (rdot(bb[0][1], ww[0][1]) + rdot(bb[1][1], ww[1][1]))
        s01 = csub(q, cadd(cmulc(ww[0][1], bb[0][0]), cmulc(ww[1][1], bb[1][0])))
        dets = 1.0 / (s00 * s11 - size2(s01))
        j00, j11, j01 = s11 * dets, s00 * dets, cscale(-dets, s01)
        hit = ((lane >= k) & (lane < k + 4)) | ((lane >= 64 + k) & (lane < 68 + k))
        rows = []
        for j in range(4):
            real = jnp.where(hit, jnp.where(lane == k + j, 1.0, 0.0), row_of(w, r0 + j))
            imag = jnp.where(hit, jnp.where(lane == 64 + k + j, 1.0, 0.0), row_of(wi, r0 + j))
            rows.append((real, imag))
        t2 = csub(rows[2], cadd(cm(conj(ww[0][0]), rows[0]), cm(conj(ww[1][0]), rows[1])))
        t3 = csub(rows[3], cadd(cm(conj(ww[0][1]), rows[0]), cm(conj(ww[1][1]), rows[1])))
        x2 = cadd(cscale(j00, t2), cm(j01, t3))
        x3 = cadd(cscale(j11, t3), cm(conj(j01), t2))
        u0 = cadd(cscale(ia, rows[0]), cm(ib, rows[1]))
        u1 = cadd(cscale(id_, rows[1]), cm(conj(ib), rows[0]))
        x0 = csub(u0, cadd(cm(ww[0][0], x2), cm(ww[0][1], x3)))
        x1 = csub(u1, cadd(cm(ww[1][0], x2), cm(ww[1][1], x3)))
        g = [x0, x1, x2, x3]
        for t in range(8):
            terms = [cr[j][t] * g[j][0] + ci[j][t] * g[j][1] for j in range(4)]
            mt = jnp.where(hit, 0.0, ms[t]) - ((terms[0] + terms[1]) + (terms[2] + terms[3]))
            if t == t0:
                for j in range(4):
                    mt = jnp.where(sub == r0 + j, g[j][0], mt)
            ms[t] = mt
    return jnp.concatenate(ms, axis=0)


def solve(g_ref, steer_ref, parity):
    scale = 1.0 / 32768.0
    order = (0, 2, 1, 3)
    r64 = lax.broadcasted_iota(jnp.int32, (64, 64), 0)
    c64 = lax.broadcasted_iota(jnp.int32, (64, 64), 1)

    def block(g, rows):
        return jnp.concatenate([g_ref[g, m, rows] for m in order], axis=0) * scale

    def diagonal(g):
        pk = block(g, slice(32, 40))
        k = jnp.concatenate([pk[:, :64], pk[:, 64:]], axis=0)
        kt = k.T
        real = jnp.where(r64 >= c64, k, kt)
        imag = jnp.where(r64 < c64, k, jnp.where(r64 == c64, 0.0, -kt))
        return jnp.concatenate([real, imag], axis=1)

    a11 = diagonal(0)
    a33 = diagonal(1)
    a22 = diagonal(2)
    a12 = block(2, slice(0, 16))
    a13 = block(1, slice(16, 32))
    a32 = block(2, slice(16, 32))
    p = hermitian_inverse(a11)
    v21 = cdot(adjoint(a12), p)
    v31 = cdot(adjoint(a13), p)
    s22 = a22 - cdot(v21, a12)
    s32 = a32 - cdot(v31, a12)
    s33 = a33 - cdot(v31, a13)
    q = hermitian_inverse(s22)
    v32 = cdot(s32, q)
    s33 = s33 - cdot(v32, adjoint(s32))
    r = hermitian_inverse(s33)
    t = steer_ref[...]
    y3 = cdot(t, r)
    y2 = -cdot(y3, v32)
    y1 = -cdot(y2, v21) - cdot(y3, v31)
    norm = lax.rsqrt(jnp.sum(t * y3, axis=1, keepdims=True))
    real = [(v[:, :64] * norm) for v in (y1, y3, y2)]
    imag = [(v[:, 64:] * -norm) for v in (y1, y3, y2)]
    rows = jnp.concatenate(
        [jnp.concatenate(real, axis=1), jnp.concatenate(imag, axis=1)], axis=0
    )
    zero = jnp.zeros((16, 64), F32)
    even = jnp.concatenate([rows, zero], axis=1)
    odd = jnp.concatenate([zero, rows], axis=1)
    return jnp.where(parity == 0, even, odd).astype(BF16)


def selection(bin_ref, block_ref, beam_ref, owner_ref, select, turn, back):
    s_iota = lax.broadcasted_iota(jnp.int32, (256, 128), 0)
    named = (s_iota // 2 == owner_ref[...]).astype(F32)
    before = (
        lax.broadcasted_iota(jnp.int32, (128, 128), 0)
        < lax.broadcasted_iota(jnp.int32, (128, 128), 1)
    ).astype(F32)
    earlier = jnp.dot(named.astype(BF16), before.astype(BF16), preferred_element_type=F32)
    pick = jnp.where(earlier == (s_iota % 2).astype(F32), named, 0.0).astype(BF16)
    wanted = block_ref[...] * 256 + bin_ref[...] * 8 + beam_ref[...]
    t_iota = lax.broadcasted_iota(jnp.int32, (512, 128), 0)
    holds = (t_iota == wanted).astype(F32).astype(BF16)
    select[...] = lax.dot_general(pick, holds, NT, preferred_element_type=F32).astype(BF16)
    o = lax.broadcasted_iota(jnp.int32, (256, 256), 0)
    i = lax.broadcasted_iota(jnp.int32, (256, 256), 1)
    turn[...] = (i == o % 32 // 2 * 16 + o // 32 * 2 + o % 2).astype(F32).astype(BF16)
    back[...] = (i == o % 16 // 2 * 32 + o // 16 * 2 + o % 2).astype(F32).astype(BF16)


def kernel(
    stop, few,
    raw_ref, rep_in, dft_in, steer_in, bin_in, block_in, beam_in, owner_in,
    out_ref,
    raw, pkl, pkr, hl, hr, tza, tzb, s, sr, p, r1, a1, rp, rm, a2, r3, gath, wall, table,
    select, turn, back, slots, d1, mid, d2,
    rep_ref, dft_ref, steer_ref, bin_ref, block_ref, beam_ref, owner_ref,
    ls, ms, hs, ht, s1, t1, s2, t2, s3, t3, s5, t5, s6, t6, s7, t7, s8, t8, s9, t9,
):
    me = lax.axis_index("range")
    core = me % 2
    y = me // 2 % 4
    x = me // 8 % 4
    z = me // 32
    zx = me // 8
    yc = me % 8
    bin_ = me // 4
    member = me % 4
    sib = me + 1 - 2 * core
    sa = 32 - 24 * core
    sb = 8 + 24 * core
    a = me // sa % 4
    b = me // sb % 4
    left = (me + 127) % 128
    right = (me + 1) % 128

    def along(stride, coord, j):
        return me + ((coord + j) % 4 - coord) * stride

    near = []
    for delta in (-1, 0, 1):
        for j in range(4):
            if delta or j:
                near.append((delta, j, (bin_ + delta + 32) % 32 * 4 + (member + j) % 4))
    bins = [(bin_ + j) % 32 for j in range(1, 32)]
    planes = [(z + j // 4) % 4 * 4 + (x + j % 4) % 4 for j in range(1, 16)]
    froms = [(z + 4 - j // 4) % 4 * 4 + (x + 4 - j % 4) % 4 for j in range(1, 16)]
    posts = [(yc + j) % 8 for j in range(1, 8)]
    sheet = [
        ((b + j // 4) % 4, (y + j % 4) % 4)
        for j in (10, 9, 11, 6, 14, 2, 8, 5, 7, 13, 15, 1, 3, 4, 12)
    ]
    spots = [me + (q - b) * sb + (r - y) * 2 for q, r in sheet]
    partners = [left, right, sib, along(sa, a, 1), along(sa, a, 3)] + spots
    if not few:
        partners += [to for _, _, to in near] + [q * 4 + member for q in bins]
        partners += [q * 8 + yc for q in planes] + [zx * 8 + q for q in posts]

    small = [
        pltpu.make_async_copy(src, dst, ms.at[n])
        for n, (src, dst) in enumerate(
            [
                (rep_in, rep_ref), (dft_in, dft_ref), (steer_in, steer_ref), (bin_in, bin_ref),
                (block_in, block_ref), (beam_in, beam_ref), (owner_in, owner_ref),
            ]
        )
    ]
    small[0].start()
    loads = []
    for i in range(4):
        at = pl.ds(16 * i, 16)
        copy = pltpu.make_async_copy(raw_ref.at[:, at], raw.at[:, at], ls.at[i])
        copy.start()
        loads.append(copy)
    for copy in small[1:]:
        copy.start()
    barrier = pltpu.get_barrier_semaphore()
    for to in partners:
        pl.semaphore_signal(barrier, inc=1, device_id=(to,), device_id_type=MESH)
    for i in range(4):
        at = pl.ds(16 * i, 16)
        loads[i].wait()
        pkl[at] = jnp.concatenate([raw[0, at, :, 0:64], raw[1, at, :, 0:64]], axis=-1)
        pkr[at] = jnp.concatenate([raw[0, at, :, 192:256], raw[1, at, :, 192:256]], axis=-1)
    pl.semaphore_wait(barrier, len(partners))
    copies = []

    def finish():
        for copy in copies:
            copy.wait_send()

    if stop < 0:
        for copy in small:
            copy.wait()
        out_ref[...] = pkl[0, :1, :1].astype(F32) + jnp.zeros((256, 256), F32)
        return finish()

    def to_left(i):
        at = pl.ds(16 * i, 16)
        return remote(pkl.at[at], hr.at[at], hs.at[0, i], ht.at[0, i], left)

    for i in range(4):
        at = pl.ds(16 * i, 16)
        copy = remote(pkr.at[at], hl.at[at], hs.at[1, i], ht.at[1, i], right)
        copy.start()
        copies.append(copy)

        @pl.when(me > 0)
        def _():
            to_left(i).start()

    @pl.when(me == 127)
    def _():
        hr[...] = jnp.zeros_like(hr)

    small[0].wait()
    build_toeplitz(rep_ref, jnp.where(me > 0, 1.0, 0.0).astype(F32), tza, tzb)
    for copy in small[1:]:
        copy.wait()
    selection(bin_ref, block_ref, beam_ref, owner_ref, select, turn, back)
    for i in range(4):
        copies[i].wait_recv()

        @pl.when(me < 127)
        def _():
            to_left(i).wait_recv()

        spectra_part(i, raw, hl, hr, dft_ref, s, tza, tzb)

    @pl.when(me > 0)
    def _():
        for i in range(4):
            to_left(i).wait_send()

    s[0:2] = s[32:34]
    s[34] = s[2]
    share = remote(s.at[pl.ds(2, 32), :, pl.ds(0, 128)], sr.at[pl.ds(2, 32)], s9, t9, left)
    if stop < 1:
        out_ref[...] = s[0, :1, :256].astype(F32) + jnp.zeros((256, 256), F32)
        return finish()

    order = (2, 1, 3, 0)
    oa = me // sb % 4
    for j in order:
        q = (oa + j) % 4
        for u in range(4):
            cross_products(q * (1 + 3 * core) + u * (4 - 3 * core), s, p)
        at = pl.ds(q * 8, 8)
        copy = remote(p.at[1 - core, at], r1.at[at], s1.at[j], t1.at[j], sib)
        copy.start()
        copies.append(copy)
    share.start()
    copies.append(share)
    if stop < 2:
        for j in order:
            at = pl.ds((a + j) % 4 * 8, 8)
            remote(p.at[core, at], r1.at[at], s1.at[j], t1.at[j], sib).wait_recv()
        share.wait_recv()
        out_ref[...] = p[0, 0, :1, :1] + jnp.zeros((256, 256), F32)
        return finish()

    rings = []

    def ring(src, dst, n, to):
        copy = remote(src, dst, s2.at[n], t2.at[n], to)
        copy.start()
        copies.append(copy)
        rings.append(copy)

    ahead, behind = along(sa, a, 1), along(sa, a, 3)
    base = {j: (a + j) % 4 * 8 for j in range(4)}
    for j in order:
        at = pl.ds(base[j], 8)
        remote(p.at[core, at], r1.at[at], s1.at[j], t1.at[j], sib).wait_recv()
        a1[at] = p[core, at] + r1[at]
        if j == 2:
            ring(a1.at[pl.ds(base[2], 4)], rp.at[0], 0, ahead)
            ring(a1.at[pl.ds(base[2] + 4, 4)], rm.at[0], 1, behind)
        elif j == 1:
            ring(a1.at[pl.ds(base[1] + 4, 4)], rp.at[1], 2, ahead)
        elif j == 3:
            ring(a1.at[pl.ds(base[3], 4)], rm.at[1], 3, behind)
    rings[0].wait_recv()
    at = pl.ds(base[1], 4)
    a1[at] = a1[at] + rp[0]
    ring(a1.at[at], rp.at[2], 4, ahead)
    rings[1].wait_recv()
    at = pl.ds(base[3] + 4, 4)
    a1[at] = a1[at] + rm[0]
    ring(a1.at[at], rm.at[2], 5, behind)
    for n in (2, 3):
        rings[n].wait_recv()
    at = pl.ds(base[0] + 4, 4)
    a2[4:8] = a1[at] + rp[1]
    at = pl.ds(base[0], 4)
    a2[0:4] = a1[at] + rm[1]
    rings[4].wait_recv()
    a2[0:4] = a2[0:4] + rp[2]
    rings[5].wait_recv()
    a2[4:8] = a2[4:8] + rm[2]
    if stop < 3:
        share.wait_recv()
        out_ref[...] = a2[0, :1, :1] + jnp.zeros((256, 256), F32)
        return finish()

    for n, (q, r) in enumerate(sheet):
        src = a2.at[q * 2 + r // 2, pl.ds(pl.multiple_of(r % 2 * 40, 8), 40)]
        copy = remote(src, r3.at[n], s3.at[n], t3.at[n], spots[n])
        copy.start()
        copies.append(copy)
    for n in range(15):
        remote(r3.at[n], r3.at[n], s3.at[n], t3.at[n], sib).wait_recv()
    mine = a2[b * 2 + y // 2, pl.ds(pl.multiple_of(y % 2 * 40, 8), 40)]
    terms = [mine] + [r3[n] for n in range(15)]
    while len(terms) > 1:
        terms = [u + v for u, v in zip(terms[::2], terms[1::2])]
    gath[1, member] = terms[0]
    if stop < 4:
        share.wait_recv()
        out_ref[...] = terms[0][:1, :1] + jnp.zeros((256, 256), F32)
        return finish()
    needs = {-1: pl.ds(0, 40), 0: pl.ds(16, 24), 1: pl.ds(32, 8)}
    for n, (delta, j, to) in enumerate(near):
        rows = needs[delta]
        copy = remote(
            gath.at[1, member, rows], gath.at[1 - delta, member, rows], s5.at[n],
            t5.at[1 - delta, member], to,
        )
        copy.start()
        copies.append(copy)
    for delta, j, _ in near:
        rows = needs[delta]
        m = (member + j) % 4
        remote(
            gath.at[1, member, rows], gath.at[1 - delta, m, rows], s5.at[0],
            t5.at[1 - delta, m], sib,
        ).wait_recv()
    if stop < 5:
        share.wait_recv()
        out_ref[...] = gath[2, 0, :1, :1] + jnp.zeros((256, 256), F32)
        return finish()

    wall[bin_] = solve(gath, steer_ref, bin_ % 2)
    share.wait_recv()
    sr[0:2] = sr[32:34]
    sr[34] = sr[2]
    if stop < 6:
        out_ref[...] = wall[bin_, :1].astype(F32) + jnp.zeros((256, 256), F32)
        return finish()
    for n, to in enumerate(bins):
        copy = remote(wall.at[bin_], wall.at[bin_], s6.at[n], t6.at[bin_], to * 4 + member)
        copy.start()
        copies.append(copy)

    for n in range(16):
        duo = (bin_ // 2 + 16 - n) % 16
        first = duo * 2
        waits = (first, first + 1) if n else (bin_ + 1 - 2 * (bin_ % 2),)
        for q in waits:
            remote(wall.at[q], wall.at[q], s6.at[0], t6.at[q], sib).wait_recv()
        lhs = wall[pl.ds(first, 2)].reshape(32, 256)
        rhs = jnp.concatenate(
            [
                s[pl.ds(first + 1, 4), :, 128:512].reshape(256, 384),
                sr[pl.ds(first + 1, 4)].reshape(256, 128),
            ],
            axis=1,
        )
        prod = jnp.dot(lhs, rhs, preferred_element_type=F32)
        top = jnp.concatenate([prod[0:8], prod[16:24]], axis=0)
        low = jnp.concatenate([prod[8:16], prod[24:32]], axis=0)
        beam = (top - turned(low)).astype(BF16)
        for i in range(2):
            rows = pl.ds(pl.multiple_of(256 * i + first * 8, 16), 16)
            table[rows] = beam[:, 256 * i : 256 * i + 256]
    if stop < 7:
        out_ref[...] = table[0:256].astype(F32)
        return finish()

    slots[...] = (
        jnp.dot(select[...], table[...], preferred_element_type=F32)
        .astype(BF16)
        .reshape(16, 16, 256)
    )
    for j, q in enumerate(planes):
        copy = remote(slots.at[q], d1.at[zx], s7.at[j], t7.at[j], q * 8 + yc)
        copy.start()
        copies.append(copy)
    d1[zx] = slots[zx]
    for j, q in enumerate(froms):
        remote(slots.at[q], d1.at[q], s7.at[j], t7.at[j], sib).wait_recv()
    mid[...] = (
        jnp.dot(turn[...], d1[...].reshape(256, 256), preferred_element_type=F32)
        .astype(BF16)
        .reshape(8, 32, 256)
    )
    if stop < 8:
        out_ref[...] = mid[...].reshape(256, 256).astype(F32)
        return finish()
    for j, q in enumerate(posts):
        copy = remote(mid.at[q], d2.at[yc], s8.at[j], t8.at[j], zx * 8 + q)
        copy.start()
        copies.append(copy)
    d2[yc] = mid[yc]
    for j in range(7):
        q = (yc + 7 - j) % 8
        remote(mid.at[q], d2.at[q], s8.at[j], t8.at[j], sib).wait_recv()
    rows = jnp.dot(back[...], d2[...].reshape(256, 256), preferred_element_type=F32)
    t, v = rows[:, :128], rows[:, 128:]
    low = lax.broadcasted_iota(jnp.int32, (256, 128), 1) < 64
    out_ref[:, :128] = jnp.where(low, t, pltpu.roll(v, 64, 1))
    out_ref[:, 128:] = jnp.where(low, pltpu.roll(t, 64, 1), v)
    finish()


def program(raw, replica, det_bin, det_block, det_beam, owner, stop, few):
    dma = pltpu.SemaphoreType.DMA
    vm = pltpu.VMEM
    rows = (1, 128)
    return pl.pallas_call(
        functools.partial(kernel, stop, few),
        out_shape=jax.ShapeDtypeStruct((256, 256), F32),
        in_specs=[HBM] * 8,
        out_specs=VMEM,
        scratch_shapes=[
            vm((2, 64, 32, 256), BF16),
            vm((64, 32, 128), BF16),
            vm((64, 32, 128), BF16),
            vm((64, 32, 128), BF16),
            vm((64, 32, 128), BF16),
            vm((640, 256), BF16),
            vm((640, 256), BF16),
            vm((35, 64, 512), BF16),
            vm((35, 64, 128), BF16),
            vm((2, 32, 80, 128), F32),
            vm((32, 80, 128), F32),
            vm((32, 80, 128), F32),
            vm((3, 4, 80, 128), F32),
            vm((3, 4, 80, 128), F32),
            vm((8, 80, 128), F32),
            vm((15, 40, 128), F32),
            vm((3, 4, 40, 128), F32),
            vm((32, 16, 256), BF16),
            vm((512, 256), BF16),
            vm((256, 512), BF16),
            vm((256, 256), BF16),
            vm((256, 256), BF16),
            vm((16, 16, 256), BF16),
            vm((16, 16, 256), BF16),
            vm((8, 32, 256), BF16),
            vm((8, 32, 256), BF16),
            vm((2, 128), BF16),
            vm((512, 256), BF16),
            vm((8, 128), F32),
            vm(rows, jnp.int32), vm(rows, jnp.int32), vm(rows, jnp.int32), vm(rows, jnp.int32),
            dma((4,)), dma((7,)), dma((2, 4)), dma((2, 4)),
            dma((4,)), dma((4,)), dma((6,)), dma((6,)), dma((15,)), dma((15,)),
            dma((11,)), dma((3, 4)), dma((31,)), dma((32,)),
            dma((15,)), dma((15,)), dma((7,)), dma((7,)), dma(()), dma(()),
        ],
        compiler_params=pltpu.CompilerParams(
            collective_id=0, has_side_effects=True, vmem_limit_bytes=LIMIT
        ),
        name="stap",
    )(
        raw, replica, jnp.asarray(dft_matrix()), jnp.asarray(steer_rows()),
        det_bin, det_block, det_beam, owner,
    )


def on_device(stop, few, raw, replica, det_bin, det_block, det_beam, det_owner):
    rows = [v.reshape(1, 128) for v in (det_bin, det_block, det_beam, det_owner)]
    return program(raw, replica, *rows, stop=stop, few=few)


def solution(mesh, stop=9, few=True):
    in_specs = (
        P(None, None, None, "range"),
        P(),
        P("range"),
        P("range"),
        P("range"),
        P("range", None),
    )
    return jax.shard_map(
        functools.partial(on_device, stop, few),
        mesh=mesh,
        in_specs=in_specs,
        out_specs=P("range", None),
        check_vma=False,
    )
```

```python
import functools
import math

import jax
import jax.numpy as jnp
import numpy as np
from jax import lax
from jax.experimental import pallas as pl
from jax.experimental.pallas import tpu as pltpu
from jax.sharding import PartitionSpec as P

C = 64
PULSES = 32
TAPS = 128
BEAMS = 8
F32 = jnp.float32
BF16 = jnp.bfloat16
MESH = pl.DeviceIdType.MESH
VMEM = pl.BlockSpec(memory_space=pltpu.VMEM)
HBM = pl.BlockSpec(memory_space=pltpu.HBM)
NT = (((1,), (1,)), ((), ()))
LIMIT = 63 * 1024 * 1024


def dft_matrix():
    index = np.arange(PULSES)
    angle = 2.0 * math.pi / PULSES * (index[:, None] * index[None, :] % PULSES)
    scale = PULSES**-0.5
    real = np.cos(angle) * scale
    imag = -np.sin(angle) * scale
    eye = np.eye(8)
    kr = np.einsum("pd,ab->dabp", real, eye).reshape(256, 256)
    ki = np.einsum("pd,ab->dabp", imag, eye).reshape(256, 256)
    full = np.concatenate([np.concatenate([kr, -ki], 1), np.concatenate([ki, kr], 1)], 0)
    return full.astype(jnp.bfloat16)


def steer_rows():
    sines = -0.8 + 1.6 * np.arange(BEAMS, dtype=np.float32) / np.float32(BEAMS - 1)
    angle = (math.pi * np.arange(C, dtype=np.float32)[None, :] * sines[:, None]).astype(np.float32)
    return np.concatenate([np.cos(angle), -np.sin(angle)], 1).astype(np.float32)


def remote(src, dst, send, recv, to):
    return pltpu.make_async_remote_copy(
        src_ref=src, dst_ref=dst, send_sem=send, recv_sem=recv, device_id=(to,), device_id_type=MESH
    )


def build_toeplitz(rep_ref, keep, tza, tz):
    def band(v):
        wide = jnp.concatenate(
            [jnp.broadcast_to(v, (TAPS, TAPS)), jnp.zeros((TAPS, TAPS), F32)], axis=1
        )
        return pltpu.roll(wide, 0, 1, stride=1, stride_axis=0).T

    rep = rep_ref[...].astype(F32)
    tr = band(rep[0:1])
    ti = band(rep[1:2])
    full = jnp.concatenate(
        [jnp.concatenate([tr, -ti], axis=1), jnp.concatenate([ti, tr], axis=1)], axis=0
    )
    tz[...] = full.astype(BF16)
    row = lax.broadcasted_iota(jnp.int32, (512, 256), 0) % 256
    lane = lax.broadcasted_iota(jnp.int32, (512, 256), 1) % 128
    tza[...] = jnp.where((row >= 64) & (lane < 64), full * keep, full).astype(BF16)


def join(*parts):
    return jnp.concatenate(parts, axis=-1)


def window_inner(at, raw, ur, ui):
    for n, u in enumerate((ur, ui)):
        u[at, :, 128:256] = join(raw[n, at, :, 64:128], raw[n, at, :, 128:192])


def window_edges(at, raw, hl, hr, ur, ui):
    for n, u in enumerate((ur, ui)):
        lanes = slice(64 * n, 64 * n + 64)
        u[at, :, 0:128] = join(hl[at, :, lanes], raw[n, at, :, 0:64])
        u[at, :, 256:384] = join(raw[n, at, :, 192:256], hr[at, :, lanes])


def spectra_part(i, ur, ui, dft_ref, s, tza, tz):
    first = 16 * i
    for b in range(2):
        ys = []
        for n in range(2):
            at = pl.ds(first + 8 * n, 8)
            gates = slice(128 * b, 128 * b + 256)
            window = join(ur[at, :, gates].reshape(256, 256), ui[at, :, gates].reshape(256, 256))
            band = tz[...] if b else tza[...]
            ys.append(jnp.dot(window, band, preferred_element_type=F32).astype(BF16))
        ya, yb = ys
        y = jnp.concatenate(
            [join(ya[:, :128], yb[:, :128]), join(ya[:, 128:], yb[:, 128:])], axis=0
        )
        out = jnp.dot(dft_ref[...], y, preferred_element_type=F32)
        for p in range(2):
            h = out[256 * p : 256 * p + 256]
            v = jnp.concatenate(
                [h[:, :128].reshape(32, 8, 128), h[:, 128:].reshape(32, 8, 128)], axis=1
            )
            lanes = 256 * b + 128 * p
            s[2:34, first : first + 16, lanes : lanes + 128] = v.astype(BF16)


def snake(k):
    z = k // 4
    x = k % 4
    return z, x + z % 2 * (3 - 2 * x)


def home(q):
    z, x = snake(q // 2)
    return z * 32 + x * 8 + q % 2 * 4


def beam_pair(first, wall, s, sr, table):
    lhs = wall[pl.ds(first, 2)].reshape(32, 256)
    rhs = join(
        s[pl.ds(first + 1, 4)].reshape(256, 512), sr[pl.ds(first + 1, 4)].reshape(256, 128)
    )
    prod = jnp.dot(lhs, rhs, preferred_element_type=F32)
    top = jnp.concatenate([prod[0:8], prod[16:24]], axis=0)
    low = jnp.concatenate([prod[8:16], prod[24:32]], axis=0)
    half = lax.broadcasted_iota(jnp.int32, (16, 128), 1) < 64

    def flip(v):
        return pltpu.roll(v, 64, 1)

    parts = []
    for at in (0, 256):
        parts.append(flip(top[:, at : at + 128] + low[:, at + 128 : at + 256]))
        parts.append(flip(top[:, at + 128 : at + 256] - low[:, at : at + 128]))
    turn = flip(low[:, 512:])
    last = top[:, 512:] + jnp.where(half, turn, -turn)
    lanes = [
        jnp.where(half, parts[0], parts[2]),
        jnp.where(half, parts[1], parts[3]),
        jnp.where(half, parts[2], flip(last)),
        jnp.where(half, parts[3], last),
    ]
    for i in range(2):
        rows = pl.ds(pl.multiple_of(256 * i + first * 8, 16), 16)
        table[rows] = join(*lanes[2 * i : 2 * i + 2]).astype(BF16)


def store_products(p, places, two, one, zero):
    lane = lax.broadcasted_iota(jnp.int32, (32, 128), 1)
    row = lax.broadcasted_iota(jnp.int32, (32, 128), 0)
    swapped = pltpu.roll(zero, 64, 1)
    top = jnp.where(row >= lane, zero[:32], swapped[:32])
    bottom = jnp.where(row + 32 >= lane - 64, swapped[32:], zero[32:])
    packed = jnp.where(lane < 64, top, bottom)
    for h in range(2):
        pos = places[h]
        for q in range(2):
            a = 32 * h + 16 * q
            p[h, pos, 40 * q : 40 * q + 16] = two[a : a + 16]
            p[h, pos, 40 * q + 16 : 40 * q + 32] = one[a : a + 16]
            p[h, pos, 40 * q + 32 : 40 * q + 40] = packed[a // 2 : a // 2 + 8]


def cross_products(z, x, s, p):
    f = 2 * (4 * z + x + z % 2 * (3 - 2 * x))
    lhs = s[pl.ds(f, 4)].reshape(256, 512)
    rhs = []
    for n in range(2):
        v = s[f + 2 + n]
        rhs += [v, join(-v[:, 128:256], v[:, :128], -v[:, 384:], v[:, 256:384])]
    prod = lax.dot_general(lhs, jnp.concatenate(rhs, axis=0), NT, preferred_element_type=F32)
    first, second = (z * 8 + x * 2, x * 8 + z * 2), (z * 8 + x * 2 + 1, x * 8 + z * 2 + 1)
    store_products(p, first, prod[:64, :128], prod[64:128, :128], prod[128:192, :128])
    store_products(p, second, prod[64:128, 128:], prod[128:192, 128:], prod[192:, 128:])


def times_i(m):
    return jnp.concatenate([-m[:, 64:], m[:, :64]], axis=1)


def cdot(x, y):
    return jnp.dot(
        x, jnp.concatenate([y, times_i(y)], axis=0),
        preferred_element_type=F32, precision=lax.Precision.HIGHEST,
    )


def adjoint(m):
    t = m.T
    return jnp.concatenate([t[:64], -t[64:]], axis=1)


def lane_of(v, k):
    return jnp.broadcast_to(v[:, k : k + 1], (8, 128))


def row_of(v, r):
    return jnp.broadcast_to(v[r : r + 1], (8, 128))


def cmul(x, y):
    return (x[0] * y[0] - x[1] * y[1], x[0] * y[1] + x[1] * y[0])


def cmulc(x, y):
    return (x[0] * y[0] + x[1] * y[1], x[1] * y[0] - x[0] * y[1])


def cadd(x, y):
    return (x[0] + y[0], x[1] + y[1])


def csub(x, y):
    return (x[0] - y[0], x[1] - y[1])


def cscale(x, c):
    return (x * c[0], x * c[1])


def conj(x):
    return (x[0], -x[1])


def size2(x):
    return x[0] * x[0] + x[1] * x[1]


def rdot(x, y):
    return x[0] * y[0] + x[1] * y[1]


def cm(c, row):
    v, w = row
    return (c[0] * v + c[1] * w, c[0] * w - c[1] * v)


def hermitian_inverse(m):
    lane = lax.broadcasted_iota(jnp.int32, (8, 128), 1)
    sub = lax.broadcasted_iota(jnp.int32, (8, 128), 0)
    ms = [m[8 * t : 8 * t + 8] for t in range(8)]
    for k in range(0, 64, 4):
        t0, r0 = divmod(k, 8)
        w = ms[t0]
        wi = times_i(w)
        cr = [[lane_of(v, k + j) for v in ms] for j in range(4)]
        ci = [[lane_of(v, 64 + k + j) for v in ms] for j in range(4)]

        def entry(i, j):
            return (row_of(cr[j][t0], r0 + i), row_of(ci[j][t0], r0 + i))

        a, d, b = entry(0, 0)[0], entry(1, 1)[0], entry(0, 1)
        p, s, q = entry(2, 2)[0], entry(3, 3)[0], entry(2, 3)
        bb = [[entry(0, 2), entry(0, 3)], [entry(1, 2), entry(1, 3)]]
        det = 1.0 / (a * d - size2(b))
        ia, id_, ib = d * det, a * det, cscale(-det, b)
        ww = [
            [cadd(cscale(ia, bb[0][j]), cmul(ib, bb[1][j])) for j in range(2)],
            [cadd(cmul(conj(ib), bb[0][j]), cscale(id_, bb[1][j])) for j in range(2)],
        ]
        s00 = p - (rdot(bb[0][0], ww[0][0]) + rdot(bb[1][0], ww[1][0]))
        s11 = s - (rdot(bb[0][1], ww[0][1]) + rdot(bb[1][1], ww[1][1]))
        s01 = csub(q, cadd(cmulc(ww[0][1], bb[0][0]), cmulc(ww[1][1], bb[1][0])))
        dets = 1.0 / (s00 * s11 - size2(s01))
        j00, j11, j01 = s11 * dets, s00 * dets, cscale(-dets, s01)
        hit = ((lane >= k) & (lane < k + 4)) | ((lane >= 64 + k) & (lane < 68 + k))
        rows = []
        for j in range(4):
            real = jnp.where(hit, jnp.where(lane == k + j, 1.0, 0.0), row_of(w, r0 + j))
            imag = jnp.where(hit, jnp.where(lane == 64 + k + j, 1.0, 0.0), row_of(wi, r0 + j))
            rows.append((real, imag))
        t2 = csub(rows[2], cadd(cm(conj(ww[0][0]), rows[0]), cm(conj(ww[1][0]), rows[1])))
        t3 = csub(rows[3], cadd(cm(conj(ww[0][1]), rows[0]), cm(conj(ww[1][1]), rows[1])))
        x2 = cadd(cscale(j00, t2), cm(j01, t3))
        x3 = cadd(cscale(j11, t3), cm(conj(j01), t2))
        u0 = cadd(cscale(ia, rows[0]), cm(ib, rows[1]))
        u1 = cadd(cscale(id_, rows[1]), cm(conj(ib), rows[0]))
        x0 = csub(u0, cadd(cm(ww[0][0], x2), cm(ww[0][1], x3)))
        x1 = csub(u1, cadd(cm(ww[1][0], x2), cm(ww[1][1], x3)))
        g = [x0, x1, x2, x3]
        for t in range(8):
            terms = [cr[j][t] * g[j][0] + ci[j][t] * g[j][1] for j in range(4)]
            mt = jnp.where(hit, 0.0, ms[t]) - ((terms[0] + terms[1]) + (terms[2] + terms[3]))
            if t == t0:
                for j in range(4):
                    mt = jnp.where(sub == r0 + j, g[j][0], mt)
            ms[t] = mt
    return jnp.concatenate(ms, axis=0)


def solve(g_ref, steer_ref, parity):
    scale = 1.0 / 32768.0
    order = (0, 2, 1, 3)
    r64 = lax.broadcasted_iota(jnp.int32, (64, 64), 0)
    c64 = lax.broadcasted_iota(jnp.int32, (64, 64), 1)

    def block(g, rows):
        return jnp.concatenate([g_ref[g, m, rows] for m in order], axis=0) * scale

    def diagonal(g):
        pk = block(g, slice(32, 40))
        k = jnp.concatenate([pk[:, :64], pk[:, 64:]], axis=0)
        kt = k.T
        real = jnp.where(r64 >= c64, k, kt)
        imag = jnp.where(r64 < c64, k, jnp.where(r64 == c64, 0.0, -kt))
        return jnp.concatenate([real, imag], axis=1)

    a11 = diagonal(0)
    a33 = diagonal(1)
    a22 = diagonal(2)
    a12 = block(2, slice(0, 16))
    a13 = block(1, slice(16, 32))
    a32 = block(2, slice(16, 32))
    p = hermitian_inverse(a11)
    v21 = cdot(adjoint(a12), p)
    v31 = cdot(adjoint(a13), p)
    s22 = a22 - cdot(v21, a12)
    s32 = a32 - cdot(v31, a12)
    s33 = a33 - cdot(v31, a13)
    q = hermitian_inverse(s22)
    v32 = cdot(s32, q)
    s33 = s33 - cdot(v32, adjoint(s32))
    r = hermitian_inverse(s33)
    t = steer_ref[...]
    y3 = cdot(t, r)
    y2 = -cdot(y3, v32)
    y1 = -cdot(y2, v21) - cdot(y3, v31)
    norm = lax.rsqrt(jnp.sum(t * y3, axis=1, keepdims=True))
    real = [(v[:, :64] * norm) for v in (y1, y3, y2)]
    imag = [(v[:, 64:] * -norm) for v in (y1, y3, y2)]
    rows = jnp.concatenate(
        [jnp.concatenate(real, axis=1), jnp.concatenate(imag, axis=1)], axis=0
    )
    zero = jnp.zeros((16, 64), F32)
    even = jnp.concatenate([rows, zero], axis=1)
    odd = jnp.concatenate([zero, rows], axis=1)
    return jnp.where(parity == 0, even, odd).astype(BF16)


def selection(bin_ref, block_ref, beam_ref, owner_ref, select, turn, back):
    s_iota = lax.broadcasted_iota(jnp.int32, (256, 128), 0)
    named = (s_iota // 2 == owner_ref[...]).astype(F32)
    before = (
        lax.broadcasted_iota(jnp.int32, (128, 128), 0)
        < lax.broadcasted_iota(jnp.int32, (128, 128), 1)
    ).astype(F32)
    earlier = jnp.dot(named.astype(BF16), before.astype(BF16), preferred_element_type=F32)
    pick = jnp.where(earlier == (s_iota % 2).astype(F32), named, 0.0).astype(BF16)
    wanted = block_ref[...] * 256 + bin_ref[...] * 8 + beam_ref[...]
    t_iota = lax.broadcasted_iota(jnp.int32, (512, 128), 0)
    holds = (t_iota == wanted).astype(F32).astype(BF16)
    select[...] = lax.dot_general(pick, holds, NT, preferred_element_type=F32).astype(BF16)
    o = lax.broadcasted_iota(jnp.int32, (256, 256), 0)
    i = lax.broadcasted_iota(jnp.int32, (256, 256), 1)
    turn[...] = (i == o % 32 // 2 * 16 + o // 32 * 2 + o % 2).astype(F32).astype(BF16)
    back[...] = (i == o % 16 // 2 * 32 + o // 16 * 2 + o % 2).astype(F32).astype(BF16)


def kernel(
    stop, few,
    raw_ref, rep_in, dft_in, steer_in, bin_in, block_in, beam_in, owner_in,
    out_ref,
    raw, pkl, pkr, hl, hr, ur, ui, tza, tz, s, pks, sr, p, r1, a1, rp, rm, a2, r3, gath, wall, table,
    select, turn, back, slots, d1, mid, d2,
    rep_ref, dft_ref, steer_ref, bin_ref, block_ref, beam_ref, owner_ref,
    ls, ms, hs, ht, s1, t1, s2, t2, s3, t3, s5, t5, s6, t6, s7, t7, s8, t8, s9, t9,
):
    me = lax.axis_index("range")
    core = me % 2
    y = me // 2 % 4
    x = me // 8 % 4
    z = me // 32
    zx = me // 8
    yc = me % 8
    bin_ = 2 * (4 * z + x + z % 2 * (3 - 2 * x)) + y // 2
    member = me % 4
    sib = me + 1 - 2 * core
    sa = 32 - 24 * core
    sb = 8 + 24 * core
    a = me // sa % 4
    b = me // sb % 4
    left = (me + 127) % 128
    right = (me + 1) % 128

    def along(stride, coord, j):
        return me + ((coord + j) % 4 - coord) * stride

    near = []
    for delta in (-1, 0, 1):
        for j in range(4):
            if delta or j:
                near.append((delta, j, home((bin_ + delta + 32) % 32) + (member + j) % 4))
    bins = [(bin_ + j) % 32 for j in range(1, 32)]
    planes = [(z + j // 4) % 4 * 4 + (x + j % 4) % 4 for j in range(1, 16)]
    froms = [(z + 4 - j // 4) % 4 * 4 + (x + 4 - j % 4) % 4 for j in range(1, 16)]
    posts = [(yc + j) % 8 for j in range(1, 8)]
    sheet = [
        ((b + j // 4) % 4, (y + j % 4) % 4)
        for j in (10, 9, 11, 6, 14, 2, 8, 5, 7, 13, 15, 1, 3, 4, 12)
    ]
    spots = [me + (q - b) * sb + (r - y) * 2 for q, r in sheet]
    partners = [left, right, sib, along(sa, a, 1), along(sa, a, 3)] + spots
    if not few:
        partners += [to for _, _, to in near] + [home(q) + member for q in bins]
        partners += [q * 8 + yc for q in planes] + [zx * 8 + q for q in posts]

    small = [
        pltpu.make_async_copy(src, dst, ms.at[n])
        for n, (src, dst) in enumerate(
            [
                (rep_in, rep_ref), (dft_in, dft_ref), (steer_in, steer_ref), (bin_in, bin_ref),
                (block_in, block_ref), (beam_in, beam_ref), (owner_in, owner_ref),
            ]
        )
    ]
    small[0].start()
    loads = []
    for i in range(4):
        at = pl.ds(16 * i, 16)
        copy = pltpu.make_async_copy(raw_ref.at[:, at], raw.at[:, at], ls.at[i])
        copy.start()
        loads.append(copy)
    for copy in small[1:]:
        copy.start()
    barrier = pltpu.get_barrier_semaphore()
    for to in partners:
        pl.semaphore_signal(barrier, inc=1, device_id=(to,), device_id_type=MESH)
    for i in range(4):
        at = pl.ds(16 * i, 16)
        loads[i].wait()
        pkl[at] = jnp.concatenate([raw[0, at, :, 0:64], raw[1, at, :, 0:64]], axis=-1)
        pkr[at] = jnp.concatenate([raw[0, at, :, 192:256], raw[1, at, :, 192:256]], axis=-1)
        window_inner(at, raw, ur, ui)
    pl.semaphore_wait(barrier, len(partners))
    copies = []

    def finish():
        for copy in copies:
            copy.wait_send()

    if stop < 0:
        for copy in small:
            copy.wait()
        out_ref[...] = pkl[0, :1, :1].astype(F32) + jnp.zeros((256, 256), F32)
        return finish()

    def to_left(i):
        at = pl.ds(16 * i, 16)
        return remote(pkl.at[at], hr.at[at], hs.at[0, i], ht.at[0, i], left)

    for i in range(4):
        at = pl.ds(16 * i, 16)
        copy = remote(pkr.at[at], hl.at[at], hs.at[1, i], ht.at[1, i], right)
        copy.start()
        copies.append(copy)

        @pl.when(me > 0)
        def _():
            to_left(i).start()

    @pl.when(me == 127)
    def _():
        hr[...] = jnp.zeros_like(hr)

    small[0].wait()
    build_toeplitz(rep_ref, jnp.where(me > 0, 1.0, 0.0).astype(F32), tza, tz)
    for copy in small[1:]:
        copy.wait()
    selection(bin_ref, block_ref, beam_ref, owner_ref, select, turn, back)
    for i in range(4):
        copies[i].wait_recv()

        @pl.when(me < 127)
        def _():
            to_left(i).wait_recv()

        window_edges(pl.ds(16 * i, 16), raw, hl, hr, ur, ui)
        spectra_part(i, ur, ui, dft_ref, s, tza, tz)

    @pl.when(me > 0)
    def _():
        for i in range(4):
            to_left(i).wait_send()

    s[0:2] = s[32:34]
    s[34] = s[2]
    pks[...] = join(s[2:34, :, 0:64], s[2:34, :, 128:192])
    share = remote(pks, sr.at[pl.ds(2, 32)], s9, t9, left)
    if stop < 1:
        out_ref[...] = s[0, :1, :256].astype(F32) + jnp.zeros((256, 256), F32)
        return finish()

    order = (2, 1, 3, 0)
    oa = me // sb % 4
    for j in order:
        q = (oa + j) % 4
        for u in range(4):
            cross_products(core * q + (1 - core) * u, core * u + (1 - core) * q, s, p)
        at = pl.ds(q * 8, 8)
        copy = remote(p.at[1 - core, at], r1.at[at], s1.at[j], t1.at[j], sib)
        copy.start()
        copies.append(copy)
    share.start()
    copies.append(share)
    if stop < 2:
        for j in order:
            at = pl.ds((a + j) % 4 * 8, 8)
            remote(p.at[core, at], r1.at[at], s1.at[j], t1.at[j], sib).wait_recv()
        share.wait_recv()
        out_ref[...] = p[0, 0, :1, :1] + jnp.zeros((256, 256), F32)
        return finish()

    rings = []

    def ring(src, dst, n, to):
        copy = remote(src, dst, s2.at[n], t2.at[n], to)
        copy.start()
        copies.append(copy)
        rings.append(copy)

    ahead, behind = along(sa, a, 1), along(sa, a, 3)
    base = {j: (a + j) % 4 * 8 for j in range(4)}
    for j in order:
        at = pl.ds(base[j], 8)
        remote(p.at[core, at], r1.at[at], s1.at[j], t1.at[j], sib).wait_recv()
        a1[at] = p[core, at] + r1[at]
        if j == 2:
            ring(a1.at[pl.ds(base[2], 4)], rp.at[0], 0, ahead)
            ring(a1.at[pl.ds(base[2] + 4, 4)], rm.at[0], 1, behind)
        elif j == 1:
            ring(a1.at[pl.ds(base[1] + 4, 4)], rp.at[1], 2, ahead)
        elif j == 3:
            ring(a1.at[pl.ds(base[3], 4)], rm.at[1], 3, behind)
    rings[0].wait_recv()
    at = pl.ds(base[1], 4)
    a1[at] = a1[at] + rp[0]
    ring(a1.at[at], rp.at[2], 4, ahead)
    rings[1].wait_recv()
    at = pl.ds(base[3] + 4, 4)
    a1[at] = a1[at] + rm[0]
    ring(a1.at[at], rm.at[2], 5, behind)
    for n in (2, 3):
        rings[n].wait_recv()
    at = pl.ds(base[0] + 4, 4)
    a2[4:8] = a1[at] + rp[1]
    at = pl.ds(base[0], 4)
    a2[0:4] = a1[at] + rm[1]
    rings[4].wait_recv()
    a2[0:4] = a2[0:4] + rp[2]
    rings[5].wait_recv()
    a2[4:8] = a2[4:8] + rm[2]
    if stop < 3:
        share.wait_recv()
        out_ref[...] = a2[0, :1, :1] + jnp.zeros((256, 256), F32)
        return finish()

    for n, (q, r) in enumerate(sheet):
        src = a2.at[q * 2 + r // 2, pl.ds(pl.multiple_of(r % 2 * 40, 8), 40)]
        copy = remote(src, r3.at[n], s3.at[n], t3.at[n], spots[n])
        copy.start()
        copies.append(copy)
    for n in range(15):
        remote(r3.at[n], r3.at[n], s3.at[n], t3.at[n], sib).wait_recv()
    mine = a2[b * 2 + y // 2, pl.ds(pl.multiple_of(y % 2 * 40, 8), 40)]
    terms = [mine] + [r3[n] for n in range(15)]
    while len(terms) > 1:
        terms = [u + v for u, v in zip(terms[::2], terms[1::2])]
    gath[1, member] = terms[0]
    if stop < 4:
        share.wait_recv()
        out_ref[...] = terms[0][:1, :1] + jnp.zeros((256, 256), F32)
        return finish()
    needs = {-1: pl.ds(0, 40), 0: pl.ds(16, 24), 1: pl.ds(32, 8)}
    for n, (delta, j, to) in enumerate(near):
        rows = needs[delta]
        copy = remote(
            gath.at[1, member, rows], gath.at[1 - delta, member, rows], s5.at[n],
            t5.at[1 - delta, member], to,
        )
        copy.start()
        copies.append(copy)
    for delta, j, _ in near:
        rows = needs[delta]
        m = (member + j) % 4
        remote(
            gath.at[1, member, rows], gath.at[1 - delta, m, rows], s5.at[0],
            t5.at[1 - delta, m], sib,
        ).wait_recv()
    if stop < 5:
        share.wait_recv()
        out_ref[...] = gath[2, 0, :1, :1] + jnp.zeros((256, 256), F32)
        return finish()

    wall[bin_] = solve(gath, steer_ref, bin_ % 2)
    share.wait_recv()
    sr[0:2] = sr[32:34]
    sr[34] = sr[2]
    if stop < 6:
        out_ref[...] = wall[bin_, :1].astype(F32) + jnp.zeros((256, 256), F32)
        return finish()
    for n, to in enumerate(bins):
        copy = remote(wall.at[bin_], wall.at[bin_], s6.at[n], t6.at[bin_], home(to) + member)
        copy.start()
        copies.append(copy)

    for n in range(16):
        duo = (bin_ // 2 + 16 - n) % 16
        first = duo * 2
        waits = (first, first + 1) if n else (bin_ + 1 - 2 * (bin_ % 2),)
        for q in waits:
            remote(wall.at[q], wall.at[q], s6.at[0], t6.at[q], sib).wait_recv()
        beam_pair(first, wall, s, sr, table)
    if stop < 7:
        out_ref[...] = table[0:256].astype(F32)
        return finish()

    slots[...] = (
        jnp.dot(select[...], table[...], preferred_element_type=F32)
        .astype(BF16)
        .reshape(16, 16, 256)
    )
    for j, q in enumerate(planes):
        copy = remote(slots.at[q], d1.at[zx], s7.at[j], t7.at[j], q * 8 + yc)
        copy.start()
        copies.append(copy)
    d1[zx] = slots[zx]
    for j, q in enumerate(froms):
        remote(slots.at[q], d1.at[q], s7.at[j], t7.at[j], sib).wait_recv()
    mid[...] = (
        jnp.dot(turn[...], d1[...].reshape(256, 256), preferred_element_type=F32)
        .astype(BF16)
        .reshape(8, 32, 256)
    )
    if stop < 8:
        out_ref[...] = mid[...].reshape(256, 256).astype(F32)
        return finish()
    for j, q in enumerate(posts):
        copy = remote(mid.at[q], d2.at[yc], s8.at[j], t8.at[j], zx * 8 + q)
        copy.start()
        copies.append(copy)
    d2[yc] = mid[yc]
    for j in range(7):
        q = (yc + 7 - j) % 8
        remote(mid.at[q], d2.at[q], s8.at[j], t8.at[j], sib).wait_recv()
    out_ref[...] = jnp.dot(back[...], d2[...].reshape(256, 256), preferred_element_type=F32)
    finish()


def program(raw, replica, det_bin, det_block, det_beam, owner, stop, few):
    dma = pltpu.SemaphoreType.DMA
    vm = pltpu.VMEM
    rows = (1, 128)
    return pl.pallas_call(
        functools.partial(kernel, stop, few),
        out_shape=jax.ShapeDtypeStruct((256, 256), F32),
        in_specs=[HBM] * 8,
        out_specs=VMEM,
        scratch_shapes=[
            vm((2, 64, 32, 256), BF16),
            vm((64, 32, 128), BF16),
            vm((64, 32, 128), BF16),
            vm((64, 32, 128), BF16),
            vm((64, 32, 128), BF16),
            vm((64, 32, 384), BF16),
            vm((64, 32, 384), BF16),
            vm((512, 256), BF16),
            vm((512, 256), BF16),
            vm((35, 64, 512), BF16),
            vm((32, 64, 128), BF16),
            vm((35, 64, 128), BF16),
            vm((2, 32, 80, 128), F32),
            vm((32, 80, 128), F32),
            vm((32, 80, 128), F32),
            vm((3, 4, 80, 128), F32),
            vm((3, 4, 80, 128), F32),
            vm((8, 80, 128), F32),
            vm((15, 40, 128), F32),
            vm((3, 4, 40, 128), F32),
            vm((32, 16, 256), BF16),
            vm((512, 256), BF16),
            vm((256, 512), BF16),
            vm((256, 256), BF16),
            vm((256, 256), BF16),
            vm((16, 16, 256), BF16),
            vm((16, 16, 256), BF16),
            vm((8, 32, 256), BF16),
            vm((8, 32, 256), BF16),
            vm((2, 128), BF16),
            vm((512, 512), BF16),
            vm((8, 128), F32),
            vm(rows, jnp.int32), vm(rows, jnp.int32), vm(rows, jnp.int32), vm(rows, jnp.int32),
            dma((4,)), dma((7,)), dma((2, 4)), dma((2, 4)),
            dma((4,)), dma((4,)), dma((6,)), dma((6,)), dma((15,)), dma((15,)),
            dma((11,)), dma((3, 4)), dma((31,)), dma((32,)),
            dma((15,)), dma((15,)), dma((7,)), dma((7,)), dma(()), dma(()),
        ],
        compiler_params=pltpu.CompilerParams(
            collective_id=0, has_side_effects=True, vmem_limit_bytes=LIMIT
        ),
        name="stap",
    )(
        raw, replica, jnp.asarray(dft_matrix()), jnp.asarray(steer_rows()),
        det_bin, det_block, det_beam, owner,
    )


def on_device(stop, few, raw, replica, det_bin, det_block, det_beam, det_owner):
    rows = [v.reshape(1, 128) for v in (det_bin, det_block, det_beam, det_owner)]
    return program(raw, replica, *rows, stop=stop, few=few)


def solution(mesh, stop=9, few=True):
    in_specs = (
        P(None, None, None, "range"),
        P(),
        P("range"),
        P("range"),
        P("range"),
        P("range", None),
    )
    return jax.shard_map(
        functools.partial(on_device, stop, few),
        mesh=mesh,
        in_specs=in_specs,
        out_specs=P("range", None),
        check_vma=False,
    )
```

```python
import functools
import math

import jax
import jax.numpy as jnp
import numpy as np
from jax import lax
from jax.experimental import pallas as pl
from jax.experimental.pallas import tpu as pltpu
from jax.sharding import PartitionSpec as P

C = 64
PULSES = 32
TAPS = 128
BEAMS = 8
F32 = jnp.float32
BF16 = jnp.bfloat16
MESH = pl.DeviceIdType.MESH
VMEM = pl.BlockSpec(memory_space=pltpu.VMEM)
HBM = pl.BlockSpec(memory_space=pltpu.HBM)
NT = (((1,), (1,)), ((), ()))
LIMIT = 63 * 1024 * 1024


def dft_matrix():
    index = np.arange(PULSES)
    angle = 2.0 * math.pi / PULSES * (index[:, None] * index[None, :] % PULSES)
    scale = PULSES**-0.5
    real = np.cos(angle) * scale
    imag = -np.sin(angle) * scale
    eye = np.eye(8)
    kr = np.einsum("pd,ab->dabp", real, eye).reshape(256, 256)
    ki = np.einsum("pd,ab->dabp", imag, eye).reshape(256, 256)
    full = np.concatenate([np.concatenate([kr, -ki], 1), np.concatenate([ki, kr], 1)], 0)
    return full.astype(jnp.bfloat16)


def steer_rows():
    sines = -0.8 + 1.6 * np.arange(BEAMS, dtype=np.float32) / np.float32(BEAMS - 1)
    angle = (math.pi * np.arange(C, dtype=np.float32)[None, :] * sines[:, None]).astype(np.float32)
    return np.concatenate([np.cos(angle), -np.sin(angle)], 1).astype(np.float32)


def remote(src, dst, send, recv, to):
    return pltpu.make_async_remote_copy(
        src_ref=src, dst_ref=dst, send_sem=send, recv_sem=recv, device_id=(to,), device_id_type=MESH
    )


def build_toeplitz(rep_ref, keep, tza, tz):
    def band(v):
        wide = jnp.concatenate(
            [jnp.broadcast_to(v, (TAPS, TAPS)), jnp.zeros((TAPS, TAPS), F32)], axis=1
        )
        return pltpu.roll(wide, 0, 1, stride=1, stride_axis=0).T

    rep = rep_ref[...].astype(F32)
    tr = band(rep[0:1])
    ti = band(rep[1:2])
    full = jnp.concatenate(
        [jnp.concatenate([tr, -ti], axis=1), jnp.concatenate([ti, tr], axis=1)], axis=0
    )
    tz[...] = full.astype(BF16)
    row = lax.broadcasted_iota(jnp.int32, (512, 256), 0) % 256
    lane = lax.broadcasted_iota(jnp.int32, (512, 256), 1) % 128
    tza[...] = jnp.where((row >= 64) & (lane < 64), full * keep, full).astype(BF16)


def join(*parts):
    return jnp.concatenate(parts, axis=-1)


def window_inner(at, raw, ur, ui):
    for n, u in enumerate((ur, ui)):
        u[at, :, 128:256] = join(raw[n, at, :, 64:128], raw[n, at, :, 128:192])


def window_edges(at, raw, hl, hr, ur, ui):
    for n, u in enumerate((ur, ui)):
        lanes = slice(64 * n, 64 * n + 64)
        u[at, :, 0:128] = join(hl[at, :, lanes], raw[n, at, :, 0:64])
        u[at, :, 256:384] = join(raw[n, at, :, 192:256], hr[at, :, lanes])


def spectra_part(i, ur, ui, dft_ref, s, tza, tz):
    first = 16 * i
    for b in range(2):
        ys = []
        for n in range(2):
            at = pl.ds(first + 8 * n, 8)
            gates = slice(128 * b, 128 * b + 256)
            window = join(ur[at, :, gates].reshape(256, 256), ui[at, :, gates].reshape(256, 256))
            band = tz[...] if b else tza[...]
            ys.append(jnp.dot(window, band, preferred_element_type=F32).astype(BF16))
        ya, yb = ys
        y = jnp.concatenate(
            [join(ya[:, :128], yb[:, :128]), join(ya[:, 128:], yb[:, 128:])], axis=0
        )
        out = jnp.dot(dft_ref[...], y, preferred_element_type=F32)
        for p in range(2):
            h = out[256 * p : 256 * p + 256]
            v = jnp.concatenate(
                [h[:, :128].reshape(32, 8, 128), h[:, 128:].reshape(32, 8, 128)], axis=1
            )
            lanes = 256 * b + 128 * p
            s[2:34, first : first + 16, lanes : lanes + 128] = v.astype(BF16)


def snake(k):
    z = k // 4
    x = k % 4
    return z, x + z % 2 * (3 - 2 * x)


def home(q):
    z, x = snake(q // 2)
    return z * 32 + x * 8 + q % 2 * 4


def facing(q, mine, member):
    return home(q) + (member // 2 + q + mine) % 2 * 2 + member % 2


def beam_pair(first, wall, s, sr, table):
    lhs = wall[pl.ds(first, 2)].reshape(32, 256)
    rhs = join(
        s[pl.ds(first + 1, 4)].reshape(256, 512), sr[pl.ds(first + 1, 4)].reshape(256, 128)
    )
    prod = jnp.dot(lhs, rhs, preferred_element_type=F32)
    top = jnp.concatenate([prod[0:8], prod[16:24]], axis=0)
    low = jnp.concatenate([prod[8:16], prod[24:32]], axis=0)
    half = lax.broadcasted_iota(jnp.int32, (16, 128), 1) < 64

    def flip(v):
        return pltpu.roll(v, 64, 1)

    parts = []
    for at in (0, 256):
        parts.append(flip(top[:, at : at + 128] + low[:, at + 128 : at + 256]))
        parts.append(flip(top[:, at + 128 : at + 256] - low[:, at : at + 128]))
    turn = flip(low[:, 512:])
    last = top[:, 512:] + jnp.where(half, turn, -turn)
    lanes = [
        jnp.where(half, parts[0], parts[2]),
        jnp.where(half, parts[1], parts[3]),
        jnp.where(half, parts[2], flip(last)),
        jnp.where(half, parts[3], last),
    ]
    for i in range(2):
        rows = pl.ds(pl.multiple_of(256 * i + first * 8, 16), 16)
        table[rows] = join(*lanes[2 * i : 2 * i + 2]).astype(BF16)


def store_products(p, places, two, one, zero):
    lane = lax.broadcasted_iota(jnp.int32, (32, 128), 1)
    row = lax.broadcasted_iota(jnp.int32, (32, 128), 0)
    swapped = pltpu.roll(zero, 64, 1)
    top = jnp.where(row >= lane, zero[:32], swapped[:32])
    bottom = jnp.where(row + 32 >= lane - 64, swapped[32:], zero[32:])
    packed = jnp.where(lane < 64, top, bottom)
    for h in range(2):
        pos = places[h]
        for q in range(2):
            a = 32 * h + 16 * q
            p[h, pos, 40 * q : 40 * q + 16] = two[a : a + 16]
            p[h, pos, 40 * q + 16 : 40 * q + 32] = one[a : a + 16]
            p[h, pos, 40 * q + 32 : 40 * q + 40] = packed[a // 2 : a // 2 + 8]


def cross_products(z, x, s, p):
    f = 2 * (4 * z + x + z % 2 * (3 - 2 * x))
    lhs = s[pl.ds(f, 4)].reshape(256, 512)
    rhs = []
    for n in range(2):
        v = s[f + 2 + n]
        rhs += [v, join(-v[:, 128:256], v[:, :128], -v[:, 384:], v[:, 256:384])]
    prod = lax.dot_general(lhs, jnp.concatenate(rhs, axis=0), NT, preferred_element_type=F32)
    first, second = (z * 8 + x * 2, x * 8 + z * 2), (z * 8 + x * 2 + 1, x * 8 + z * 2 + 1)
    store_products(p, first, prod[:64, :128], prod[64:128, :128], prod[128:192, :128])
    store_products(p, second, prod[64:128, 128:], prod[128:192, 128:], prod[192:, 128:])


def times_i(m):
    return jnp.concatenate([-m[:, 64:], m[:, :64]], axis=1)


def cdot(x, y):
    return jnp.dot(
        x, jnp.concatenate([y, times_i(y)], axis=0),
        preferred_element_type=F32, precision=lax.Precision.HIGHEST,
    )


def adjoint(m):
    t = m.T
    return jnp.concatenate([t[:64], -t[64:]], axis=1)


def lane_of(v, k):
    return jnp.broadcast_to(v[:, k : k + 1], (8, 128))


def row_of(v, r):
    return jnp.broadcast_to(v[r : r + 1], (8, 128))


def cmul(x, y):
    return (x[0] * y[0] - x[1] * y[1], x[0] * y[1] + x[1] * y[0])


def cmulc(x, y):
    return (x[0] * y[0] + x[1] * y[1], x[1] * y[0] - x[0] * y[1])


def cadd(x, y):
    return (x[0] + y[0], x[1] + y[1])


def csub(x, y):
    return (x[0] - y[0], x[1] - y[1])


def cscale(x, c):
    return (x * c[0], x * c[1])


def conj(x):
    return (x[0], -x[1])


def size2(x):
    return x[0] * x[0] + x[1] * x[1]


def rdot(x, y):
    return x[0] * y[0] + x[1] * y[1]


def cm(c, row):
    v, w = row
    return (c[0] * v + c[1] * w, c[0] * w - c[1] * v)


def hermitian_inverse(m):
    lane = lax.broadcasted_iota(jnp.int32, (8, 128), 1)
    sub = lax.broadcasted_iota(jnp.int32, (8, 128), 0)
    ms = [m[8 * t : 8 * t + 8] for t in range(8)]
    for k in range(0, 64, 4):
        t0, r0 = divmod(k, 8)
        w = ms[t0]
        wi = times_i(w)
        cr = [[lane_of(v, k + j) for v in ms] for j in range(4)]
        ci = [[lane_of(v, 64 + k + j) for v in ms] for j in range(4)]

        def entry(i, j):
            return (row_of(cr[j][t0], r0 + i), row_of(ci[j][t0], r0 + i))

        a, d, b = entry(0, 0)[0], entry(1, 1)[0], entry(0, 1)
        p, s, q = entry(2, 2)[0], entry(3, 3)[0], entry(2, 3)
        bb = [[entry(0, 2), entry(0, 3)], [entry(1, 2), entry(1, 3)]]
        det = 1.0 / (a * d - size2(b))
        ia, id_, ib = d * det, a * det, cscale(-det, b)
        ww = [
            [cadd(cscale(ia, bb[0][j]), cmul(ib, bb[1][j])) for j in range(2)],
            [cadd(cmul(conj(ib), bb[0][j]), cscale(id_, bb[1][j])) for j in range(2)],
        ]
        s00 = p - (rdot(bb[0][0], ww[0][0]) + rdot(bb[1][0], ww[1][0]))
        s11 = s - (rdot(bb[0][1], ww[0][1]) + rdot(bb[1][1], ww[1][1]))
        s01 = csub(q, cadd(cmulc(ww[0][1], bb[0][0]), cmulc(ww[1][1], bb[1][0])))
        dets = 1.0 / (s00 * s11 - size2(s01))
        j00, j11, j01 = s11 * dets, s00 * dets, cscale(-dets, s01)
        hit = ((lane >= k) & (lane < k + 4)) | ((lane >= 64 + k) & (lane < 68 + k))
        rows = []
        for j in range(4):
            real = jnp.where(hit, jnp.where(lane == k + j, 1.0, 0.0), row_of(w, r0 + j))
            imag = jnp.where(hit, jnp.where(lane == 64 + k + j, 1.0, 0.0), row_of(wi, r0 + j))
            rows.append((real, imag))
        t2 = csub(rows[2], cadd(cm(conj(ww[0][0]), rows[0]), cm(conj(ww[1][0]), rows[1])))
        t3 = csub(rows[3], cadd(cm(conj(ww[0][1]), rows[0]), cm(conj(ww[1][1]), rows[1])))
        x2 = cadd(cscale(j00, t2), cm(j01, t3))
        x3 = cadd(cscale(j11, t3), cm(conj(j01), t2))
        u0 = cadd(cscale(ia, rows[0]), cm(ib, rows[1]))
        u1 = cadd(cscale(id_, rows[1]), cm(conj(ib), rows[0]))
        x0 = csub(u0, cadd(cm(ww[0][0], x2), cm(ww[0][1], x3)))
        x1 = csub(u1, cadd(cm(ww[1][0], x2), cm(ww[1][1], x3)))
        g = [x0, x1, x2, x3]
        for t in range(8):
            terms = [cr[j][t] * g[j][0] + ci[j][t] * g[j][1] for j in range(4)]
            mt = jnp.where(hit, 0.0, ms[t]) - ((terms[0] + terms[1]) + (terms[2] + terms[3]))
            if t == t0:
                for j in range(4):
                    mt = jnp.where(sub == r0 + j, g[j][0], mt)
            ms[t] = mt
    return jnp.concatenate(ms, axis=0)


def solve(g_ref, steer_ref, parity):
    scale = 1.0 / 32768.0
    order = (0, 2, 1, 3)
    r64 = lax.broadcasted_iota(jnp.int32, (64, 64), 0)
    c64 = lax.broadcasted_iota(jnp.int32, (64, 64), 1)

    def block(g, rows):
        return jnp.concatenate([g_ref[g, m, rows] for m in order], axis=0) * scale

    def diagonal(g):
        pk = block(g, slice(32, 40))
        k = jnp.concatenate([pk[:, :64], pk[:, 64:]], axis=0)
        kt = k.T
        real = jnp.where(r64 >= c64, k, kt)
        imag = jnp.where(r64 < c64, k, jnp.where(r64 == c64, 0.0, -kt))
        return jnp.concatenate([real, imag], axis=1)

    a11 = diagonal(0)
    a33 = diagonal(1)
    a22 = diagonal(2)
    a12 = block(2, slice(0, 16))
    a13 = block(1, slice(16, 32))
    a32 = block(2, slice(16, 32))
    p = hermitian_inverse(a11)
    v21 = cdot(adjoint(a12), p)
    v31 = cdot(adjoint(a13), p)
    s22 = a22 - cdot(v21, a12)
    s32 = a32 - cdot(v31, a12)
    s33 = a33 - cdot(v31, a13)
    q = hermitian_inverse(s22)
    v32 = cdot(s32, q)
    s33 = s33 - cdot(v32, adjoint(s32))
    r = hermitian_inverse(s33)
    t = steer_ref[...]
    y3 = cdot(t, r)
    y2 = -cdot(y3, v32)
    y1 = -cdot(y2, v21) - cdot(y3, v31)
    norm = lax.rsqrt(jnp.sum(t * y3, axis=1, keepdims=True))
    real = [(v[:, :64] * norm) for v in (y1, y3, y2)]
    imag = [(v[:, 64:] * -norm) for v in (y1, y3, y2)]
    rows = jnp.concatenate(
        [jnp.concatenate(real, axis=1), jnp.concatenate(imag, axis=1)], axis=0
    )
    zero = jnp.zeros((16, 64), F32)
    even = jnp.concatenate([rows, zero], axis=1)
    odd = jnp.concatenate([zero, rows], axis=1)
    return jnp.where(parity == 0, even, odd).astype(BF16)


def selection(bin_ref, block_ref, beam_ref, owner_ref, select, turn, back):
    s_iota = lax.broadcasted_iota(jnp.int32, (256, 128), 0)
    named = (s_iota // 2 == owner_ref[...]).astype(F32)
    before = (
        lax.broadcasted_iota(jnp.int32, (128, 128), 0)
        < lax.broadcasted_iota(jnp.int32, (128, 128), 1)
    ).astype(F32)
    earlier = jnp.dot(named.astype(BF16), before.astype(BF16), preferred_element_type=F32)
    pick = jnp.where(earlier == (s_iota % 2).astype(F32), named, 0.0).astype(BF16)
    wanted = block_ref[...] * 256 + bin_ref[...] * 8 + beam_ref[...]
    t_iota = lax.broadcasted_iota(jnp.int32, (512, 128), 0)
    holds = (t_iota == wanted).astype(F32).astype(BF16)
    select[...] = lax.dot_general(pick, holds, NT, preferred_element_type=F32).astype(BF16)
    o = lax.broadcasted_iota(jnp.int32, (256, 256), 0)
    i = lax.broadcasted_iota(jnp.int32, (256, 256), 1)
    turn[...] = (i == o % 32 // 2 * 16 + o // 32 * 2 + o % 2).astype(F32).astype(BF16)
    back[...] = (i == o % 16 // 2 * 32 + o // 16 * 2 + o % 2).astype(F32).astype(BF16)


def kernel(
    stop, few,
    raw_ref, rep_in, dft_in, steer_in, bin_in, block_in, beam_in, owner_in,
    out_ref,
    raw, pkl, pkr, hl, hr, ur, ui, tza, tz, s, pks, sr, p, r1, a1, rp, rm, a2, r3, gath, wall, table,
    select, turn, back, slots, d1, mid, d2,
    rep_ref, dft_ref, steer_ref, bin_ref, block_ref, beam_ref, owner_ref,
    ls, ms, hs, ht, s1, t1, s2, t2, s3, t3, s5, t5, s6, t6, s7, t7, s8, t8, s9, t9,
):
    me = lax.axis_index("range")
    core = me % 2
    y = me // 2 % 4
    x = me // 8 % 4
    z = me // 32
    zx = me // 8
    yc = me % 8
    bin_ = 2 * (4 * z + x + z % 2 * (3 - 2 * x)) + y // 2
    member = me % 4
    sib = me + 1 - 2 * core
    sa = 32 - 24 * core
    sb = 8 + 24 * core
    a = me // sa % 4
    b = me // sb % 4
    left = (me + 127) % 128
    right = (me + 1) % 128

    def along(stride, coord, j):
        return me + ((coord + j) % 4 - coord) * stride

    near = []
    for delta in (-1, 0, 1):
        for j in range(4):
            if delta or j:
                near.append((delta, j, home((bin_ + delta + 32) % 32) + (member + j) % 4))
    bins = [(bin_ + j) % 32 for j in range(1, 32)]
    planes = [(z + j // 4) % 4 * 4 + (x + j % 4) % 4 for j in range(1, 16)]
    froms = [(z + 4 - j // 4) % 4 * 4 + (x + 4 - j % 4) % 4 for j in range(1, 16)]
    posts = [(yc + j) % 8 for j in range(1, 8)]
    sheet = [
        ((b + j // 4) % 4, (y + j % 4) % 4)
        for j in (10, 9, 11, 6, 14, 2, 8, 5, 7, 13, 15, 1, 3, 4, 12)
    ]
    spots = [me + (q - b) * sb + (r - y) * 2 for q, r in sheet]
    partners = [left, right, sib, along(sa, a, 1), along(sa, a, 3)] + spots
    if not few:
        partners += [to for _, _, to in near] + [facing(q, bin_, member) for q in bins]
        partners += [q * 8 + yc for q in planes] + [zx * 8 + q for q in posts]

    small = [
        pltpu.make_async_copy(src, dst, ms.at[n])
        for n, (src, dst) in enumerate(
            [
                (rep_in, rep_ref), (dft_in, dft_ref), (steer_in, steer_ref), (bin_in, bin_ref),
                (block_in, block_ref), (beam_in, beam_ref), (owner_in, owner_ref),
            ]
        )
    ]
    small[0].start()
    loads = []
    for i in range(4):
        at = pl.ds(16 * i, 16)
        copy = pltpu.make_async_copy(raw_ref.at[:, at], raw.at[:, at], ls.at[i])
        copy.start()
        loads.append(copy)
    for copy in small[1:]:
        copy.start()
    barrier = pltpu.get_barrier_semaphore()
    for to in partners:
        pl.semaphore_signal(barrier, inc=1, device_id=(to,), device_id_type=MESH)
    for i in range(4):
        at = pl.ds(16 * i, 16)
        loads[i].wait()
        pkl[at] = jnp.concatenate([raw[0, at, :, 0:64], raw[1, at, :, 0:64]], axis=-1)
        pkr[at] = jnp.concatenate([raw[0, at, :, 192:256], raw[1, at, :, 192:256]], axis=-1)
        window_inner(at, raw, ur, ui)
    pl.semaphore_wait(barrier, len(partners))
    copies = []

    def finish():
        for copy in copies:
            copy.wait_send()

    if stop < 0:
        for copy in small:
            copy.wait()
        out_ref[...] = (pkl[0, :1, :1].astype(F32) + jnp.zeros((256, 256), F32)).astype(BF16)
        return finish()

    def to_left(i):
        at = pl.ds(16 * i, 16)
        return remote(pkl.at[at], hr.at[at], hs.at[0, i], ht.at[0, i], left)

    for i in range(4):
        at = pl.ds(16 * i, 16)
        copy = remote(pkr.at[at], hl.at[at], hs.at[1, i], ht.at[1, i], right)
        copy.start()
        copies.append(copy)

        @pl.when(me > 0)
        def _():
            to_left(i).start()

    @pl.when(me == 127)
    def _():
        hr[...] = jnp.zeros_like(hr)

    small[0].wait()
    build_toeplitz(rep_ref, jnp.where(me > 0, 1.0, 0.0).astype(F32), tza, tz)
    for copy in small[1:]:
        copy.wait()
    selection(bin_ref, block_ref, beam_ref, owner_ref, select, turn, back)
    for i in range(4):
        copies[i].wait_recv()

        @pl.when(me < 127)
        def _():
            to_left(i).wait_recv()

        window_edges(pl.ds(16 * i, 16), raw, hl, hr, ur, ui)
        spectra_part(i, ur, ui, dft_ref, s, tza, tz)

    @pl.when(me > 0)
    def _():
        for i in range(4):
            to_left(i).wait_send()

    s[0:2] = s[32:34]
    s[34] = s[2]
    pks[...] = join(s[2:34, :, 0:64], s[2:34, :, 128:192])
    share = remote(pks, sr.at[pl.ds(2, 32)], s9, t9, left)
    if stop < 1:
        out_ref[...] = (s[0, :1, :256].astype(F32) + jnp.zeros((256, 256), F32)).astype(BF16)
        return finish()

    order = (2, 1, 3, 0)
    oa = me // sb % 4
    for j in order:
        q = (oa + j) % 4
        for u in range(4):
            cross_products(core * q + (1 - core) * u, core * u + (1 - core) * q, s, p)
        at = pl.ds(q * 8, 8)
        copy = remote(p.at[1 - core, at], r1.at[at], s1.at[j], t1.at[j], sib)
        copy.start()
        copies.append(copy)
    if stop < 2:
        for j in order:
            at = pl.ds((a + j) % 4 * 8, 8)
            remote(p.at[core, at], r1.at[at], s1.at[j], t1.at[j], sib).wait_recv()
        out_ref[...] = (p[0, 0, :1, :1] + jnp.zeros((256, 256), F32)).astype(BF16)
        return finish()

    rings = []

    def ring(src, dst, n, to):
        copy = remote(src, dst, s2.at[n], t2.at[n], to)
        copy.start()
        copies.append(copy)
        rings.append(copy)

    ahead, behind = along(sa, a, 1), along(sa, a, 3)
    base = {j: (a + j) % 4 * 8 for j in range(4)}
    for j in order:
        at = pl.ds(base[j], 8)
        remote(p.at[core, at], r1.at[at], s1.at[j], t1.at[j], sib).wait_recv()
        a1[at] = p[core, at] + r1[at]
        if j == 2:
            ring(a1.at[pl.ds(base[2], 4)], rp.at[0], 0, ahead)
            ring(a1.at[pl.ds(base[2] + 4, 4)], rm.at[0], 1, behind)
        elif j == 1:
            ring(a1.at[pl.ds(base[1] + 4, 4)], rp.at[1], 2, ahead)
        elif j == 3:
            ring(a1.at[pl.ds(base[3], 4)], rm.at[1], 3, behind)
    rings[0].wait_recv()
    at = pl.ds(base[1], 4)
    a1[at] = a1[at] + rp[0]
    ring(a1.at[at], rp.at[2], 4, ahead)
    rings[1].wait_recv()
    at = pl.ds(base[3] + 4, 4)
    a1[at] = a1[at] + rm[0]
    ring(a1.at[at], rm.at[2], 5, behind)
    for n in (2, 3):
        rings[n].wait_recv()
    at = pl.ds(base[0] + 4, 4)
    a2[4:8] = a1[at] + rp[1]
    at = pl.ds(base[0], 4)
    a2[0:4] = a1[at] + rm[1]
    rings[4].wait_recv()
    a2[0:4] = a2[0:4] + rp[2]
    rings[5].wait_recv()
    a2[4:8] = a2[4:8] + rm[2]
    if stop < 3:
        out_ref[...] = (a2[0, :1, :1] + jnp.zeros((256, 256), F32)).astype(BF16)
        return finish()

    for n, (q, r) in enumerate(sheet):
        src = a2.at[q * 2 + r // 2, pl.ds(pl.multiple_of(r % 2 * 40, 8), 40)]
        copy = remote(src, r3.at[n], s3.at[n], t3.at[n], spots[n])
        copy.start()
        copies.append(copy)
    for n in range(15):
        remote(r3.at[n], r3.at[n], s3.at[n], t3.at[n], sib).wait_recv()
    mine = a2[b * 2 + y // 2, pl.ds(pl.multiple_of(y % 2 * 40, 8), 40)]
    terms = [mine] + [r3[n] for n in range(15)]
    while len(terms) > 1:
        terms = [u + v for u, v in zip(terms[::2], terms[1::2])]
    gath[1, member] = terms[0]
    if stop < 4:
        out_ref[...] = (terms[0][:1, :1] + jnp.zeros((256, 256), F32)).astype(BF16)
        return finish()
    needs = {-1: pl.ds(0, 40), 0: pl.ds(16, 24), 1: pl.ds(32, 8)}
    for n, (delta, j, to) in enumerate(near):
        rows = needs[delta]
        copy = remote(
            gath.at[1, member, rows], gath.at[1 - delta, member, rows], s5.at[n],
            t5.at[1 - delta, member], to,
        )
        copy.start()
        copies.append(copy)
    for delta, j, _ in near:
        rows = needs[delta]
        m = (member + j) % 4
        remote(
            gath.at[1, member, rows], gath.at[1 - delta, m, rows], s5.at[0],
            t5.at[1 - delta, m], sib,
        ).wait_recv()
    if stop < 5:
        out_ref[...] = (gath[2, 0, :1, :1] + jnp.zeros((256, 256), F32)).astype(BF16)
        return finish()

    share.start()
    copies.append(share)
    wall[bin_] = solve(gath, steer_ref, bin_ % 2)
    share.wait_recv()
    sr[0:2] = sr[32:34]
    sr[34] = sr[2]
    if stop < 6:
        out_ref[...] = (wall[bin_, :1].astype(F32) + jnp.zeros((256, 256), F32)).astype(BF16)
        return finish()
    for n, to in enumerate(bins):
        copy = remote(wall.at[bin_], wall.at[bin_], s6.at[n], t6.at[bin_], facing(to, bin_, member))
        copy.start()
        copies.append(copy)

    for n in range(16):
        duo = (bin_ // 2 + 16 - n) % 16
        first = duo * 2
        waits = (first, first + 1) if n else (bin_ + 1 - 2 * (bin_ % 2),)
        for q in waits:
            remote(wall.at[q], wall.at[q], s6.at[0], t6.at[q], sib).wait_recv()
        beam_pair(first, wall, s, sr, table)
    if stop < 7:
        out_ref[...] = (table[0:256].astype(F32)).astype(BF16)
        return finish()

    slots[...] = (
        jnp.dot(select[...], table[...], preferred_element_type=F32)
        .astype(BF16)
        .reshape(16, 16, 256)
    )
    for j, q in enumerate(planes):
        copy = remote(slots.at[q], d1.at[zx], s7.at[j], t7.at[j], q * 8 + yc)
        copy.start()
        copies.append(copy)
    d1[zx] = slots[zx]
    for j, q in enumerate(froms):
        remote(slots.at[q], d1.at[q], s7.at[j], t7.at[j], sib).wait_recv()
    mid[...] = (
        jnp.dot(turn[...], d1[...].reshape(256, 256), preferred_element_type=F32)
        .astype(BF16)
        .reshape(8, 32, 256)
    )
    if stop < 8:
        out_ref[...] = (mid[...].reshape(256, 256).astype(F32)).astype(BF16)
        return finish()
    for j, q in enumerate(posts):
        copy = remote(mid.at[q], d2.at[yc], s8.at[j], t8.at[j], zx * 8 + q)
        copy.start()
        copies.append(copy)
    d2[yc] = mid[yc]
    for j in range(7):
        q = (yc + 7 - j) % 8
        remote(mid.at[q], d2.at[q], s8.at[j], t8.at[j], sib).wait_recv()
    rows = jnp.dot(back[...], d2[...].reshape(256, 256), preferred_element_type=F32)
    out_ref[...] = rows.astype(BF16)
    finish()


def program(raw, replica, det_bin, det_block, det_beam, owner, stop, few):
    dma = pltpu.SemaphoreType.DMA
    vm = pltpu.VMEM
    rows = (1, 128)
    return pl.pallas_call(
        functools.partial(kernel, stop, few),
        out_shape=jax.ShapeDtypeStruct((256, 256), BF16),
        in_specs=[HBM] * 8,
        out_specs=VMEM,
        scratch_shapes=[
            vm((2, 64, 32, 256), BF16),
            vm((64, 32, 128), BF16),
            vm((64, 32, 128), BF16),
            vm((64, 32, 128), BF16),
            vm((64, 32, 128), BF16),
            vm((64, 32, 384), BF16),
            vm((64, 32, 384), BF16),
            vm((512, 256), BF16),
            vm((512, 256), BF16),
            vm((35, 64, 512), BF16),
            vm((32, 64, 128), BF16),
            vm((35, 64, 128), BF16),
            vm((2, 32, 80, 128), F32),
            vm((32, 80, 128), F32),
            vm((32, 80, 128), F32),
            vm((3, 4, 80, 128), F32),
            vm((3, 4, 80, 128), F32),
            vm((8, 80, 128), F32),
            vm((15, 40, 128), F32),
            vm((3, 4, 40, 128), F32),
            vm((32, 16, 256), BF16),
            vm((512, 256), BF16),
            vm((256, 512), BF16),
            vm((256, 256), BF16),
            vm((256, 256), BF16),
            vm((16, 16, 256), BF16),
            vm((16, 16, 256), BF16),
            vm((8, 32, 256), BF16),
            vm((8, 32, 256), BF16),
            vm((2, 128), BF16),
            vm((512, 512), BF16),
            vm((8, 128), F32),
            vm(rows, jnp.int32), vm(rows, jnp.int32), vm(rows, jnp.int32), vm(rows, jnp.int32),
            dma((4,)), dma((7,)), dma((2, 4)), dma((2, 4)),
            dma((4,)), dma((4,)), dma((6,)), dma((6,)), dma((15,)), dma((15,)),
            dma((11,)), dma((3, 4)), dma((31,)), dma((32,)),
            dma((15,)), dma((15,)), dma((7,)), dma((7,)), dma(()), dma(()),
        ],
        compiler_params=pltpu.CompilerParams(
            collective_id=0, has_side_effects=True, vmem_limit_bytes=LIMIT
        ),
        name="stap",
    )(
        raw, replica, jnp.asarray(dft_matrix()), jnp.asarray(steer_rows()),
        det_bin, det_block, det_beam, owner,
    )


def on_device(stop, few, raw, replica, det_bin, det_block, det_beam, det_owner):
    rows = [v.reshape(1, 128) for v in (det_bin, det_block, det_beam, det_owner)]
    return program(raw, replica, *rows, stop=stop, few=few).astype(F32)


def solution(mesh, stop=9, few=True):
    in_specs = (
        P(None, None, None, "range"),
        P(),
        P("range"),
        P("range"),
        P("range"),
        P("range", None),
    )
    return jax.shard_map(
        functools.partial(on_device, stop, few),
        mesh=mesh,
        in_specs=in_specs,
        out_specs=P("range", None),
        check_vma=False,
    )
```

```python
import functools
import math

import jax
import jax.numpy as jnp
import numpy as np
from jax import lax
from jax.experimental import pallas as pl
from jax.experimental.pallas import tpu as pltpu
from jax.sharding import PartitionSpec as P

C = 64
PULSES = 32
TAPS = 128
BEAMS = 8
F32 = jnp.float32
BF16 = jnp.bfloat16
MESH = pl.DeviceIdType.MESH
VMEM = pl.BlockSpec(memory_space=pltpu.VMEM)
HBM = pl.BlockSpec(memory_space=pltpu.HBM)
NT = (((1,), (1,)), ((), ()))
LIMIT = 63 * 1024 * 1024
FAR = (10, 9, 11, 6, 14, 2, 8, 5, 7, 13, 15, 1, 3, 4, 12)
POSTS = (4, 5, 3, 2, 6, 7, 1)


def dft_matrix():
    index = np.arange(PULSES)
    angle = 2.0 * math.pi / PULSES * (index[:, None] * index[None, :] % PULSES)
    scale = PULSES**-0.5
    real = np.cos(angle) * scale
    imag = -np.sin(angle) * scale
    eye = np.eye(8)
    kr = np.einsum("pd,ab->dabp", real, eye).reshape(256, 256)
    ki = np.einsum("pd,ab->dabp", imag, eye).reshape(256, 256)
    full = np.concatenate([np.concatenate([kr, -ki], 1), np.concatenate([ki, kr], 1)], 0)
    return full.astype(jnp.bfloat16)


def steer_rows():
    sines = -0.8 + 1.6 * np.arange(BEAMS, dtype=np.float32) / np.float32(BEAMS - 1)
    angle = (math.pi * np.arange(C, dtype=np.float32)[None, :] * sines[:, None]).astype(np.float32)
    return np.concatenate([np.cos(angle), -np.sin(angle)], 1).astype(np.float32)


def remote(src, dst, send, recv, to):
    return pltpu.make_async_remote_copy(
        src_ref=src, dst_ref=dst, send_sem=send, recv_sem=recv, device_id=(to,), device_id_type=MESH
    )


def build_toeplitz(rep_ref, keep, tza, tz):
    def band(v):
        wide = jnp.concatenate(
            [jnp.broadcast_to(v, (TAPS, TAPS)), jnp.zeros((TAPS, TAPS), F32)], axis=1
        )
        return pltpu.roll(wide, 0, 1, stride=1, stride_axis=0).T

    rep = rep_ref[...].astype(F32)
    tr = band(rep[0:1])
    ti = band(rep[1:2])
    full = jnp.concatenate(
        [jnp.concatenate([tr, -ti], axis=1), jnp.concatenate([ti, tr], axis=1)], axis=0
    )
    tz[...] = full.astype(BF16)
    row = lax.broadcasted_iota(jnp.int32, (512, 256), 0) % 256
    lane = lax.broadcasted_iota(jnp.int32, (512, 256), 1) % 128
    tza[...] = jnp.where((row >= 64) & (lane < 64), full * keep, full).astype(BF16)


def join(*parts):
    return jnp.concatenate(parts, axis=-1)


def window_inner(at, raw, ur, ui):
    for n, u in enumerate((ur, ui)):
        u[at, :, 128:256] = join(raw[n, at, :, 64:128], raw[n, at, :, 128:192])


def window_edges(at, raw, hl, hr, ur, ui):
    for n, u in enumerate((ur, ui)):
        lanes = slice(64 * n, 64 * n + 64)
        u[at, :, 0:128] = join(hl[at, :, lanes], raw[n, at, :, 0:64])
        u[at, :, 256:384] = join(raw[n, at, :, 192:256], hr[at, :, lanes])


def spectra_part(i, ur, ui, dft_ref, s, tza, tz):
    first = 16 * i
    for b in range(2):
        ys = []
        for n in range(2):
            at = pl.ds(first + 8 * n, 8)
            gates = slice(128 * b, 128 * b + 256)
            window = join(ur[at, :, gates].reshape(256, 256), ui[at, :, gates].reshape(256, 256))
            band = tz[...] if b else tza[...]
            ys.append(jnp.dot(window, band, preferred_element_type=F32).astype(BF16))
        ya, yb = ys
        y = jnp.concatenate(
            [join(ya[:, :128], yb[:, :128]), join(ya[:, 128:], yb[:, 128:])], axis=0
        )
        out = jnp.dot(dft_ref[...], y, preferred_element_type=F32)
        for p in range(2):
            h = out[256 * p : 256 * p + 256]
            v = jnp.concatenate(
                [h[:, :128].reshape(32, 8, 128), h[:, 128:].reshape(32, 8, 128)], axis=1
            )
            lanes = 256 * b + 128 * p
            s[2:34, first : first + 16, lanes : lanes + 128] = v.astype(BF16)


def snake(k):
    z = k // 4
    x = k % 4
    return z, x + z % 2 * (3 - 2 * x)


def home(q):
    z, x = snake(q // 2)
    return z * 32 + x * 8 + q % 2 * 2


def at_home(q, member):
    return home(q) + member // 2 * 4 + member % 2


def beam_pair(first, wall, s, sr, table):
    lhs = wall[pl.ds(first, 2)].reshape(32, 256)
    rhs = join(
        s[pl.ds(first + 1, 4)].reshape(256, 512), sr[pl.ds(first + 1, 4)].reshape(256, 128)
    )
    prod = jnp.dot(lhs, rhs, preferred_element_type=F32)
    top = jnp.concatenate([prod[0:8], prod[16:24]], axis=0)
    low = jnp.concatenate([prod[8:16], prod[24:32]], axis=0)
    half = lax.broadcasted_iota(jnp.int32, (16, 128), 1) < 64

    def flip(v):
        return pltpu.roll(v, 64, 1)

    parts = []
    for at in (0, 256):
        parts.append(flip(top[:, at : at + 128] + low[:, at + 128 : at + 256]))
        parts.append(flip(top[:, at + 128 : at + 256] - low[:, at : at + 128]))
    turn = flip(low[:, 512:])
    last = top[:, 512:] + jnp.where(half, turn, -turn)
    lanes = [
        jnp.where(half, parts[0], parts[2]),
        jnp.where(half, parts[1], parts[3]),
        jnp.where(half, parts[2], flip(last)),
        jnp.where(half, parts[3], last),
    ]
    for i in range(2):
        rows = pl.ds(pl.multiple_of(256 * i + first * 8, 16), 16)
        table[rows] = join(*lanes[2 * i : 2 * i + 2]).astype(BF16)


def store_products(p, places, two, one, zero):
    lane = lax.broadcasted_iota(jnp.int32, (32, 128), 1)
    row = lax.broadcasted_iota(jnp.int32, (32, 128), 0)
    swapped = pltpu.roll(zero, 64, 1)
    top = jnp.where(row >= lane, zero[:32], swapped[:32])
    bottom = jnp.where(row + 32 >= lane - 64, swapped[32:], zero[32:])
    packed = jnp.where(lane < 64, top, bottom)
    for h in range(2):
        pos = places[h]
        for q in range(2):
            a = 32 * h + 16 * q
            p[h, pos, 40 * q : 40 * q + 16] = two[a : a + 16]
            p[h, pos, 40 * q + 16 : 40 * q + 32] = one[a : a + 16]
            p[h, pos, 40 * q + 32 : 40 * q + 40] = packed[a // 2 : a // 2 + 8]


def cross_products(z, x, s, p):
    f = 2 * (4 * z + x + z % 2 * (3 - 2 * x))
    lhs = s[pl.ds(f, 4)].reshape(256, 512)
    rhs = []
    for n in range(2):
        v = s[f + 2 + n]
        rhs += [v, join(-v[:, 128:256], v[:, :128], -v[:, 384:], v[:, 256:384])]
    prod = lax.dot_general(lhs, jnp.concatenate(rhs, axis=0), NT, preferred_element_type=F32)
    first, second = (z * 8 + x * 2, x * 8 + z * 2), (z * 8 + x * 2 + 1, x * 8 + z * 2 + 1)
    store_products(p, first, prod[:64, :128], prod[64:128, :128], prod[128:192, :128])
    store_products(p, second, prod[64:128, 128:], prod[128:192, 128:], prod[192:, 128:])


def times_i(m):
    return jnp.concatenate([-m[:, 64:], m[:, :64]], axis=1)


def cdot(x, y):
    return jnp.dot(
        x, jnp.concatenate([y, times_i(y)], axis=0),
        preferred_element_type=F32, precision=lax.Precision.HIGHEST,
    )


def adjoint(m):
    t = m.T
    return jnp.concatenate([t[:64], -t[64:]], axis=1)


def lane_of(v, k):
    return jnp.broadcast_to(v[:, k : k + 1], (8, 128))


def row_of(v, r):
    return jnp.broadcast_to(v[r : r + 1], (8, 128))


def cmul(x, y):
    return (x[0] * y[0] - x[1] * y[1], x[0] * y[1] + x[1] * y[0])


def cmulc(x, y):
    return (x[0] * y[0] + x[1] * y[1], x[1] * y[0] - x[0] * y[1])


def cadd(x, y):
    return (x[0] + y[0], x[1] + y[1])


def csub(x, y):
    return (x[0] - y[0], x[1] - y[1])


def cscale(x, c):
    return (x * c[0], x * c[1])


def conj(x):
    return (x[0], -x[1])


def size2(x):
    return x[0] * x[0] + x[1] * x[1]


def rdot(x, y):
    return x[0] * y[0] + x[1] * y[1]


def cm(c, row):
    v, w = row
    return (c[0] * v + c[1] * w, c[0] * w - c[1] * v)


def hermitian_inverse(m):
    lane = lax.broadcasted_iota(jnp.int32, (8, 128), 1)
    sub = lax.broadcasted_iota(jnp.int32, (8, 128), 0)
    ms = [m[8 * t : 8 * t + 8] for t in range(8)]
    for k in range(0, 64, 4):
        t0, r0 = divmod(k, 8)
        w = ms[t0]
        wi = times_i(w)
        cr = [[lane_of(v, k + j) for v in ms] for j in range(4)]
        ci = [[lane_of(v, 64 + k + j) for v in ms] for j in range(4)]

        def entry(i, j):
            return (row_of(cr[j][t0], r0 + i), row_of(ci[j][t0], r0 + i))

        a, d, b = entry(0, 0)[0], entry(1, 1)[0], entry(0, 1)
        p, s, q = entry(2, 2)[0], entry(3, 3)[0], entry(2, 3)
        bb = [[entry(0, 2), entry(0, 3)], [entry(1, 2), entry(1, 3)]]
        det = 1.0 / (a * d - size2(b))
        ia, id_, ib = d * det, a * det, cscale(-det, b)
        ww = [
            [cadd(cscale(ia, bb[0][j]), cmul(ib, bb[1][j])) for j in range(2)],
            [cadd(cmul(conj(ib), bb[0][j]), cscale(id_, bb[1][j])) for j in range(2)],
        ]
        s00 = p - (rdot(bb[0][0], ww[0][0]) + rdot(bb[1][0], ww[1][0]))
        s11 = s - (rdot(bb[0][1], ww[0][1]) + rdot(bb[1][1], ww[1][1]))
        s01 = csub(q, cadd(cmulc(ww[0][1], bb[0][0]), cmulc(ww[1][1], bb[1][0])))
        dets = 1.0 / (s00 * s11 - size2(s01))
        j00, j11, j01 = s11 * dets, s00 * dets, cscale(-dets, s01)
        hit = ((lane >= k) & (lane < k + 4)) | ((lane >= 64 + k) & (lane < 68 + k))
        rows = []
        for j in range(4):
            real = jnp.where(hit, jnp.where(lane == k + j, 1.0, 0.0), row_of(w, r0 + j))
            imag = jnp.where(hit, jnp.where(lane == 64 + k + j, 1.0, 0.0), row_of(wi, r0 + j))
            rows.append((real, imag))
        t2 = csub(rows[2], cadd(cm(conj(ww[0][0]), rows[0]), cm(conj(ww[1][0]), rows[1])))
        t3 = csub(rows[3], cadd(cm(conj(ww[0][1]), rows[0]), cm(conj(ww[1][1]), rows[1])))
        x2 = cadd(cscale(j00, t2), cm(j01, t3))
        x3 = cadd(cscale(j11, t3), cm(conj(j01), t2))
        u0 = cadd(cscale(ia, rows[0]), cm(ib, rows[1]))
        u1 = cadd(cscale(id_, rows[1]), cm(conj(ib), rows[0]))
        x0 = csub(u0, cadd(cm(ww[0][0], x2), cm(ww[0][1], x3)))
        x1 = csub(u1, cadd(cm(ww[1][0], x2), cm(ww[1][1], x3)))
        g = [x0, x1, x2, x3]
        for t in range(8):
            terms = [cr[j][t] * g[j][0] + ci[j][t] * g[j][1] for j in range(4)]
            mt = jnp.where(hit, 0.0, ms[t]) - ((terms[0] + terms[1]) + (terms[2] + terms[3]))
            if t == t0:
                for j in range(4):
                    mt = jnp.where(sub == r0 + j, g[j][0], mt)
            ms[t] = mt
    return jnp.concatenate(ms, axis=0)


def solve(g_ref, steer_ref, parity):
    scale = 1.0 / 32768.0
    order = (0, 2, 1, 3)
    r64 = lax.broadcasted_iota(jnp.int32, (64, 64), 0)
    c64 = lax.broadcasted_iota(jnp.int32, (64, 64), 1)

    def block(g, rows):
        return jnp.concatenate([g_ref[g, m, rows] for m in order], axis=0) * scale

    def diagonal(g):
        pk = block(g, slice(32, 40))
        k = jnp.concatenate([pk[:, :64], pk[:, 64:]], axis=0)
        kt = k.T
        real = jnp.where(r64 >= c64, k, kt)
        imag = jnp.where(r64 < c64, k, jnp.where(r64 == c64, 0.0, -kt))
        return jnp.concatenate([real, imag], axis=1)

    a11 = diagonal(0)
    a33 = diagonal(1)
    a22 = diagonal(2)
    a12 = block(2, slice(0, 16))
    a13 = block(1, slice(16, 32))
    a32 = block(2, slice(16, 32))
    p = hermitian_inverse(a11)
    v21 = cdot(adjoint(a12), p)
    v31 = cdot(adjoint(a13), p)
    s22 = a22 - cdot(v21, a12)
    s32 = a32 - cdot(v31, a12)
    s33 = a33 - cdot(v31, a13)
    q = hermitian_inverse(s22)
    v32 = cdot(s32, q)
    s33 = s33 - cdot(v32, adjoint(s32))
    r = hermitian_inverse(s33)
    t = steer_ref[...]
    y3 = cdot(t, r)
    y2 = -cdot(y3, v32)
    y1 = -cdot(y2, v21) - cdot(y3, v31)
    norm = lax.rsqrt(jnp.sum(t * y3, axis=1, keepdims=True))
    real = [(v[:, :64] * norm) for v in (y1, y3, y2)]
    imag = [(v[:, 64:] * -norm) for v in (y1, y3, y2)]
    rows = jnp.concatenate(
        [jnp.concatenate(real, axis=1), jnp.concatenate(imag, axis=1)], axis=0
    )
    zero = jnp.zeros((16, 64), F32)
    even = jnp.concatenate([rows, zero], axis=1)
    odd = jnp.concatenate([zero, rows], axis=1)
    return jnp.where(parity == 0, even, odd).astype(BF16)


def selection(bin_ref, block_ref, beam_ref, owner_ref, select, turn, back):
    s_iota = lax.broadcasted_iota(jnp.int32, (256, 128), 0)
    named = (s_iota // 2 == owner_ref[...]).astype(F32)
    before = (
        lax.broadcasted_iota(jnp.int32, (128, 128), 0)
        < lax.broadcasted_iota(jnp.int32, (128, 128), 1)
    ).astype(F32)
    earlier = jnp.dot(named.astype(BF16), before.astype(BF16), preferred_element_type=F32)
    pick = jnp.where(earlier == (s_iota % 2).astype(F32), named, 0.0).astype(BF16)
    wanted = block_ref[...] * 256 + bin_ref[...] * 8 + beam_ref[...]
    t_iota = lax.broadcasted_iota(jnp.int32, (512, 128), 0)
    holds = (t_iota == wanted).astype(F32).astype(BF16)
    select[...] = lax.dot_general(pick, holds, NT, preferred_element_type=F32).astype(BF16)
    o = lax.broadcasted_iota(jnp.int32, (256, 256), 0)
    i = lax.broadcasted_iota(jnp.int32, (256, 256), 1)
    turn[...] = (i == o % 32 // 2 * 16 + o // 32 * 2 + o % 2).astype(F32).astype(BF16)
    back[...] = (i == o % 16 // 2 * 32 + o // 16 * 2 + o % 2).astype(F32).astype(BF16)


def kernel(
    stop, few,
    raw_ref, rep_in, dft_in, steer_in, bin_in, block_in, beam_in, owner_in,
    out_ref,
    raw, pkl, pkr, hl, hr, ur, ui, tza, tz, s, pks, sr, p, r1, a1, rp, rm, a2, r3, gath, wall, table,
    select, turn, back, slots, d1, mid, d2,
    rep_ref, dft_ref, steer_ref, bin_ref, block_ref, beam_ref, owner_ref,
    ls, ms, hs, ht, s1, t1, s2, t2, s3, t3, s5, t5, s6, t6, s7, t7, s8, t8, s9, t9,
):
    me = lax.axis_index("range")
    core = me % 2
    y = me // 2 % 4
    x = me // 8 % 4
    z = me // 32
    zx = me // 8
    yc = me % 8
    bin_ = 2 * (4 * z + x + z % 2 * (3 - 2 * x)) + y % 2
    member = y // 2 * 2 + core
    sib = me + 1 - 2 * core
    sa = 32 - 24 * core
    sb = 8 + 24 * core
    a = me // sa % 4
    b = me // sb % 4
    left = (me + 127) % 128
    right = (me + 1) % 128

    def along(stride, coord, j):
        return me + ((coord + j) % 4 - coord) * stride

    near = []
    for delta in (-1, 0, 1):
        for j in range(4):
            if delta or j:
                near.append((delta, j, at_home((bin_ + delta + 32) % 32, (member + j) % 4)))
    bins = [(bin_ + j) % 32 for j in sorted(range(1, 32), key=lambda j: abs(j - 16))]
    planes = [(z + j // 4) % 4 * 4 + (x + j % 4) % 4 for j in FAR]
    froms = [(z + 4 - j // 4) % 4 * 4 + (x + 4 - j % 4) % 4 for j in FAR]
    posts = [(yc + j) % 8 for j in POSTS]
    sheet = [
        ((b + j // 4) % 4, (y + j % 4) % 4)
        for j in FAR
    ]
    spots = [me + (q - b) * sb + (r - y) * 2 for q, r in sheet]
    partners = [left, right, sib, along(sa, a, 1), along(sa, a, 3)] + spots
    if not few:
        partners += [to for _, _, to in near] + [at_home(q, member) for q in bins]
        partners += [q * 8 + yc for q in planes] + [zx * 8 + q for q in posts]

    small = [
        pltpu.make_async_copy(src, dst, ms.at[n])
        for n, (src, dst) in enumerate(
            [
                (rep_in, rep_ref), (dft_in, dft_ref), (steer_in, steer_ref), (bin_in, bin_ref),
                (block_in, block_ref), (beam_in, beam_ref), (owner_in, owner_ref),
            ]
        )
    ]
    small[0].start()
    loads = []
    for i in range(4):
        at = pl.ds(16 * i, 16)
        copy = pltpu.make_async_copy(raw_ref.at[:, at], raw.at[:, at], ls.at[i])
        copy.start()
        loads.append(copy)
    for copy in small[1:]:
        copy.start()
    barrier = pltpu.get_barrier_semaphore()
    for to in partners:
        pl.semaphore_signal(barrier, inc=1, device_id=(to,), device_id_type=MESH)
    for i in range(4):
        at = pl.ds(16 * i, 16)
        loads[i].wait()
        pkl[at] = jnp.concatenate([raw[0, at, :, 0:64], raw[1, at, :, 0:64]], axis=-1)
        pkr[at] = jnp.concatenate([raw[0, at, :, 192:256], raw[1, at, :, 192:256]], axis=-1)
        window_inner(at, raw, ur, ui)
    pl.semaphore_wait(barrier, len(partners))
    copies = []

    def finish():
        for copy in copies:
            copy.wait_send()

    if stop < 0:
        for copy in small:
            copy.wait()
        out_ref[...] = (pkl[0, :1, :1].astype(F32) + jnp.zeros((256, 256), F32)).astype(BF16)
        return finish()

    def to_left(i):
        at = pl.ds(16 * i, 16)
        return remote(pkl.at[at], hr.at[at], hs.at[0, i], ht.at[0, i], left)

    for i in range(4):
        at = pl.ds(16 * i, 16)
        copy = remote(pkr.at[at], hl.at[at], hs.at[1, i], ht.at[1, i], right)
        copy.start()
        copies.append(copy)

        @pl.when(me > 0)
        def _():
            to_left(i).start()

    @pl.when(me == 127)
    def _():
        hr[...] = jnp.zeros_like(hr)

    small[0].wait()
    build_toeplitz(rep_ref, jnp.where(me > 0, 1.0, 0.0).astype(F32), tza, tz)
    for copy in small[1:]:
        copy.wait()
    selection(bin_ref, block_ref, beam_ref, owner_ref, select, turn, back)
    for i in range(4):
        copies[i].wait_recv()

        @pl.when(me < 127)
        def _():
            to_left(i).wait_recv()

        window_edges(pl.ds(16 * i, 16), raw, hl, hr, ur, ui)
        spectra_part(i, ur, ui, dft_ref, s, tza, tz)

    @pl.when(me > 0)
    def _():
        for i in range(4):
            to_left(i).wait_send()

    s[0:2] = s[32:34]
    s[34] = s[2]
    pks[...] = join(s[2:34, :, 0:64], s[2:34, :, 128:192])
    share = remote(pks, sr.at[pl.ds(2, 32)], s9, t9, left)
    if stop < 1:
        out_ref[...] = (s[0, :1, :256].astype(F32) + jnp.zeros((256, 256), F32)).astype(BF16)
        return finish()

    order = (2, 1, 3, 0)
    oa = me // sb % 4
    for j in order:
        q = (oa + j) % 4
        for u in range(4):
            cross_products(core * q + (1 - core) * u, core * u + (1 - core) * q, s, p)
        at = pl.ds(q * 8, 8)
        copy = remote(p.at[1 - core, at], r1.at[at], s1.at[j], t1.at[j], sib)
        copy.start()
        copies.append(copy)
    if stop < 2:
        for j in order:
            at = pl.ds((a + j) % 4 * 8, 8)
            remote(p.at[core, at], r1.at[at], s1.at[j], t1.at[j], sib).wait_recv()
        out_ref[...] = (p[0, 0, :1, :1] + jnp.zeros((256, 256), F32)).astype(BF16)
        return finish()

    rings = []

    def ring(src, dst, n, to):
        copy = remote(src, dst, s2.at[n], t2.at[n], to)
        copy.start()
        copies.append(copy)
        rings.append(copy)

    ahead, behind = along(sa, a, 1), along(sa, a, 3)
    base = {j: (a + j) % 4 * 8 for j in range(4)}
    for j in order:
        at = pl.ds(base[j], 8)
        remote(p.at[core, at], r1.at[at], s1.at[j], t1.at[j], sib).wait_recv()
        a1[at] = p[core, at] + r1[at]
        if j == 2:
            ring(a1.at[pl.ds(base[2], 4)], rp.at[0], 0, ahead)
            ring(a1.at[pl.ds(base[2] + 4, 4)], rm.at[0], 1, behind)
        elif j == 1:
            ring(a1.at[pl.ds(base[1] + 4, 4)], rp.at[1], 2, ahead)
        elif j == 3:
            ring(a1.at[pl.ds(base[3], 4)], rm.at[1], 3, behind)
    rings[0].wait_recv()
    at = pl.ds(base[1], 4)
    a1[at] = a1[at] + rp[0]
    ring(a1.at[at], rp.at[2], 4, ahead)
    rings[1].wait_recv()
    at = pl.ds(base[3] + 4, 4)
    a1[at] = a1[at] + rm[0]
    ring(a1.at[at], rm.at[2], 5, behind)
    for n in (2, 3):
        rings[n].wait_recv()
    at = pl.ds(base[0] + 4, 4)
    a2[4:8] = a1[at] + rp[1]
    at = pl.ds(base[0], 4)
    a2[0:4] = a1[at] + rm[1]
    rings[4].wait_recv()
    a2[0:4] = a2[0:4] + rp[2]
    rings[5].wait_recv()
    a2[4:8] = a2[4:8] + rm[2]
    if stop < 3:
        out_ref[...] = (a2[0, :1, :1] + jnp.zeros((256, 256), F32)).astype(BF16)
        return finish()

    for n, (q, r) in enumerate(sheet):
        src = a2.at[q * 2 + r % 2, pl.ds(pl.multiple_of(r // 2 * 40, 8), 40)]
        copy = remote(src, r3.at[n], s3.at[n], t3.at[n], spots[n])
        copy.start()
        copies.append(copy)
    for n in range(15):
        remote(r3.at[n], r3.at[n], s3.at[n], t3.at[n], sib).wait_recv()
    mine = a2[b * 2 + y % 2, pl.ds(pl.multiple_of(y // 2 * 40, 8), 40)]
    terms = [mine] + [r3[n] for n in range(15)]
    while len(terms) > 1:
        terms = [u + v for u, v in zip(terms[::2], terms[1::2])]
    gath[1, member] = terms[0]
    if stop < 4:
        out_ref[...] = (terms[0][:1, :1] + jnp.zeros((256, 256), F32)).astype(BF16)
        return finish()
    needs = {-1: pl.ds(0, 40), 0: pl.ds(16, 24), 1: pl.ds(32, 8)}
    for n, (delta, j, to) in enumerate(near):
        rows = needs[delta]
        copy = remote(
            gath.at[1, member, rows], gath.at[1 - delta, member, rows], s5.at[n],
            t5.at[1 - delta, member], to,
        )
        copy.start()
        copies.append(copy)
    for delta, j, _ in near:
        rows = needs[delta]
        m = (member + j) % 4
        remote(
            gath.at[1, member, rows], gath.at[1 - delta, m, rows], s5.at[0],
            t5.at[1 - delta, m], sib,
        ).wait_recv()
    if stop < 5:
        out_ref[...] = (gath[2, 0, :1, :1] + jnp.zeros((256, 256), F32)).astype(BF16)
        return finish()

    share.start()
    copies.append(share)
    wall[bin_] = solve(gath, steer_ref, bin_ % 2)
    share.wait_recv()
    sr[0:2] = sr[32:34]
    sr[34] = sr[2]
    if stop < 6:
        out_ref[...] = (wall[bin_, :1].astype(F32) + jnp.zeros((256, 256), F32)).astype(BF16)
        return finish()
    for n, to in enumerate(bins):
        copy = remote(wall.at[bin_], wall.at[bin_], s6.at[n], t6.at[bin_], at_home(to, member))
        copy.start()
        copies.append(copy)

    for n in (0, 1, 15, 2, 14, 3, 13, 4, 12, 5, 11, 6, 10, 7, 9, 8):
        duo = (bin_ // 2 + 16 - n) % 16
        first = duo * 2
        waits = (first, first + 1) if n else (bin_ + 1 - 2 * (bin_ % 2),)
        for q in waits:
            remote(wall.at[q], wall.at[q], s6.at[0], t6.at[q], sib).wait_recv()
        beam_pair(first, wall, s, sr, table)
    if stop < 7:
        out_ref[...] = (table[0:256].astype(F32)).astype(BF16)
        return finish()

    slots[...] = (
        jnp.dot(select[...], table[...], preferred_element_type=F32)
        .astype(BF16)
        .reshape(16, 16, 256)
    )
    for j, q in enumerate(planes):
        copy = remote(slots.at[q], d1.at[zx], s7.at[j], t7.at[j], q * 8 + yc)
        copy.start()
        copies.append(copy)
    d1[zx] = slots[zx]
    for j, q in enumerate(froms):
        remote(slots.at[q], d1.at[q], s7.at[j], t7.at[j], sib).wait_recv()
    mid[...] = (
        jnp.dot(turn[...], d1[...].reshape(256, 256), preferred_element_type=F32)
        .astype(BF16)
        .reshape(8, 32, 256)
    )
    if stop < 8:
        out_ref[...] = (mid[...].reshape(256, 256).astype(F32)).astype(BF16)
        return finish()
    for j, q in enumerate(posts):
        copy = remote(mid.at[q], d2.at[yc], s8.at[j], t8.at[j], zx * 8 + q)
        copy.start()
        copies.append(copy)
    d2[yc] = mid[yc]
    for j, step in enumerate(POSTS):
        q = (yc + 8 - step) % 8
        remote(mid.at[q], d2.at[q], s8.at[j], t8.at[j], sib).wait_recv()
    rows = jnp.dot(back[...], d2[...].reshape(256, 256), preferred_element_type=F32)
    out_ref[...] = rows.astype(BF16)
    finish()


def program(raw, replica, det_bin, det_block, det_beam, owner, stop, few):
    dma = pltpu.SemaphoreType.DMA
    vm = pltpu.VMEM
    rows = (1, 128)
    return pl.pallas_call(
        functools.partial(kernel, stop, few),
        out_shape=jax.ShapeDtypeStruct((256, 256), BF16),
        in_specs=[HBM] * 8,
        out_specs=VMEM,
        scratch_shapes=[
            vm((2, 64, 32, 256), BF16),
            vm((64, 32, 128), BF16),
            vm((64, 32, 128), BF16),
            vm((64, 32, 128), BF16),
            vm((64, 32, 128), BF16),
            vm((64, 32, 384), BF16),
            vm((64, 32, 384), BF16),
            vm((512, 256), BF16),
            vm((512, 256), BF16),
            vm((35, 64, 512), BF16),
            vm((32, 64, 128), BF16),
            vm((35, 64, 128), BF16),
            vm((2, 32, 80, 128), F32),
            vm((32, 80, 128), F32),
            vm((32, 80, 128), F32),
            vm((3, 4, 80, 128), F32),
            vm((3, 4, 80, 128), F32),
            vm((8, 80, 128), F32),
            vm((15, 40, 128), F32),
            vm((3, 4, 40, 128), F32),
            vm((32, 16, 256), BF16),
            vm((512, 256), BF16),
            vm((256, 512), BF16),
            vm((256, 256), BF16),
            vm((256, 256), BF16),
            vm((16, 16, 256), BF16),
            vm((16, 16, 256), BF16),
            vm((8, 32, 256), BF16),
            vm((8, 32, 256), BF16),
            vm((2, 128), BF16),
            vm((512, 512), BF16),
            vm((8, 128), F32),
            vm(rows, jnp.int32), vm(rows, jnp.int32), vm(rows, jnp.int32), vm(rows, jnp.int32),
            dma((4,)), dma((7,)), dma((2, 4)), dma((2, 4)),
            dma((4,)), dma((4,)), dma((6,)), dma((6,)), dma((15,)), dma((15,)),
            dma((11,)), dma((3, 4)), dma((31,)), dma((32,)),
            dma((15,)), dma((15,)), dma((7,)), dma((7,)), dma(()), dma(()),
        ],
        compiler_params=pltpu.CompilerParams(
            collective_id=0, has_side_effects=True, vmem_limit_bytes=LIMIT
        ),
        name="stap",
    )(
        raw, replica, jnp.asarray(dft_matrix()), jnp.asarray(steer_rows()),
        det_bin, det_block, det_beam, owner,
    )


def on_device(stop, few, raw, replica, det_bin, det_block, det_beam, det_owner):
    rows = [v.reshape(1, 128) for v in (det_bin, det_block, det_beam, det_owner)]
    return program(raw, replica, *rows, stop=stop, few=few).astype(F32)


def solution(mesh, stop=9, few=True):
    in_specs = (
        P(None, None, None, "range"),
        P(),
        P("range"),
        P("range"),
        P("range"),
        P("range", None),
    )
    return jax.shard_map(
        functools.partial(on_device, stop, few),
        mesh=mesh,
        in_specs=in_specs,
        out_specs=P("range", None),
        check_vma=False,
    )
```

```python
import math

import jax
import jax.numpy as jnp
import numpy as np
from jax import lax
from jax.experimental import pallas as pl
from jax.experimental.pallas import tpu as pltpu
from jax.sharding import PartitionSpec as P

C = 64
PULSES = 32
TAPS = 128
BEAMS = 8
F32 = jnp.float32
BF16 = jnp.bfloat16
MESH = pl.DeviceIdType.MESH
VMEM = pl.BlockSpec(memory_space=pltpu.VMEM)
HBM = pl.BlockSpec(memory_space=pltpu.HBM)
NT = (((1,), (1,)), ((), ()))
LIMIT = 63 * 1024 * 1024
FAR = (10, 9, 11, 6, 14, 2, 8, 5, 7, 13, 15, 1, 3, 4, 12)
POSTS = (4, 5, 3, 2, 6, 7, 1)


def dft_matrix():
    index = np.arange(PULSES)
    angle = 2.0 * math.pi / PULSES * (index[:, None] * index[None, :] % PULSES)
    scale = PULSES**-0.5
    real = np.cos(angle) * scale
    imag = -np.sin(angle) * scale
    eye = np.eye(8)
    kr = np.einsum("pd,ab->dabp", real, eye).reshape(256, 256)
    ki = np.einsum("pd,ab->dabp", imag, eye).reshape(256, 256)
    full = np.concatenate([np.concatenate([kr, -ki], 1), np.concatenate([ki, kr], 1)], 0)
    return full.astype(jnp.bfloat16)


def steer_rows():
    sines = -0.8 + 1.6 * np.arange(BEAMS, dtype=np.float32) / np.float32(BEAMS - 1)
    angle = (math.pi * np.arange(C, dtype=np.float32)[None, :] * sines[:, None]).astype(np.float32)
    return np.concatenate([np.cos(angle), -np.sin(angle)], 1).astype(np.float32)


def remote(src, dst, send, recv, to):
    return pltpu.make_async_remote_copy(
        src_ref=src, dst_ref=dst, send_sem=send, recv_sem=recv, device_id=(to,), device_id_type=MESH
    )


def build_toeplitz(rep_ref, keep, tza, tz):
    def band(v):
        wide = jnp.concatenate(
            [jnp.broadcast_to(v, (TAPS, TAPS)), jnp.zeros((TAPS, TAPS), F32)], axis=1
        )
        return pltpu.roll(wide, 0, 1, stride=1, stride_axis=0).T

    rep = rep_ref[...].astype(F32)
    tr = band(rep[0:1])
    ti = band(rep[1:2])
    full = jnp.concatenate(
        [jnp.concatenate([tr, -ti], axis=1), jnp.concatenate([ti, tr], axis=1)], axis=0
    )
    tz[...] = full.astype(BF16)
    row = lax.broadcasted_iota(jnp.int32, (512, 256), 0) % 256
    lane = lax.broadcasted_iota(jnp.int32, (512, 256), 1) % 128
    tza[...] = jnp.where((row >= 64) & (lane < 64), full * keep, full).astype(BF16)


def join(*parts):
    return jnp.concatenate(parts, axis=-1)


def window_inner(at, raw, ur, ui):
    for n, u in enumerate((ur, ui)):
        u[at, :, 128:256] = join(raw[n, at, :, 64:128], raw[n, at, :, 128:192])


def window_edges(at, raw, hl, hr, ur, ui):
    for n, u in enumerate((ur, ui)):
        lanes = slice(64 * n, 64 * n + 64)
        u[at, :, 0:128] = join(hl[at, :, lanes], raw[n, at, :, 0:64])
        u[at, :, 256:384] = join(raw[n, at, :, 192:256], hr[at, :, lanes])


def spectra_part(i, ur, ui, dft_ref, s, tza, tz):
    first = 16 * i
    for b in range(2):
        ys = []
        for n in range(2):
            at = pl.ds(first + 8 * n, 8)
            gates = slice(128 * b, 128 * b + 256)
            window = join(ur[at, :, gates].reshape(256, 256), ui[at, :, gates].reshape(256, 256))
            band = tz[...] if b else tza[...]
            ys.append(jnp.dot(window, band, preferred_element_type=F32).astype(BF16))
        ya, yb = ys
        y = jnp.concatenate(
            [join(ya[:, :128], yb[:, :128]), join(ya[:, 128:], yb[:, 128:])], axis=0
        )
        out = jnp.dot(dft_ref[...], y, preferred_element_type=F32)
        for p in range(2):
            h = out[256 * p : 256 * p + 256]
            v = jnp.concatenate(
                [h[:, :128].reshape(32, 8, 128), h[:, 128:].reshape(32, 8, 128)], axis=1
            )
            lanes = 256 * b + 128 * p
            s[2:34, first : first + 16, lanes : lanes + 128] = v.astype(BF16)


def snake(k):
    z = k // 4
    x = k % 4
    return z, x + z % 2 * (3 - 2 * x)


def home(q):
    z, x = snake(q // 2)
    return z * 32 + x * 8 + q % 2 * 2


def at_home(q, member):
    return home(q) + member // 2 * 4 + member % 2


def beam_pair(first, wall, s, sr, table):
    lhs = wall[pl.ds(first, 2)].reshape(32, 256)
    rhs = join(
        s[pl.ds(first + 1, 4)].reshape(256, 512), sr[pl.ds(first + 1, 4)].reshape(256, 128)
    )
    prod = jnp.dot(lhs, rhs, preferred_element_type=F32)
    top = jnp.concatenate([prod[0:8], prod[16:24]], axis=0)
    low = jnp.concatenate([prod[8:16], prod[24:32]], axis=0)
    half = lax.broadcasted_iota(jnp.int32, (16, 128), 1) < 64

    def flip(v):
        return pltpu.roll(v, 64, 1)

    parts = []
    for at in (0, 256):
        parts.append(flip(top[:, at : at + 128] + low[:, at + 128 : at + 256]))
        parts.append(flip(top[:, at + 128 : at + 256] - low[:, at : at + 128]))
    turn = flip(low[:, 512:])
    last = top[:, 512:] + jnp.where(half, turn, -turn)
    lanes = [
        jnp.where(half, parts[0], parts[2]),
        jnp.where(half, parts[1], parts[3]),
        jnp.where(half, parts[2], flip(last)),
        jnp.where(half, parts[3], last),
    ]
    for i in range(2):
        rows = pl.ds(pl.multiple_of(256 * i + first * 8, 16), 16)
        table[rows] = join(*lanes[2 * i : 2 * i + 2]).astype(BF16)


def store_products(p, places, two, one, zero):
    lane = lax.broadcasted_iota(jnp.int32, (32, 128), 1)
    row = lax.broadcasted_iota(jnp.int32, (32, 128), 0)
    swapped = pltpu.roll(zero, 64, 1)
    top = jnp.where(row >= lane, zero[:32], swapped[:32])
    bottom = jnp.where(row + 32 >= lane - 64, swapped[32:], zero[32:])
    packed = jnp.where(lane < 64, top, bottom)
    for h in range(2):
        pos = places[h]
        for q in range(2):
            a = 32 * h + 16 * q
            p[h, pos, 40 * q : 40 * q + 16] = two[a : a + 16]
            p[h, pos, 40 * q + 16 : 40 * q + 32] = one[a : a + 16]
            p[h, pos, 40 * q + 32 : 40 * q + 40] = packed[a // 2 : a // 2 + 8]


def cross_products(z, x, s, p):
    f = 2 * (4 * z + x + z % 2 * (3 - 2 * x))
    lhs = s[pl.ds(f, 4)].reshape(256, 512)
    rhs = []
    for n in range(2):
        v = s[f + 2 + n]
        rhs += [v, join(-v[:, 128:256], v[:, :128], -v[:, 384:], v[:, 256:384])]
    prod = lax.dot_general(lhs, jnp.concatenate(rhs, axis=0), NT, preferred_element_type=F32)
    first, second = (z * 8 + x * 2, x * 8 + z * 2), (z * 8 + x * 2 + 1, x * 8 + z * 2 + 1)
    store_products(p, first, prod[:64, :128], prod[64:128, :128], prod[128:192, :128])
    store_products(p, second, prod[64:128, 128:], prod[128:192, 128:], prod[192:, 128:])


def times_i(m):
    return jnp.concatenate([-m[:, 64:], m[:, :64]], axis=1)


def cdot(x, y):
    return jnp.dot(
        x, jnp.concatenate([y, times_i(y)], axis=0),
        preferred_element_type=F32, precision=lax.Precision.HIGHEST,
    )


def adjoint(m):
    t = m.T
    return jnp.concatenate([t[:64], -t[64:]], axis=1)


def lane_of(v, k):
    return jnp.broadcast_to(v[:, k : k + 1], (8, 128))


def row_of(v, r):
    return jnp.broadcast_to(v[r : r + 1], (8, 128))


def cmul(x, y):
    return (x[0] * y[0] - x[1] * y[1], x[0] * y[1] + x[1] * y[0])


def cmulc(x, y):
    return (x[0] * y[0] + x[1] * y[1], x[1] * y[0] - x[0] * y[1])


def cadd(x, y):
    return (x[0] + y[0], x[1] + y[1])


def csub(x, y):
    return (x[0] - y[0], x[1] - y[1])


def cscale(x, c):
    return (x * c[0], x * c[1])


def conj(x):
    return (x[0], -x[1])


def size2(x):
    return x[0] * x[0] + x[1] * x[1]


def rdot(x, y):
    return x[0] * y[0] + x[1] * y[1]


def cm(c, row):
    v, w = row
    return (c[0] * v + c[1] * w, c[0] * w - c[1] * v)


def hermitian_inverse(m):
    lane = lax.broadcasted_iota(jnp.int32, (8, 128), 1)
    sub = lax.broadcasted_iota(jnp.int32, (8, 128), 0)
    ms = [m[8 * t : 8 * t + 8] for t in range(8)]
    for k in range(0, 64, 4):
        t0, r0 = divmod(k, 8)
        w = ms[t0]
        wi = pltpu.roll(w, 64, 1)
        wi = jnp.where(lane < 64, -wi, wi)
        cr = [[lane_of(v, k + j) for v in ms] for j in range(4)]
        ci = [[lane_of(v, 64 + k + j) for v in ms] for j in range(4)]

        def entry(i, j):
            return (row_of(cr[j][t0], r0 + i), row_of(ci[j][t0], r0 + i))

        a, d, b = entry(0, 0)[0], entry(1, 1)[0], entry(0, 1)
        p, s, q = entry(2, 2)[0], entry(3, 3)[0], entry(2, 3)
        bb = [[entry(0, 2), entry(0, 3)], [entry(1, 2), entry(1, 3)]]
        det = 1.0 / (a * d - size2(b))
        ia, id_, ib = d * det, a * det, cscale(-det, b)
        ww = [
            [cadd(cscale(ia, bb[0][j]), cmul(ib, bb[1][j])) for j in range(2)],
            [cadd(cmul(conj(ib), bb[0][j]), cscale(id_, bb[1][j])) for j in range(2)],
        ]
        s00 = p - (rdot(bb[0][0], ww[0][0]) + rdot(bb[1][0], ww[1][0]))
        s11 = s - (rdot(bb[0][1], ww[0][1]) + rdot(bb[1][1], ww[1][1]))
        s01 = csub(q, cadd(cmulc(ww[0][1], bb[0][0]), cmulc(ww[1][1], bb[1][0])))
        dets = 1.0 / (s00 * s11 - size2(s01))
        j00, j11, j01 = s11 * dets, s00 * dets, cscale(-dets, s01)
        hit = ((lane >= k) & (lane < k + 4)) | ((lane >= 64 + k) & (lane < 68 + k))
        rows = []
        for j in range(4):
            real = jnp.where(hit, jnp.where(lane == k + j, 1.0, 0.0), row_of(w, r0 + j))
            imag = jnp.where(hit, jnp.where(lane == 64 + k + j, 1.0, 0.0), row_of(wi, r0 + j))
            rows.append((real, imag))
        t2 = csub(rows[2], cadd(cm(conj(ww[0][0]), rows[0]), cm(conj(ww[1][0]), rows[1])))
        t3 = csub(rows[3], cadd(cm(conj(ww[0][1]), rows[0]), cm(conj(ww[1][1]), rows[1])))
        x2 = cadd(cscale(j00, t2), cm(j01, t3))
        x3 = cadd(cscale(j11, t3), cm(conj(j01), t2))
        u0 = cadd(cscale(ia, rows[0]), cm(ib, rows[1]))
        u1 = cadd(cscale(id_, rows[1]), cm(conj(ib), rows[0]))
        x0 = csub(u0, cadd(cm(ww[0][0], x2), cm(ww[0][1], x3)))
        x1 = csub(u1, cadd(cm(ww[1][0], x2), cm(ww[1][1], x3)))
        g = [x0, x1, x2, x3]
        for t in range(8):
            terms = [cr[j][t] * g[j][0] + ci[j][t] * g[j][1] for j in range(4)]
            mt = jnp.where(hit, 0.0, ms[t]) - ((terms[0] + terms[1]) + (terms[2] + terms[3]))
            if t == t0:
                for j in range(4):
                    mt = jnp.where(sub == r0 + j, g[j][0], mt)
            ms[t] = mt
    return jnp.concatenate(ms, axis=0)


def solve(g_ref, steer_ref, parity, others):
    scale = 1.0 / 32768.0
    order = (0, 2, 1, 3)
    r64 = lax.broadcasted_iota(jnp.int32, (64, 64), 0)
    c64 = lax.broadcasted_iota(jnp.int32, (64, 64), 1)

    def block(g, rows):
        return jnp.concatenate([g_ref[g, m, rows] for m in order], axis=0) * scale

    def diagonal(g):
        pk = block(g, slice(32, 40))
        k = jnp.concatenate([pk[:, :64], pk[:, 64:]], axis=0)
        kt = k.T
        real = jnp.where(r64 >= c64, k, kt)
        imag = jnp.where(r64 < c64, k, jnp.where(r64 == c64, 0.0, -kt))
        return jnp.concatenate([real, imag], axis=1)

    p = hermitian_inverse(diagonal(0))
    others()
    a33 = diagonal(1)
    a22 = diagonal(2)
    a12 = block(2, slice(0, 16))
    a13 = block(1, slice(16, 32))
    a32 = block(2, slice(16, 32))
    v21 = cdot(adjoint(a12), p)
    v31 = cdot(adjoint(a13), p)
    s22 = a22 - cdot(v21, a12)
    s32 = a32 - cdot(v31, a12)
    s33 = a33 - cdot(v31, a13)
    q = hermitian_inverse(s22)
    v32 = cdot(s32, q)
    s33 = s33 - cdot(v32, adjoint(s32))
    r = hermitian_inverse(s33)
    t = steer_ref[...]
    y3 = cdot(t, r)
    y2 = -cdot(y3, v32)
    y1 = -cdot(y2, v21) - cdot(y3, v31)
    norm = lax.rsqrt(jnp.sum(t * y3, axis=1, keepdims=True))
    real = [(v[:, :64] * norm) for v in (y1, y3, y2)]
    imag = [(v[:, 64:] * -norm) for v in (y1, y3, y2)]
    rows = jnp.concatenate(
        [jnp.concatenate(real, axis=1), jnp.concatenate(imag, axis=1)], axis=0
    )
    zero = jnp.zeros((16, 64), F32)
    even = jnp.concatenate([rows, zero], axis=1)
    odd = jnp.concatenate([zero, rows], axis=1)
    return jnp.where(parity == 0, even, odd).astype(BF16)


def selection(bin_ref, block_ref, beam_ref, owner_ref, select, turn, back):
    s_iota = lax.broadcasted_iota(jnp.int32, (256, 128), 0)
    named = (s_iota // 2 == owner_ref[...]).astype(F32)
    before = (
        lax.broadcasted_iota(jnp.int32, (128, 128), 0)
        < lax.broadcasted_iota(jnp.int32, (128, 128), 1)
    ).astype(F32)
    earlier = jnp.dot(named.astype(BF16), before.astype(BF16), preferred_element_type=F32)
    pick = jnp.where(earlier == (s_iota % 2).astype(F32), named, 0.0).astype(BF16)
    wanted = block_ref[...] * 256 + bin_ref[...] * 8 + beam_ref[...]
    t_iota = lax.broadcasted_iota(jnp.int32, (512, 128), 0)
    holds = (t_iota == wanted).astype(F32).astype(BF16)
    select[...] = lax.dot_general(pick, holds, NT, preferred_element_type=F32).astype(BF16)
    o = lax.broadcasted_iota(jnp.int32, (256, 256), 0)
    i = lax.broadcasted_iota(jnp.int32, (256, 256), 1)
    turn[...] = (i == o % 32 // 2 * 16 + o // 32 * 2 + o % 2).astype(F32).astype(BF16)
    back[...] = (i == o % 16 // 2 * 32 + o // 16 * 2 + o % 2).astype(F32).astype(BF16)


def kernel(
    raw_ref, rep_in, dft_in, steer_in, bin_in, block_in, beam_in, owner_in,
    out_ref,
    raw, pkl, pkr, hl, hr, ur, ui, tza, tz, s, pks, sr, p, r1, a1, rp, rm, a2, r3, gath, wall, table,
    select, turn, back, slots, d1, mid, d2,
    rep_ref, dft_ref, steer_ref, bin_ref, block_ref, beam_ref, owner_ref,
    ls, ms, hs, ht, s1, t1, s2, t2, s3, t3, s5, t5, s6, t6, s7, t7, s8, t8, s9, t9,
):
    me = lax.axis_index("range")
    core = me % 2
    y = me // 2 % 4
    x = me // 8 % 4
    z = me // 32
    zx = me // 8
    yc = me % 8
    bin_ = 2 * (4 * z + x + z % 2 * (3 - 2 * x)) + y % 2
    member = y // 2 * 2 + core
    sib = me + 1 - 2 * core
    sa = 32 - 24 * core
    sb = 8 + 24 * core
    a = me // sa % 4
    b = me // sb % 4
    left = (me + 127) % 128
    right = (me + 1) % 128

    def along(stride, coord, j):
        return me + ((coord + j) % 4 - coord) * stride

    near = []
    for delta in (1, -1, 0):
        for j in range(4):
            if delta or j:
                near.append((delta, j, at_home((bin_ + delta + 32) % 32, (member + j) % 4)))
    bins = [(bin_ + j) % 32 for j in sorted(range(1, 32), key=lambda j: abs(j - 16))]
    planes = [(z + j // 4) % 4 * 4 + (x + j % 4) % 4 for j in FAR]
    froms = [(z + 4 - j // 4) % 4 * 4 + (x + 4 - j % 4) % 4 for j in FAR]
    posts = [(yc + j) % 8 for j in POSTS]
    sheet = [
        ((b + j // 4) % 4, (y + j % 4) % 4)
        for j in FAR
    ]
    spots = [me + (q - b) * sb + (r - y) * 2 for q, r in sheet]
    partners = [left, right, sib, along(sa, a, 1), along(sa, a, 3)] + spots
    small = [
        pltpu.make_async_copy(src, dst, ms.at[n])
        for n, (src, dst) in enumerate(
            [
                (rep_in, rep_ref), (dft_in, dft_ref), (steer_in, steer_ref), (bin_in, bin_ref),
                (block_in, block_ref), (beam_in, beam_ref), (owner_in, owner_ref),
            ]
        )
    ]
    small[0].start()
    loads = []
    for i in range(4):
        at = pl.ds(16 * i, 16)
        copy = pltpu.make_async_copy(raw_ref.at[:, at], raw.at[:, at], ls.at[i])
        copy.start()
        loads.append(copy)
    for copy in small[1:]:
        copy.start()
    barrier = pltpu.get_barrier_semaphore()
    for to in partners:
        pl.semaphore_signal(barrier, inc=1, device_id=(to,), device_id_type=MESH)
    for i in range(4):
        at = pl.ds(16 * i, 16)
        loads[i].wait()
        pkl[at] = jnp.concatenate([raw[0, at, :, 0:64], raw[1, at, :, 0:64]], axis=-1)
        pkr[at] = jnp.concatenate([raw[0, at, :, 192:256], raw[1, at, :, 192:256]], axis=-1)
        window_inner(at, raw, ur, ui)
    pl.semaphore_wait(barrier, len(partners))
    copies = []

    def finish():
        for copy in copies:
            copy.wait_send()


    def to_left(i):
        at = pl.ds(16 * i, 16)
        return remote(pkl.at[at], hr.at[at], hs.at[0, i], ht.at[0, i], left)

    for i in range(4):
        at = pl.ds(16 * i, 16)
        copy = remote(pkr.at[at], hl.at[at], hs.at[1, i], ht.at[1, i], right)
        copy.start()
        copies.append(copy)

        @pl.when(me > 0)
        def _():
            to_left(i).start()

    @pl.when(me == 127)
    def _():
        hr[...] = jnp.zeros_like(hr)

    small[0].wait()
    build_toeplitz(rep_ref, jnp.where(me > 0, 1.0, 0.0).astype(F32), tza, tz)
    for copy in small[1:]:
        copy.wait()
    selection(bin_ref, block_ref, beam_ref, owner_ref, select, turn, back)
    for i in range(4):
        copies[i].wait_recv()

        @pl.when(me < 127)
        def _():
            to_left(i).wait_recv()

        window_edges(pl.ds(16 * i, 16), raw, hl, hr, ur, ui)
        spectra_part(i, ur, ui, dft_ref, s, tza, tz)

    @pl.when(me > 0)
    def _():
        for i in range(4):
            to_left(i).wait_send()

    s[0:2] = s[32:34]
    s[34] = s[2]
    pks[...] = join(s[2:34, :, 0:64], s[2:34, :, 128:192])
    share = remote(pks, sr.at[pl.ds(2, 32)], s9, t9, left)

    order = (2, 1, 3, 0)
    oa = me // sb % 4
    for j in order:
        q = (oa + j) % 4
        for u in range(4):
            cross_products(core * q + (1 - core) * u, core * u + (1 - core) * q, s, p)
        at = pl.ds(q * 8, 8)
        copy = remote(p.at[1 - core, at], r1.at[at], s1.at[j], t1.at[j], sib)
        copy.start()
        copies.append(copy)

    rings = []

    def ring(src, dst, n, to):
        copy = remote(src, dst, s2.at[n], t2.at[n], to)
        copy.start()
        copies.append(copy)
        rings.append(copy)

    ahead, behind = along(sa, a, 1), along(sa, a, 3)
    base = {j: (a + j) % 4 * 8 for j in range(4)}
    for j in order:
        at = pl.ds(base[j], 8)
        remote(p.at[core, at], r1.at[at], s1.at[j], t1.at[j], sib).wait_recv()
        a1[at] = p[core, at] + r1[at]
        if j == 2:
            ring(a1.at[pl.ds(base[2], 4)], rp.at[0], 0, ahead)
            ring(a1.at[pl.ds(base[2] + 4, 4)], rm.at[0], 1, behind)
        elif j == 1:
            ring(a1.at[pl.ds(base[1] + 4, 4)], rp.at[1], 2, ahead)
        elif j == 3:
            ring(a1.at[pl.ds(base[3], 4)], rm.at[1], 3, behind)
    rings[0].wait_recv()
    at = pl.ds(base[1], 4)
    a1[at] = a1[at] + rp[0]
    ring(a1.at[at], rp.at[2], 4, ahead)
    rings[1].wait_recv()
    at = pl.ds(base[3] + 4, 4)
    a1[at] = a1[at] + rm[0]
    ring(a1.at[at], rm.at[2], 5, behind)
    for n in (2, 3):
        rings[n].wait_recv()
    at = pl.ds(base[0] + 4, 4)
    a2[4:8] = a1[at] + rp[1]
    at = pl.ds(base[0], 4)
    a2[0:4] = a1[at] + rm[1]
    rings[4].wait_recv()
    a2[0:4] = a2[0:4] + rp[2]
    rings[5].wait_recv()
    a2[4:8] = a2[4:8] + rm[2]

    for n, (q, r) in enumerate(sheet):
        src = a2.at[q * 2 + r % 2, pl.ds(pl.multiple_of(r // 2 * 40, 8), 40)]
        copy = remote(src, r3.at[n], s3.at[n], t3.at[n], spots[n])
        copy.start()
        copies.append(copy)
    for n in range(15):
        remote(r3.at[n], r3.at[n], s3.at[n], t3.at[n], sib).wait_recv()
    mine = a2[b * 2 + y % 2, pl.ds(pl.multiple_of(y // 2 * 40, 8), 40)]
    terms = [mine] + [r3[n] for n in range(15)]
    while len(terms) > 1:
        terms = [u + v for u, v in zip(terms[::2], terms[1::2])]
    gath[1, member] = terms[0]
    needs = {-1: pl.ds(0, 40), 0: pl.ds(16, 24), 1: pl.ds(32, 8)}
    for n, (delta, j, to) in enumerate(near):
        rows = needs[delta]
        copy = remote(
            gath.at[1, member, rows], gath.at[1 - delta, member, rows], s5.at[n],
            t5.at[1 - delta, member], to,
        )
        copy.start()
        copies.append(copy)

    def arrived(deltas):
        for delta, j, _ in near:
            if delta in deltas:
                part = gath.at[1 - delta, (member + j) % 4, needs[delta]]
                remote(part, part, s5.at[0], t5.at[1 - delta, (member + j) % 4], sib).wait_recv()

    arrived((1,))

    def others():
        arrived((-1, 0))
        share.start()
        copies.append(share)

    wall[bin_] = solve(gath, steer_ref, bin_ % 2, others)
    share.wait_recv()
    sr[0:2] = sr[32:34]
    sr[34] = sr[2]
    for n, to in enumerate(bins):
        copy = remote(wall.at[bin_], wall.at[bin_], s6.at[n], t6.at[bin_], at_home(to, member))
        copy.start()
        copies.append(copy)

    for n in (0, 1, 15, 2, 14, 3, 13, 4, 12, 5, 11, 6, 10, 7, 9, 8):
        duo = (bin_ // 2 + 16 - n) % 16
        first = duo * 2
        waits = (first, first + 1) if n else (bin_ + 1 - 2 * (bin_ % 2),)
        for q in waits:
            remote(wall.at[q], wall.at[q], s6.at[0], t6.at[q], sib).wait_recv()
        beam_pair(first, wall, s, sr, table)

    slots[...] = (
        jnp.dot(select[...], table[...], preferred_element_type=F32)
        .astype(BF16)
        .reshape(16, 16, 256)
    )
    for j, q in enumerate(planes):
        copy = remote(slots.at[q], d1.at[zx], s7.at[j], t7.at[j], q * 8 + yc)
        copy.start()
        copies.append(copy)
    d1[zx] = slots[zx]
    for j, q in enumerate(froms):
        remote(slots.at[q], d1.at[q], s7.at[j], t7.at[j], sib).wait_recv()
    mid[...] = (
        jnp.dot(turn[...], d1[...].reshape(256, 256), preferred_element_type=F32)
        .astype(BF16)
        .reshape(8, 32, 256)
    )
    for j, q in enumerate(posts):
        copy = remote(mid.at[q], d2.at[yc], s8.at[j], t8.at[j], zx * 8 + q)
        copy.start()
        copies.append(copy)
    d2[yc] = mid[yc]
    for j, step in enumerate(POSTS):
        q = (yc + 8 - step) % 8
        remote(mid.at[q], d2.at[q], s8.at[j], t8.at[j], sib).wait_recv()
    rows = jnp.dot(back[...], d2[...].reshape(256, 256), preferred_element_type=F32)
    out_ref[...] = rows.astype(BF16)
    finish()


def program(raw, replica, det_bin, det_block, det_beam, owner):
    dma = pltpu.SemaphoreType.DMA
    vm = pltpu.VMEM
    rows = (1, 128)
    return pl.pallas_call(
        kernel,
        out_shape=jax.ShapeDtypeStruct((256, 256), BF16),
        in_specs=[HBM] * 8,
        out_specs=VMEM,
        scratch_shapes=[
            vm((2, 64, 32, 256), BF16),
            vm((64, 32, 128), BF16),
            vm((64, 32, 128), BF16),
            vm((64, 32, 128), BF16),
            vm((64, 32, 128), BF16),
            vm((64, 32, 384), BF16),
            vm((64, 32, 384), BF16),
            vm((512, 256), BF16),
            vm((512, 256), BF16),
            vm((35, 64, 512), BF16),
            vm((32, 64, 128), BF16),
            vm((35, 64, 128), BF16),
            vm((2, 32, 80, 128), F32),
            vm((32, 80, 128), F32),
            vm((32, 80, 128), F32),
            vm((3, 4, 80, 128), F32),
            vm((3, 4, 80, 128), F32),
            vm((8, 80, 128), F32),
            vm((15, 40, 128), F32),
            vm((3, 4, 40, 128), F32),
            vm((32, 16, 256), BF16),
            vm((512, 256), BF16),
            vm((256, 512), BF16),
            vm((256, 256), BF16),
            vm((256, 256), BF16),
            vm((16, 16, 256), BF16),
            vm((16, 16, 256), BF16),
            vm((8, 32, 256), BF16),
            vm((8, 32, 256), BF16),
            vm((2, 128), BF16),
            vm((512, 512), BF16),
            vm((8, 128), F32),
            vm(rows, jnp.int32), vm(rows, jnp.int32), vm(rows, jnp.int32), vm(rows, jnp.int32),
            dma((4,)), dma((7,)), dma((2, 4)), dma((2, 4)),
            dma((4,)), dma((4,)), dma((6,)), dma((6,)), dma((15,)), dma((15,)),
            dma((11,)), dma((3, 4)), dma((31,)), dma((32,)),
            dma((15,)), dma((15,)), dma((7,)), dma((7,)), dma(()), dma(()),
        ],
        compiler_params=pltpu.CompilerParams(
            collective_id=0, has_side_effects=True, vmem_limit_bytes=LIMIT
        ),
        name="stap",
    )(
        raw, replica, jnp.asarray(dft_matrix()), jnp.asarray(steer_rows()),
        det_bin, det_block, det_beam, owner,
    )


def on_device(raw, replica, det_bin, det_block, det_beam, det_owner):
    rows = [v.reshape(1, 128) for v in (det_bin, det_block, det_beam, det_owner)]
    return program(raw, replica, *rows).astype(F32)


def solution(mesh):
    in_specs = (
        P(None, None, None, "range"),
        P(),
        P("range"),
        P("range"),
        P("range"),
        P("range", None),
    )
    return jax.shard_map(
        on_device,
        mesh=mesh,
        in_specs=in_specs,
        out_specs=P("range", None),
        check_vma=False,
    )
```

```python
import math

import jax
import jax.numpy as jnp
import numpy as np
from jax import lax
from jax.experimental import pallas as pl
from jax.experimental.pallas import tpu as pltpu
from jax.sharding import PartitionSpec as P

C = 64
PULSES = 32
TAPS = 128
BEAMS = 8
F32 = jnp.float32
BF16 = jnp.bfloat16
MESH = pl.DeviceIdType.MESH
VMEM = pl.BlockSpec(memory_space=pltpu.VMEM)
HBM = pl.BlockSpec(memory_space=pltpu.HBM)
NT = (((1,), (1,)), ((), ()))
LIMIT = 63 * 1024 * 1024
FAR = (10, 9, 11, 6, 14, 2, 8, 5, 7, 13, 15, 1, 3, 4, 12)
POSTS = (4, 5, 3, 2, 6, 7, 1)


def dft_matrix():
    index = np.arange(PULSES)
    angle = 2.0 * math.pi / PULSES * (index[:, None] * index[None, :] % PULSES)
    scale = PULSES**-0.5
    real = np.cos(angle) * scale
    imag = -np.sin(angle) * scale
    eye = np.eye(8)
    kr = np.einsum("pd,ab->dabp", real, eye).reshape(256, 256)
    ki = np.einsum("pd,ab->dabp", imag, eye).reshape(256, 256)
    full = np.concatenate([np.concatenate([kr, -ki], 1), np.concatenate([ki, kr], 1)], 0)
    return full.astype(jnp.bfloat16)


def steer_rows():
    sines = -0.8 + 1.6 * np.arange(BEAMS, dtype=np.float32) / np.float32(BEAMS - 1)
    angle = (math.pi * np.arange(C, dtype=np.float32)[None, :] * sines[:, None]).astype(np.float32)
    return np.concatenate([np.cos(angle), -np.sin(angle)], 1).astype(np.float32)


def remote(src, dst, send, recv, to):
    return pltpu.make_async_remote_copy(
        src_ref=src, dst_ref=dst, send_sem=send, recv_sem=recv, device_id=(to,), device_id_type=MESH
    )


def build_toeplitz(rep_ref, keep, tza, tz):
    def band(v):
        wide = jnp.concatenate(
            [jnp.broadcast_to(v, (TAPS, TAPS)), jnp.zeros((TAPS, TAPS), F32)], axis=1
        )
        return pltpu.roll(wide, 0, 1, stride=1, stride_axis=0).T

    rep = rep_ref[...].astype(F32)
    tr = band(rep[0:1])
    ti = band(rep[1:2])
    full = jnp.concatenate(
        [jnp.concatenate([tr, -ti], axis=1), jnp.concatenate([ti, tr], axis=1)], axis=0
    )
    tz[...] = full.astype(BF16)
    row = lax.broadcasted_iota(jnp.int32, (512, 256), 0) % 256
    lane = lax.broadcasted_iota(jnp.int32, (512, 256), 1) % 128
    tza[...] = jnp.where((row >= 64) & (lane < 64), full * keep, full).astype(BF16)


def join(*parts):
    return jnp.concatenate(parts, axis=-1)


def window_inner(at, raw, ur, ui):
    for n, u in enumerate((ur, ui)):
        u[at, :, 128:256] = join(raw[n, at, :, 64:128], raw[n, at, :, 128:192])


def window_edges(at, raw, hl, hr, ur, ui):
    for n, u in enumerate((ur, ui)):
        lanes = slice(64 * n, 64 * n + 64)
        u[at, :, 0:128] = join(hl[at, :, lanes], raw[n, at, :, 0:64])
        u[at, :, 256:384] = join(raw[n, at, :, 192:256], hr[at, :, lanes])


def spectra_part(i, ur, ui, dft_ref, s, tza, tz):
    first = 16 * i
    for b in range(2):
        ys = []
        for n in range(2):
            at = pl.ds(first + 8 * n, 8)
            gates = slice(128 * b, 128 * b + 256)
            window = join(ur[at, :, gates].reshape(256, 256), ui[at, :, gates].reshape(256, 256))
            band = tz[...] if b else tza[...]
            ys.append(jnp.dot(window, band, preferred_element_type=F32).astype(BF16))
        ya, yb = ys
        y = jnp.concatenate(
            [join(ya[:, :128], yb[:, :128]), join(ya[:, 128:], yb[:, 128:])], axis=0
        )
        out = jnp.dot(dft_ref[...], y, preferred_element_type=F32)
        for p in range(2):
            h = out[256 * p : 256 * p + 256]
            v = jnp.concatenate(
                [h[:, :128].reshape(32, 8, 128), h[:, 128:].reshape(32, 8, 128)], axis=1
            )
            lanes = 256 * b + 128 * p
            s[2:34, first : first + 16, lanes : lanes + 128] = v.astype(BF16)


def snake(k):
    z = k // 4
    x = k % 4
    return z, x + z % 2 * (3 - 2 * x)


def home(q):
    z, x = snake(q // 2)
    return z * 32 + x * 8 + q % 2 * 2


def at_home(q, member):
    return home(q) + member // 2 * 4 + member % 2


def beam_pair(first, wall, s, sr, table):
    lhs = wall[pl.ds(first, 2)].reshape(32, 256)
    rhs = join(
        s[pl.ds(first + 1, 4)].reshape(256, 512), sr[pl.ds(first + 1, 4)].reshape(256, 128)
    )
    prod = jnp.dot(lhs, rhs, preferred_element_type=F32)
    top = jnp.concatenate([prod[0:8], prod[16:24]], axis=0)
    low = jnp.concatenate([prod[8:16], prod[24:32]], axis=0)
    half = lax.broadcasted_iota(jnp.int32, (16, 128), 1) < 64

    def flip(v):
        return pltpu.roll(v, 64, 1)

    parts = []
    for at in (0, 256):
        parts.append(flip(top[:, at : at + 128] + low[:, at + 128 : at + 256]))
        parts.append(flip(top[:, at + 128 : at + 256] - low[:, at : at + 128]))
    turn = flip(low[:, 512:])
    last = top[:, 512:] + jnp.where(half, turn, -turn)
    lanes = [
        jnp.where(half, parts[0], parts[2]),
        jnp.where(half, parts[1], parts[3]),
        jnp.where(half, parts[2], flip(last)),
        jnp.where(half, parts[3], last),
    ]
    for i in range(2):
        rows = pl.ds(pl.multiple_of(256 * i + first * 8, 16), 16)
        table[rows] = join(*lanes[2 * i : 2 * i + 2]).astype(BF16)


def store_products(p, places, two, one, zero):
    lane = lax.broadcasted_iota(jnp.int32, (32, 128), 1)
    row = lax.broadcasted_iota(jnp.int32, (32, 128), 0)
    swapped = pltpu.roll(zero, 64, 1)
    top = jnp.where(row >= lane, zero[:32], swapped[:32])
    bottom = jnp.where(row + 32 >= lane - 64, swapped[32:], zero[32:])
    packed = jnp.where(lane < 64, top, bottom)
    for h in range(2):
        pos = places[h]
        for q in range(2):
            a = 32 * h + 16 * q
            p[h, pos, 40 * q : 40 * q + 16] = two[a : a + 16]
            p[h, pos, 40 * q + 16 : 40 * q + 32] = one[a : a + 16]
            p[h, pos, 40 * q + 32 : 40 * q + 40] = packed[a // 2 : a // 2 + 8]


def cross_products(z, x, s, p):
    f = 2 * (4 * z + x + z % 2 * (3 - 2 * x))
    lhs = s[pl.ds(f, 4)].reshape(256, 512)
    rhs = []
    for n in range(2):
        v = s[f + 2 + n]
        rhs += [v, join(-v[:, 128:256], v[:, :128], -v[:, 384:], v[:, 256:384])]
    prod = lax.dot_general(lhs, jnp.concatenate(rhs, axis=0), NT, preferred_element_type=F32)
    first, second = (z * 8 + x * 2, x * 8 + z * 2), (z * 8 + x * 2 + 1, x * 8 + z * 2 + 1)
    store_products(p, first, prod[:64, :128], prod[64:128, :128], prod[128:192, :128])
    store_products(p, second, prod[64:128, 128:], prod[128:192, 128:], prod[192:, 128:])


def times_i(m):
    return jnp.concatenate([-m[:, 64:], m[:, :64]], axis=1)


def cdot(x, y):
    return jnp.dot(
        x, jnp.concatenate([y, times_i(y)], axis=0),
        preferred_element_type=F32, precision=lax.Precision.HIGHEST,
    )


def adjoint(m):
    t = m.T
    return jnp.concatenate([t[:64], -t[64:]], axis=1)


def lane_of(v, k):
    return jnp.broadcast_to(v[:, k : k + 1], (8, 128))


def row_of(v, r):
    return jnp.broadcast_to(v[r : r + 1], (8, 128))


def cmul(x, y):
    return (x[0] * y[0] - x[1] * y[1], x[0] * y[1] + x[1] * y[0])


def cmulc(x, y):
    return (x[0] * y[0] + x[1] * y[1], x[1] * y[0] - x[0] * y[1])


def cadd(x, y):
    return (x[0] + y[0], x[1] + y[1])


def csub(x, y):
    return (x[0] - y[0], x[1] - y[1])


def cscale(x, c):
    return (x * c[0], x * c[1])


def conj(x):
    return (x[0], -x[1])


def size2(x):
    return x[0] * x[0] + x[1] * x[1]


def rdot(x, y):
    return x[0] * y[0] + x[1] * y[1]


def cm(c, row):
    v, w = row
    return (c[0] * v + c[1] * w, c[0] * w - c[1] * v)


def hermitian_inverse(m):
    lane = lax.broadcasted_iota(jnp.int32, (8, 128), 1)
    sub = lax.broadcasted_iota(jnp.int32, (8, 128), 0)
    ms = [m[8 * t : 8 * t + 8] for t in range(8)]
    for k in range(0, 64, 4):
        t0, r0 = divmod(k, 8)
        w = ms[t0]
        wi = pltpu.roll(w, 64, 1)
        wi = jnp.where(lane < 64, -wi, wi)
        cr = [[lane_of(v, k + j) for v in ms] for j in range(4)]
        ci = [[lane_of(v, 64 + k + j) for v in ms] for j in range(4)]

        def entry(i, j):
            return (row_of(cr[j][t0], r0 + i), row_of(ci[j][t0], r0 + i))

        a, d, b = entry(0, 0)[0], entry(1, 1)[0], entry(0, 1)
        p, s, q = entry(2, 2)[0], entry(3, 3)[0], entry(2, 3)
        bb = [[entry(0, 2), entry(0, 3)], [entry(1, 2), entry(1, 3)]]
        det = 1.0 / (a * d - size2(b))
        ia, id_, ib = d * det, a * det, cscale(-det, b)
        ww = [
            [cadd(cscale(ia, bb[0][j]), cmul(ib, bb[1][j])) for j in range(2)],
            [cadd(cmul(conj(ib), bb[0][j]), cscale(id_, bb[1][j])) for j in range(2)],
        ]
        s00 = p - (rdot(bb[0][0], ww[0][0]) + rdot(bb[1][0], ww[1][0]))
        s11 = s - (rdot(bb[0][1], ww[0][1]) + rdot(bb[1][1], ww[1][1]))
        s01 = csub(q, cadd(cmulc(ww[0][1], bb[0][0]), cmulc(ww[1][1], bb[1][0])))
        dets = 1.0 / (s00 * s11 - size2(s01))
        j00, j11, j01 = s11 * dets, s00 * dets, cscale(-dets, s01)
        hit = ((lane >= k) & (lane < k + 4)) | ((lane >= 64 + k) & (lane < 68 + k))
        rows = []
        for j in range(4):
            real = jnp.where(hit, jnp.where(lane == k + j, 1.0, 0.0), row_of(w, r0 + j))
            imag = jnp.where(hit, jnp.where(lane == 64 + k + j, 1.0, 0.0), row_of(wi, r0 + j))
            rows.append((real, imag))
        t2 = csub(rows[2], cadd(cm(conj(ww[0][0]), rows[0]), cm(conj(ww[1][0]), rows[1])))
        t3 = csub(rows[3], cadd(cm(conj(ww[0][1]), rows[0]), cm(conj(ww[1][1]), rows[1])))
        x2 = cadd(cscale(j00, t2), cm(j01, t3))
        x3 = cadd(cscale(j11, t3), cm(conj(j01), t2))
        u0 = cadd(cscale(ia, rows[0]), cm(ib, rows[1]))
        u1 = cadd(cscale(id_, rows[1]), cm(conj(ib), rows[0]))
        x0 = csub(u0, cadd(cm(ww[0][0], x2), cm(ww[0][1], x3)))
        x1 = csub(u1, cadd(cm(ww[1][0], x2), cm(ww[1][1], x3)))
        g = [x0, x1, x2, x3]
        for t in range(8):
            terms = [cr[j][t] * g[j][0] + ci[j][t] * g[j][1] for j in range(4)]
            mt = jnp.where(hit, 0.0, ms[t]) - ((terms[0] + terms[1]) + (terms[2] + terms[3]))
            if t == t0:
                for j in range(4):
                    mt = jnp.where(sub == r0 + j, g[j][0], mt)
            ms[t] = mt
    return jnp.concatenate(ms, axis=0)


def solve(g_ref, steer_ref, parity, others):
    scale = 1.0 / 32768.0
    order = (0, 2, 1, 3)
    r64 = lax.broadcasted_iota(jnp.int32, (64, 64), 0)
    c64 = lax.broadcasted_iota(jnp.int32, (64, 64), 1)

    def block(g, rows):
        return jnp.concatenate([g_ref[g, m, rows] for m in order], axis=0) * scale

    def diagonal(g):
        pk = block(g, slice(32, 40))
        k = jnp.concatenate([pk[:, :64], pk[:, 64:]], axis=0)
        kt = k.T
        real = jnp.where(r64 >= c64, k, kt)
        imag = jnp.where(r64 < c64, k, jnp.where(r64 == c64, 0.0, -kt))
        return jnp.concatenate([real, imag], axis=1)

    p = hermitian_inverse(diagonal(0))
    others()
    a33 = diagonal(1)
    a22 = diagonal(2)
    a12 = block(2, slice(0, 16))
    a13 = block(1, slice(16, 32))
    a32 = block(2, slice(16, 32))
    v21 = cdot(adjoint(a12), p)
    v31 = cdot(adjoint(a13), p)
    s22 = a22 - cdot(v21, a12)
    s32 = a32 - cdot(v31, a12)
    s33 = a33 - cdot(v31, a13)
    q = hermitian_inverse(s22)
    v32 = cdot(s32, q)
    s33 = s33 - cdot(v32, adjoint(s32))
    r = hermitian_inverse(s33)
    t = steer_ref[...]
    y3 = cdot(t, r)
    y2 = -cdot(y3, v32)
    y1 = -cdot(y2, v21) - cdot(y3, v31)
    norm = lax.rsqrt(jnp.sum(t * y3, axis=1, keepdims=True))
    real = [(v[:, :64] * norm) for v in (y1, y3, y2)]
    imag = [(v[:, 64:] * -norm) for v in (y1, y3, y2)]
    rows = jnp.concatenate(
        [jnp.concatenate(real, axis=1), jnp.concatenate(imag, axis=1)], axis=0
    )
    zero = jnp.zeros((16, 64), F32)
    even = jnp.concatenate([rows, zero], axis=1)
    odd = jnp.concatenate([zero, rows], axis=1)
    return jnp.where(parity == 0, even, odd).astype(BF16)


def selection(bin_ref, block_ref, beam_ref, owner_ref, select, turn, back):
    s_iota = lax.broadcasted_iota(jnp.int32, (256, 128), 0)
    named = (s_iota // 2 == owner_ref[...]).astype(F32)
    before = (
        lax.broadcasted_iota(jnp.int32, (128, 128), 0)
        < lax.broadcasted_iota(jnp.int32, (128, 128), 1)
    ).astype(F32)
    earlier = jnp.dot(named.astype(BF16), before.astype(BF16), preferred_element_type=F32)
    pick = jnp.where(earlier == (s_iota % 2).astype(F32), named, 0.0).astype(BF16)
    wanted = block_ref[...] * 256 + bin_ref[...] * 8 + beam_ref[...]
    t_iota = lax.broadcasted_iota(jnp.int32, (512, 128), 0)
    holds = (t_iota == wanted).astype(F32).astype(BF16)
    select[...] = lax.dot_general(pick, holds, NT, preferred_element_type=F32).astype(BF16)
    o = lax.broadcasted_iota(jnp.int32, (256, 256), 0)
    i = lax.broadcasted_iota(jnp.int32, (256, 256), 1)
    turn[...] = (i == o % 32 // 2 * 16 + o // 32 * 2 + o % 2).astype(F32).astype(BF16)
    back[...] = (i == o % 16 // 2 * 32 + o // 16 * 2 + o % 2).astype(F32).astype(BF16)


def kernel(
    raw_ref, rep_in, dft_in, steer_in, bin_in, block_in, beam_in, owner_in,
    out_ref,
    raw, pkl, pkr, hl, hr, ur, ui, tza, tz, s, pks, sr, p, r1, a1, rp, rm, a2, r3, gath, wall, table,
    select, turn, back, slots, d1, mid, d2,
    rep_ref, dft_ref, steer_ref, bin_ref, block_ref, beam_ref, owner_ref,
    ls, ms, hs, ht, s1, t1, s2, t2, s3, t3, s4, t4, s5, t5, s6, t6, s7, t7, s8, t8, s9, t9,
):
    me = lax.axis_index("range")
    core = me % 2
    y = me // 2 % 4
    x = me // 8 % 4
    z = me // 32
    zx = me // 8
    yc = me % 8
    bin_ = 2 * (4 * z + x + z % 2 * (3 - 2 * x)) + y % 2
    member = y // 2 * 2 + core
    sib = me + 1 - 2 * core
    sa = 32 - 24 * core
    sb = 8 + 24 * core
    a = me // sa % 4
    b = me // sb % 4
    left = (me + 127) % 128
    right = (me + 1) % 128

    def along(stride, coord, j):
        return me + ((coord + j) % 4 - coord) * stride

    near = []
    for delta in (1, -1, 0):
        for j in range(4):
            if delta or j:
                near.append((delta, j, at_home((bin_ + delta + 32) % 32, (member + j) % 4)))
    bins = [(bin_ + j) % 32 for j in sorted(range(1, 32), key=lambda j: abs(j - 16))]
    planes = [(z + j // 4) % 4 * 4 + (x + j % 4) % 4 for j in FAR]
    froms = [(z + 4 - j // 4) % 4 * 4 + (x + 4 - j % 4) % 4 for j in FAR]
    posts = [(yc + j) % 8 for j in POSTS]
    sheet = [
        ((b + j // 4) % 4, (y + j % 4) % 4)
        for j in FAR
    ]
    spots = [me + (q - b) * sb + (r - y) * 2 for q, r in sheet]
    partners = [left, right, sib, along(sa, a, 1), along(sa, a, 3)] + spots
    small = [
        pltpu.make_async_copy(src, dst, ms.at[n])
        for n, (src, dst) in enumerate(
            [
                (rep_in, rep_ref), (dft_in, dft_ref), (steer_in, steer_ref), (bin_in, bin_ref),
                (block_in, block_ref), (beam_in, beam_ref), (owner_in, owner_ref),
            ]
        )
    ]
    small[0].start()
    loads = []
    for i in range(4):
        at = pl.ds(16 * i, 16)
        copy = pltpu.make_async_copy(raw_ref.at[:, at], raw.at[:, at], ls.at[i])
        copy.start()
        loads.append(copy)
    for copy in small[1:]:
        copy.start()
    barrier = pltpu.get_barrier_semaphore()
    for to in partners:
        pl.semaphore_signal(barrier, inc=1, device_id=(to,), device_id_type=MESH)
    for i in range(4):
        at = pl.ds(16 * i, 16)
        loads[i].wait()
        pkl[at] = jnp.concatenate([raw[0, at, :, 0:64], raw[1, at, :, 0:64]], axis=-1)
        pkr[at] = jnp.concatenate([raw[0, at, :, 192:256], raw[1, at, :, 192:256]], axis=-1)
        window_inner(at, raw, ur, ui)
    pl.semaphore_wait(barrier, len(partners))
    copies = []

    def finish():
        for copy in copies:
            copy.wait_send()


    def to_left(i):
        at = pl.ds(16 * i, 16)
        return remote(pkl.at[at], hr.at[at], hs.at[0, i], ht.at[0, i], left)

    for i in range(4):
        at = pl.ds(16 * i, 16)
        copy = remote(pkr.at[at], hl.at[at], hs.at[1, i], ht.at[1, i], right)
        copy.start()
        copies.append(copy)

        @pl.when(me > 0)
        def _():
            to_left(i).start()

    @pl.when(me == 127)
    def _():
        hr[...] = jnp.zeros_like(hr)

    small[0].wait()
    build_toeplitz(rep_ref, jnp.where(me > 0, 1.0, 0.0).astype(F32), tza, tz)
    for copy in small[1:]:
        copy.wait()
    selection(bin_ref, block_ref, beam_ref, owner_ref, select, turn, back)
    for i in range(4):
        copies[i].wait_recv()

        @pl.when(me < 127)
        def _():
            to_left(i).wait_recv()

        window_edges(pl.ds(16 * i, 16), raw, hl, hr, ur, ui)
        spectra_part(i, ur, ui, dft_ref, s, tza, tz)

    @pl.when(me > 0)
    def _():
        for i in range(4):
            to_left(i).wait_send()

    s[0:2] = s[32:34]
    s[34] = s[2]
    pks[...] = join(s[2:34, :, 0:64], s[2:34, :, 128:192])
    share = remote(pks, sr.at[pl.ds(2, 32)], s9, t9, left)

    order = (2, 1, 3, 0)
    oa = me // sb % 4
    for j in order:
        q = (oa + j) % 4
        for u in range(4):
            cross_products(core * q + (1 - core) * u, core * u + (1 - core) * q, s, p)
        at = pl.ds(q * 8, 8)
        copy = remote(p.at[1 - core, at], r1.at[at], s1.at[j], t1.at[j], sib)
        copy.start()
        copies.append(copy)

    rings = []

    def ring(src, dst, n, to):
        copy = remote(src, dst, s2.at[n], t2.at[n], to)
        copy.start()
        copies.append(copy)
        rings.append(copy)

    ahead, behind = along(sa, a, 1), along(sa, a, 3)
    base = {j: (a + j) % 4 * 8 for j in range(4)}
    for j in order:
        at = pl.ds(base[j], 8)
        remote(p.at[core, at], r1.at[at], s1.at[j], t1.at[j], sib).wait_recv()
        a1[at] = p[core, at] + r1[at]
        if j == 2:
            ring(a1.at[pl.ds(base[2], 4)], rp.at[0], 0, ahead)
            ring(a1.at[pl.ds(base[2] + 4, 4)], rm.at[0], 1, behind)
        elif j == 1:
            ring(a1.at[pl.ds(base[1] + 4, 4)], rp.at[1], 2, ahead)
        elif j == 3:
            ring(a1.at[pl.ds(base[3], 4)], rm.at[1], 3, behind)
    rings[0].wait_recv()
    at = pl.ds(base[1], 4)
    a1[at] = a1[at] + rp[0]
    ring(a1.at[at], rp.at[2], 4, ahead)
    rings[1].wait_recv()
    at = pl.ds(base[3] + 4, 4)
    a1[at] = a1[at] + rm[0]
    ring(a1.at[at], rm.at[2], 5, behind)
    for n in (2, 3):
        rings[n].wait_recv()
    at = pl.ds(base[0] + 4, 4)
    a2[4:8] = a1[at] + rp[1]
    at = pl.ds(base[0], 4)
    a2[0:4] = a1[at] + rm[1]
    rings[4].wait_recv()
    a2[0:4] = a2[0:4] + rp[2]
    rings[5].wait_recv()
    a2[4:8] = a2[4:8] + rm[2]

    parts = ((pl.ds(32, 8), 32, 8, s3, t3), (pl.ds(0, 32), 0, 32, s4, t4))
    for rows, start, size, sends, lands in parts:
        for n, (q, r) in enumerate(sheet):
            at = pl.ds(pl.multiple_of(r // 2 * 40 + start, 8), size)
            copy = remote(
                a2.at[q * 2 + r % 2, at], r3.at[n, rows], sends.at[n], lands.at[n], spots[n]
            )
            copy.start()
            copies.append(copy)
    needs = {-1: pl.ds(0, 40), 0: pl.ds(16, 24), 1: pl.ds(32, 8)}

    def pass_on(deltas):
        for n, (delta, j, to) in enumerate(near):
            if delta in deltas:
                part = gath.at[1, member, needs[delta]]
                there = gath.at[1 - delta, member, needs[delta]]
                copy = remote(part, there, s5.at[n], t5.at[1 - delta, member], to)
                copy.start()
                copies.append(copy)

    for rows, start, size, sends, lands in parts:
        for n in range(15):
            remote(r3.at[n, rows], r3.at[n, rows], sends.at[n], lands.at[n], sib).wait_recv()
        at = pl.ds(pl.multiple_of(y // 2 * 40 + start, 8), size)
        terms = [a2[b * 2 + y % 2, at]] + [r3[n, rows] for n in range(15)]
        while len(terms) > 1:
            terms = [u + v for u, v in zip(terms[::2], terms[1::2])]
        gath[1, member, rows] = terms[0]
        pass_on((1,) if start else (-1, 0))

    def arrived(deltas):
        for delta, j, _ in near:
            if delta in deltas:
                part = gath.at[1 - delta, (member + j) % 4, needs[delta]]
                remote(part, part, s5.at[0], t5.at[1 - delta, (member + j) % 4], sib).wait_recv()

    arrived((1,))

    def others():
        arrived((-1, 0))
        share.start()
        copies.append(share)

    wall[bin_] = solve(gath, steer_ref, bin_ % 2, others)
    share.wait_recv()
    sr[0:2] = sr[32:34]
    sr[34] = sr[2]
    for n, to in enumerate(bins):
        copy = remote(wall.at[bin_], wall.at[bin_], s6.at[n], t6.at[bin_], at_home(to, member))
        copy.start()
        copies.append(copy)

    for n in (0, 1, 15, 2, 14, 3, 13, 4, 12, 5, 11, 6, 10, 7, 9, 8):
        duo = (bin_ // 2 + 16 - n) % 16
        first = duo * 2
        waits = (first, first + 1) if n else (bin_ + 1 - 2 * (bin_ % 2),)
        for q in waits:
            remote(wall.at[q], wall.at[q], s6.at[0], t6.at[q], sib).wait_recv()
        beam_pair(first, wall, s, sr, table)

    slots[...] = (
        jnp.dot(select[...], table[...], preferred_element_type=F32)
        .astype(BF16)
        .reshape(16, 16, 256)
    )
    for j, q in enumerate(planes):
        copy = remote(slots.at[q], d1.at[zx], s7.at[j], t7.at[j], q * 8 + yc)
        copy.start()
        copies.append(copy)
    d1[zx] = slots[zx]
    for j, q in enumerate(froms):
        remote(slots.at[q], d1.at[q], s7.at[j], t7.at[j], sib).wait_recv()
    mid[...] = (
        jnp.dot(turn[...], d1[...].reshape(256, 256), preferred_element_type=F32)
        .astype(BF16)
        .reshape(8, 32, 256)
    )
    for j, q in enumerate(posts):
        copy = remote(mid.at[q], d2.at[yc], s8.at[j], t8.at[j], zx * 8 + q)
        copy.start()
        copies.append(copy)
    d2[yc] = mid[yc]
    for j, step in enumerate(POSTS):
        q = (yc + 8 - step) % 8
        remote(mid.at[q], d2.at[q], s8.at[j], t8.at[j], sib).wait_recv()
    rows = jnp.dot(back[...], d2[...].reshape(256, 256), preferred_element_type=F32)
    out_ref[...] = rows.astype(BF16)
    finish()


def program(raw, replica, det_bin, det_block, det_beam, owner):
    dma = pltpu.SemaphoreType.DMA
    vm = pltpu.VMEM
    rows = (1, 128)
    return pl.pallas_call(
        kernel,
        out_shape=jax.ShapeDtypeStruct((256, 256), BF16),
        in_specs=[HBM] * 8,
        out_specs=VMEM,
        scratch_shapes=[
            vm((2, 64, 32, 256), BF16),
            vm((64, 32, 128), BF16),
            vm((64, 32, 128), BF16),
            vm((64, 32, 128), BF16),
            vm((64, 32, 128), BF16),
            vm((64, 32, 384), BF16),
            vm((64, 32, 384), BF16),
            vm((512, 256), BF16),
            vm((512, 256), BF16),
            vm((35, 64, 512), BF16),
            vm((32, 64, 128), BF16),
            vm((35, 64, 128), BF16),
            vm((2, 32, 80, 128), F32),
            vm((32, 80, 128), F32),
            vm((32, 80, 128), F32),
            vm((3, 4, 80, 128), F32),
            vm((3, 4, 80, 128), F32),
            vm((8, 80, 128), F32),
            vm((15, 40, 128), F32),
            vm((3, 4, 40, 128), F32),
            vm((32, 16, 256), BF16),
            vm((512, 256), BF16),
            vm((256, 512), BF16),
            vm((256, 256), BF16),
            vm((256, 256), BF16),
            vm((16, 16, 256), BF16),
            vm((16, 16, 256), BF16),
            vm((8, 32, 256), BF16),
            vm((8, 32, 256), BF16),
            vm((2, 128), BF16),
            vm((512, 512), BF16),
            vm((8, 128), F32),
            vm(rows, jnp.int32), vm(rows, jnp.int32), vm(rows, jnp.int32), vm(rows, jnp.int32),
            dma((4,)), dma((7,)), dma((2, 4)), dma((2, 4)),
            dma((4,)), dma((4,)), dma((6,)), dma((6,)), dma((15,)), dma((15,)),
            dma((15,)), dma((15,)), dma((11,)), dma((3, 4)), dma((31,)), dma((32,)),
            dma((15,)), dma((15,)), dma((7,)), dma((7,)), dma(()), dma(()),
        ],
        compiler_params=pltpu.CompilerParams(
            collective_id=0, has_side_effects=True, vmem_limit_bytes=LIMIT
        ),
        name="stap",
    )(
        raw, replica, jnp.asarray(dft_matrix()), jnp.asarray(steer_rows()),
        det_bin, det_block, det_beam, owner,
    )


def on_device(raw, replica, det_bin, det_block, det_beam, det_owner):
    rows = [v.reshape(1, 128) for v in (det_bin, det_block, det_beam, det_owner)]
    return program(raw, replica, *rows).astype(F32)


def solution(mesh):
    in_specs = (
        P(None, None, None, "range"),
        P(),
        P("range"),
        P("range"),
        P("range"),
        P("range", None),
    )
    return jax.shard_map(
        on_device,
        mesh=mesh,
        in_specs=in_specs,
        out_specs=P("range", None),
        check_vma=False,
    )
```

```python
import math

import jax
import jax.numpy as jnp
import numpy as np
from jax import lax
from jax.experimental import pallas as pl
from jax.experimental.pallas import tpu as pltpu
from jax.sharding import PartitionSpec as P

C = 64
PULSES = 32
TAPS = 128
BEAMS = 8
F32 = jnp.float32
BF16 = jnp.bfloat16
MESH = pl.DeviceIdType.MESH
VMEM = pl.BlockSpec(memory_space=pltpu.VMEM)
HBM = pl.BlockSpec(memory_space=pltpu.HBM)
NT = (((1,), (1,)), ((), ()))
LIMIT = 63 * 1024 * 1024
FAR = (10, 9, 11, 6, 14, 2, 8, 5, 7, 13, 15, 1, 3, 4, 12)
POSTS = (4, 5, 3, 2, 6, 7, 1)


def dft_matrix():
    index = np.arange(PULSES)
    angle = 2.0 * math.pi / PULSES * (index[:, None] * index[None, :] % PULSES)
    scale = PULSES**-0.5
    real = np.cos(angle) * scale
    imag = -np.sin(angle) * scale
    eye = np.eye(8)
    kr = np.einsum("pd,ab->dabp", real, eye).reshape(256, 256)
    ki = np.einsum("pd,ab->dabp", imag, eye).reshape(256, 256)
    full = np.concatenate([np.concatenate([kr, -ki], 1), np.concatenate([ki, kr], 1)], 0)
    return full.astype(jnp.bfloat16)


def steer_rows():
    sines = -0.8 + 1.6 * np.arange(BEAMS, dtype=np.float32) / np.float32(BEAMS - 1)
    angle = (math.pi * np.arange(C, dtype=np.float32)[None, :] * sines[:, None]).astype(np.float32)
    return np.concatenate([np.cos(angle), -np.sin(angle)], 1).astype(np.float32)


def remote(src, dst, send, recv, to):
    return pltpu.make_async_remote_copy(
        src_ref=src, dst_ref=dst, send_sem=send, recv_sem=recv, device_id=(to,), device_id_type=MESH
    )


def build_toeplitz(rep_ref, keep, tza, tz):
    def band(v):
        wide = jnp.concatenate(
            [jnp.broadcast_to(v, (TAPS, TAPS)), jnp.zeros((TAPS, TAPS), F32)], axis=1
        )
        return pltpu.roll(wide, 0, 1, stride=1, stride_axis=0).T

    rep = rep_ref[...].astype(F32)
    tr = band(rep[0:1])
    ti = band(rep[1:2])
    full = jnp.concatenate(
        [jnp.concatenate([tr, -ti], axis=1), jnp.concatenate([ti, tr], axis=1)], axis=0
    )
    tz[...] = full.astype(BF16)
    row = lax.broadcasted_iota(jnp.int32, (512, 256), 0) % 256
    lane = lax.broadcasted_iota(jnp.int32, (512, 256), 1) % 128
    tza[...] = jnp.where((row >= 64) & (lane < 64), full * keep, full).astype(BF16)


def join(*parts):
    return jnp.concatenate(parts, axis=-1)


def window_inner(at, raw, ur, ui):
    for n, u in enumerate((ur, ui)):
        u[at, :, 128:256] = join(raw[n, at, :, 64:128], raw[n, at, :, 128:192])


def window_edges(at, raw, hl, hr, ur, ui):
    for n, u in enumerate((ur, ui)):
        lanes = slice(64 * n, 64 * n + 64)
        u[at, :, 0:128] = join(hl[at, :, lanes], raw[n, at, :, 0:64])
        u[at, :, 256:384] = join(raw[n, at, :, 192:256], hr[at, :, lanes])


def spectra_part(i, ur, ui, dft_ref, s, tza, tz):
    first = 16 * i
    for b in range(2):
        ys = []
        for n in range(2):
            at = pl.ds(first + 8 * n, 8)
            gates = slice(128 * b, 128 * b + 256)
            window = join(ur[at, :, gates].reshape(256, 256), ui[at, :, gates].reshape(256, 256))
            band = tz[...] if b else tza[...]
            ys.append(jnp.dot(window, band, preferred_element_type=F32).astype(BF16))
        ya, yb = ys
        y = jnp.concatenate(
            [join(ya[:, :128], yb[:, :128]), join(ya[:, 128:], yb[:, 128:])], axis=0
        )
        out = jnp.dot(dft_ref[...], y, preferred_element_type=F32)
        for p in range(2):
            h = out[256 * p : 256 * p + 256]
            v = jnp.concatenate(
                [h[:, :128].reshape(32, 8, 128), h[:, 128:].reshape(32, 8, 128)], axis=1
            )
            lanes = 256 * b + 128 * p
            s[2:34, first : first + 16, lanes : lanes + 128] = v.astype(BF16)


def snake(k):
    z = k // 4
    x = k % 4
    return z, x + z % 2 * (3 - 2 * x)


def home(q):
    z, x = snake(q // 2)
    return z * 32 + x * 8 + q % 2 * 2


def at_home(q, member):
    return home(q) + member // 2 * 4 + member % 2


def beam_pair(first, wall, s, sr, table):
    lhs = wall[pl.ds(first, 2)].reshape(32, 256)
    rhs = join(
        s[pl.ds(first + 1, 4)].reshape(256, 512), sr[pl.ds(first + 1, 4)].reshape(256, 128)
    )
    prod = jnp.dot(lhs, rhs, preferred_element_type=F32)
    top = jnp.concatenate([prod[0:8], prod[16:24]], axis=0)
    low = jnp.concatenate([prod[8:16], prod[24:32]], axis=0)
    half = lax.broadcasted_iota(jnp.int32, (16, 128), 1) < 64

    def flip(v):
        return pltpu.roll(v, 64, 1)

    parts = []
    for at in (0, 256):
        parts.append(flip(top[:, at : at + 128] + low[:, at + 128 : at + 256]))
        parts.append(flip(top[:, at + 128 : at + 256] - low[:, at : at + 128]))
    turn = flip(low[:, 512:])
    last = top[:, 512:] + jnp.where(half, turn, -turn)
    lanes = [
        jnp.where(half, parts[0], parts[2]),
        jnp.where(half, parts[1], parts[3]),
        jnp.where(half, parts[2], flip(last)),
        jnp.where(half, parts[3], last),
    ]
    for i in range(2):
        rows = pl.ds(pl.multiple_of(256 * i + first * 8, 16), 16)
        table[rows] = join(*lanes[2 * i : 2 * i + 2]).astype(BF16)


def store_products(p, places, two, one, zero):
    lane = lax.broadcasted_iota(jnp.int32, (32, 128), 1)
    row = lax.broadcasted_iota(jnp.int32, (32, 128), 0)
    swapped = pltpu.roll(zero, 64, 1)
    top = jnp.where(row >= lane, zero[:32], swapped[:32])
    bottom = jnp.where(row + 32 >= lane - 64, swapped[32:], zero[32:])
    packed = jnp.where(lane < 64, top, bottom)
    for h in range(2):
        pos = places[h]
        for q in range(2):
            a = 32 * h + 16 * q
            p[h, pos, 40 * q : 40 * q + 16] = two[a : a + 16]
            p[h, pos, 40 * q + 16 : 40 * q + 32] = one[a : a + 16]
            p[h, pos, 40 * q + 32 : 40 * q + 40] = packed[a // 2 : a // 2 + 8]


def cross_products(z, x, s, p):
    f = 2 * (4 * z + x + z % 2 * (3 - 2 * x))
    lhs = s[pl.ds(f, 4)].reshape(256, 512)
    rhs = []
    for n in range(2):
        v = s[f + 2 + n]
        rhs += [v, join(-v[:, 128:256], v[:, :128], -v[:, 384:], v[:, 256:384])]
    prod = lax.dot_general(lhs, jnp.concatenate(rhs, axis=0), NT, preferred_element_type=F32)
    first, second = (z * 8 + x * 2, x * 8 + z * 2), (z * 8 + x * 2 + 1, x * 8 + z * 2 + 1)
    store_products(p, first, prod[:64, :128], prod[64:128, :128], prod[128:192, :128])
    store_products(p, second, prod[64:128, 128:], prod[128:192, 128:], prod[192:, 128:])


def times_i(m):
    return jnp.concatenate([-m[:, 64:], m[:, :64]], axis=1)


def cdot(x, y):
    return jnp.dot(
        x, jnp.concatenate([y, times_i(y)], axis=0),
        preferred_element_type=F32, precision=lax.Precision.HIGHEST,
    )


def adjoint(m):
    t = m.T
    return jnp.concatenate([t[:64], -t[64:]], axis=1)


def lane_of(v, k):
    return jnp.broadcast_to(v[:, k : k + 1], (8, 128))


def row_of(v, r):
    return jnp.broadcast_to(v[r : r + 1], (8, 128))


def cmul(x, y):
    return (x[0] * y[0] - x[1] * y[1], x[0] * y[1] + x[1] * y[0])


def cmulc(x, y):
    return (x[0] * y[0] + x[1] * y[1], x[1] * y[0] - x[0] * y[1])


def cadd(x, y):
    return (x[0] + y[0], x[1] + y[1])


def csub(x, y):
    return (x[0] - y[0], x[1] - y[1])


def cscale(x, c):
    return (x * c[0], x * c[1])


def conj(x):
    return (x[0], -x[1])


def size2(x):
    return x[0] * x[0] + x[1] * x[1]


def rdot(x, y):
    return x[0] * y[0] + x[1] * y[1]


def cm(c, row):
    v, w = row
    return (c[0] * v + c[1] * w, c[0] * w - c[1] * v)


def hermitian_inverse(m):
    lane = lax.broadcasted_iota(jnp.int32, (8, 128), 1)
    sub = lax.broadcasted_iota(jnp.int32, (8, 128), 0)
    ms = [m[8 * t : 8 * t + 8] for t in range(8)]
    for k in range(0, 64, 4):
        t0, r0 = divmod(k, 8)
        w = ms[t0]
        wi = pltpu.roll(w, 64, 1)
        wi = jnp.where(lane < 64, -wi, wi)
        cr = [[lane_of(v, k + j) for v in ms] for j in range(4)]
        ci = [[lane_of(v, 64 + k + j) for v in ms] for j in range(4)]

        def entry(i, j):
            return (row_of(cr[j][t0], r0 + i), row_of(ci[j][t0], r0 + i))

        a, d, b = entry(0, 0)[0], entry(1, 1)[0], entry(0, 1)
        p, s, q = entry(2, 2)[0], entry(3, 3)[0], entry(2, 3)
        bb = [[entry(0, 2), entry(0, 3)], [entry(1, 2), entry(1, 3)]]
        det = 1.0 / (a * d - size2(b))
        ia, id_, ib = d * det, a * det, cscale(-det, b)
        ww = [
            [cadd(cscale(ia, bb[0][j]), cmul(ib, bb[1][j])) for j in range(2)],
            [cadd(cmul(conj(ib), bb[0][j]), cscale(id_, bb[1][j])) for j in range(2)],
        ]
        s00 = p - (rdot(bb[0][0], ww[0][0]) + rdot(bb[1][0], ww[1][0]))
        s11 = s - (rdot(bb[0][1], ww[0][1]) + rdot(bb[1][1], ww[1][1]))
        s01 = csub(q, cadd(cmulc(ww[0][1], bb[0][0]), cmulc(ww[1][1], bb[1][0])))
        dets = 1.0 / (s00 * s11 - size2(s01))
        j00, j11, j01 = s11 * dets, s00 * dets, cscale(-dets, s01)
        hit = ((lane >= k) & (lane < k + 4)) | ((lane >= 64 + k) & (lane < 68 + k))
        rows = []
        for j in range(4):
            real = jnp.where(hit, jnp.where(lane == k + j, 1.0, 0.0), row_of(w, r0 + j))
            imag = jnp.where(hit, jnp.where(lane == 64 + k + j, 1.0, 0.0), row_of(wi, r0 + j))
            rows.append((real, imag))
        t2 = csub(rows[2], cadd(cm(conj(ww[0][0]), rows[0]), cm(conj(ww[1][0]), rows[1])))
        t3 = csub(rows[3], cadd(cm(conj(ww[0][1]), rows[0]), cm(conj(ww[1][1]), rows[1])))
        x2 = cadd(cscale(j00, t2), cm(j01, t3))
        x3 = cadd(cscale(j11, t3), cm(conj(j01), t2))
        u0 = cadd(cscale(ia, rows[0]), cm(ib, rows[1]))
        u1 = cadd(cscale(id_, rows[1]), cm(conj(ib), rows[0]))
        x0 = csub(u0, cadd(cm(ww[0][0], x2), cm(ww[0][1], x3)))
        x1 = csub(u1, cadd(cm(ww[1][0], x2), cm(ww[1][1], x3)))
        g = [x0, x1, x2, x3]
        for t in range(8):
            terms = [cr[j][t] * g[j][0] + ci[j][t] * g[j][1] for j in range(4)]
            mt = jnp.where(hit, 0.0, ms[t]) - ((terms[0] + terms[1]) + (terms[2] + terms[3]))
            if t == t0:
                for j in range(4):
                    mt = jnp.where(sub == r0 + j, g[j][0], mt)
            ms[t] = mt
    return jnp.concatenate(ms, axis=0)


def solve(g_ref, steer_ref, parity, others):
    scale = 1.0 / 32768.0
    order = (0, 2, 1, 3)
    r64 = lax.broadcasted_iota(jnp.int32, (64, 64), 0)
    c64 = lax.broadcasted_iota(jnp.int32, (64, 64), 1)

    def block(g, rows):
        return jnp.concatenate([g_ref[g, m, rows] for m in order], axis=0) * scale

    def diagonal(g):
        pk = block(g, slice(32, 40))
        k = jnp.concatenate([pk[:, :64], pk[:, 64:]], axis=0)
        kt = k.T
        real = jnp.where(r64 >= c64, k, kt)
        imag = jnp.where(r64 < c64, k, jnp.where(r64 == c64, 0.0, -kt))
        return jnp.concatenate([real, imag], axis=1)

    p = hermitian_inverse(diagonal(0))
    others()
    a33 = diagonal(1)
    a22 = diagonal(2)
    a12 = block(2, slice(0, 16))
    a13 = block(1, slice(16, 32))
    a32 = block(2, slice(16, 32))
    v21 = cdot(adjoint(a12), p)
    v31 = cdot(adjoint(a13), p)
    s22 = a22 - cdot(v21, a12)
    s32 = a32 - cdot(v31, a12)
    s33 = a33 - cdot(v31, a13)
    q = hermitian_inverse(s22)
    v32 = cdot(s32, q)
    s33 = s33 - cdot(v32, adjoint(s32))
    r = hermitian_inverse(s33)
    t = steer_ref[...]
    y3 = cdot(t, r)
    y2 = -cdot(y3, v32)
    y1 = -cdot(y2, v21) - cdot(y3, v31)
    norm = lax.rsqrt(jnp.sum(t * y3, axis=1, keepdims=True))
    real = [(v[:, :64] * norm) for v in (y1, y3, y2)]
    imag = [(v[:, 64:] * -norm) for v in (y1, y3, y2)]
    rows = jnp.concatenate(
        [jnp.concatenate(real, axis=1), jnp.concatenate(imag, axis=1)], axis=0
    )
    zero = jnp.zeros((16, 64), F32)
    even = jnp.concatenate([rows, zero], axis=1)
    odd = jnp.concatenate([zero, rows], axis=1)
    return jnp.where(parity == 0, even, odd).astype(BF16)


def selection(bin_ref, block_ref, beam_ref, owner_ref, select, turn, back):
    s_iota = lax.broadcasted_iota(jnp.int32, (256, 128), 0)
    named = (s_iota // 2 == owner_ref[...]).astype(F32)
    before = (
        lax.broadcasted_iota(jnp.int32, (128, 128), 0)
        < lax.broadcasted_iota(jnp.int32, (128, 128), 1)
    ).astype(F32)
    earlier = jnp.dot(named.astype(BF16), before.astype(BF16), preferred_element_type=F32)
    pick = jnp.where(earlier == (s_iota % 2).astype(F32), named, 0.0).astype(BF16)
    wanted = block_ref[...] * 256 + bin_ref[...] * 8 + beam_ref[...]
    t_iota = lax.broadcasted_iota(jnp.int32, (512, 128), 0)
    holds = (t_iota == wanted).astype(F32).astype(BF16)
    select[...] = lax.dot_general(pick, holds, NT, preferred_element_type=F32).astype(BF16)
    o = lax.broadcasted_iota(jnp.int32, (256, 256), 0)
    i = lax.broadcasted_iota(jnp.int32, (256, 256), 1)
    turn[...] = (i == o % 32 // 2 * 16 + o // 32 * 2 + o % 2).astype(F32).astype(BF16)
    back[...] = (i == o % 16 // 2 * 32 + o // 16 * 2 + o % 2).astype(F32).astype(BF16)


def kernel(
    raw_ref, rep_in, dft_in, steer_in, bin_in, block_in, beam_in, owner_in,
    out_ref,
    raw, pkl, pkr, hl, hr, ur, ui, tza, tz, s, pks, sr, p, r1, a1, rp, rm, a2, r3, gath, wall, table,
    select, turn, back, slots, d1, mid, d2,
    rep_ref, dft_ref, steer_ref, bin_ref, block_ref, beam_ref, owner_ref,
    ls, ms, hs, ht, s1, t1, s2, t2, s3, t3, s4, t4, s5, t5, s6, t6, s7, t7, s8, t8, s9, t9,
):
    me = lax.axis_index("range")
    core = me % 2
    y = me // 2 % 4
    x = me // 8 % 4
    z = me // 32
    zx = me // 8
    yc = me % 8
    bin_ = 2 * (4 * z + x + z % 2 * (3 - 2 * x)) + y % 2
    member = y // 2 * 2 + core
    sib = me + 1 - 2 * core
    sa = 32 - 24 * core
    sb = 8 + 24 * core
    a = me // sa % 4
    b = me // sb % 4
    left = (me + 127) % 128
    right = (me + 1) % 128

    def along(stride, coord, j):
        return me + ((coord + j) % 4 - coord) * stride

    near = []
    for delta in (1, -1, 0):
        for j in range(4):
            if delta or j:
                near.append((delta, j, at_home((bin_ + delta + 32) % 32, (member + j) % 4)))
    bins = [(bin_ + j) % 32 for j in sorted(range(1, 32), key=lambda j: abs(j - 16))]
    planes = [(z + j // 4) % 4 * 4 + (x + j % 4) % 4 for j in FAR]
    froms = [(z + 4 - j // 4) % 4 * 4 + (x + 4 - j % 4) % 4 for j in FAR]
    posts = [(yc + j) % 8 for j in POSTS]
    sheet = [
        ((b + j // 4) % 4, (y + j % 4) % 4)
        for j in FAR
    ]
    spots = [me + (q - b) * sb + (r - y) * 2 for q, r in sheet]
    partners = [left, right, sib, along(sa, a, 1), along(sa, a, 3)] + spots
    small = [
        pltpu.make_async_copy(src, dst, ms.at[n])
        for n, (src, dst) in enumerate(
            [
                (rep_in, rep_ref), (dft_in, dft_ref), (steer_in, steer_ref), (bin_in, bin_ref),
                (block_in, block_ref), (beam_in, beam_ref), (owner_in, owner_ref),
            ]
        )
    ]
    small[0].start()
    loads = []
    for i in range(4):
        at = pl.ds(16 * i, 16)
        copy = pltpu.make_async_copy(raw_ref.at[:, at], raw.at[:, at], ls.at[i])
        copy.start()
        loads.append(copy)
    for copy in small[1:]:
        copy.start()
    barrier = pltpu.get_barrier_semaphore()
    for to in partners:
        pl.semaphore_signal(barrier, inc=1, device_id=(to,), device_id_type=MESH)
    for i in range(4):
        at = pl.ds(16 * i, 16)
        loads[i].wait()
        pkl[at] = jnp.concatenate([raw[0, at, :, 0:64], raw[1, at, :, 0:64]], axis=-1)
        pkr[at] = jnp.concatenate([raw[0, at, :, 192:256], raw[1, at, :, 192:256]], axis=-1)
        window_inner(at, raw, ur, ui)
    pl.semaphore_wait(barrier, len(partners))
    copies = []

    def finish():
        for copy in copies:
            copy.wait_send()


    def to_left(i):
        at = pl.ds(16 * i, 16)
        return remote(pkl.at[at], hr.at[at], hs.at[0, i], ht.at[0, i], left)

    for i in range(4):
        at = pl.ds(16 * i, 16)
        copy = remote(pkr.at[at], hl.at[at], hs.at[1, i], ht.at[1, i], right)
        copy.start()
        copies.append(copy)

        @pl.when(me > 0)
        def _():
            to_left(i).start()

    @pl.when(me == 127)
    def _():
        hr[...] = jnp.zeros_like(hr)

    small[0].wait()
    build_toeplitz(rep_ref, jnp.where(me > 0, 1.0, 0.0).astype(F32), tza, tz)
    for copy in small[1:]:
        copy.wait()
    selection(bin_ref, block_ref, beam_ref, owner_ref, select, turn, back)
    for i in range(4):
        copies[i].wait_recv()

        @pl.when(me < 127)
        def _():
            to_left(i).wait_recv()

        window_edges(pl.ds(16 * i, 16), raw, hl, hr, ur, ui)
        spectra_part(i, ur, ui, dft_ref, s, tza, tz)

    @pl.when(me > 0)
    def _():
        for i in range(4):
            to_left(i).wait_send()

    s[0:2] = s[32:34]
    s[34] = s[2]
    pks[...] = join(s[2:34, :, 0:64], s[2:34, :, 128:192])
    share = remote(pks, sr.at[pl.ds(2, 32)], s9, t9, left)

    order = (2, 1, 3, 0)
    oa = me // sb % 4
    for j in order:
        q = (oa + j) % 4
        for u in range(4):
            cross_products(core * q + (1 - core) * u, core * u + (1 - core) * q, s, p)
        at = pl.ds(q * 8, 8)
        copy = remote(p.at[1 - core, at], r1.at[at], s1.at[j], t1.at[j], sib)
        copy.start()
        copies.append(copy)

    rings = []

    def ring(src, dst, n, to):
        copy = remote(src, dst, s2.at[n], t2.at[n], to)
        copy.start()
        copies.append(copy)
        rings.append(copy)

    ahead, behind = along(sa, a, 1), along(sa, a, 3)
    base = {j: (a + j) % 4 * 8 for j in range(4)}
    for j in order:
        at = pl.ds(base[j], 8)
        remote(p.at[core, at], r1.at[at], s1.at[j], t1.at[j], sib).wait_recv()
        a1[at] = p[core, at] + r1[at]
        if j == 2:
            ring(a1.at[pl.ds(base[2], 4)], rp.at[0], 0, ahead)
            ring(a1.at[pl.ds(base[2] + 4, 4)], rm.at[0], 1, behind)
        elif j == 1:
            ring(a1.at[pl.ds(base[1] + 4, 4)], rp.at[1], 2, ahead)
        elif j == 3:
            ring(a1.at[pl.ds(base[3], 4)], rm.at[1], 3, behind)
    rings[0].wait_recv()
    at = pl.ds(base[1], 4)
    a1[at] = a1[at] + rp[0]
    ring(a1.at[at], rp.at[2], 4, ahead)
    rings[1].wait_recv()
    at = pl.ds(base[3] + 4, 4)
    a1[at] = a1[at] + rm[0]
    ring(a1.at[at], rm.at[2], 5, behind)
    for n in (2, 3):
        rings[n].wait_recv()
    at = pl.ds(base[0] + 4, 4)
    a2[4:8] = a1[at] + rp[1]
    at = pl.ds(base[0], 4)
    a2[0:4] = a1[at] + rm[1]
    rings[4].wait_recv()
    a2[0:4] = a2[0:4] + rp[2]
    rings[5].wait_recv()
    a2[4:8] = a2[4:8] + rm[2]

    parts = ((pl.ds(32, 8), 32, 8, s3, t3), (pl.ds(0, 32), 0, 32, s4, t4))
    for rows, start, size, sends, lands in parts:
        for n, (q, r) in enumerate(sheet):
            at = pl.ds(pl.multiple_of(r // 2 * 40 + start, 8), size)
            copy = remote(
                a2.at[q * 2 + r % 2, at], r3.at[n, rows], sends.at[n], lands.at[n], spots[n]
            )
            copy.start()
            copies.append(copy)
    needs = {-1: pl.ds(0, 40), 0: pl.ds(16, 24), 1: pl.ds(32, 8)}

    def pass_on(deltas):
        for n, (delta, j, to) in enumerate(near):
            if delta in deltas:
                part = gath.at[1, member, needs[delta]]
                there = gath.at[1 - delta, member, needs[delta]]
                copy = remote(part, there, s5.at[n], t5.at[1 - delta, member], to)
                copy.start()
                copies.append(copy)

    for rows, start, size, sends, lands in parts:
        for n in range(15):
            remote(r3.at[n, rows], r3.at[n, rows], sends.at[n], lands.at[n], sib).wait_recv()
        at = pl.ds(pl.multiple_of(y // 2 * 40 + start, 8), size)
        terms = [a2[b * 2 + y % 2, at]] + [r3[n, rows] for n in range(15)]
        while len(terms) > 1:
            terms = [u + v for u, v in zip(terms[::2], terms[1::2])]
        gath[1, member, rows] = terms[0]
        pass_on((1,) if start else (-1, 0))

    def arrived(deltas):
        for delta, j, _ in near:
            if delta in deltas:
                part = gath.at[1 - delta, (member + j) % 4, needs[delta]]
                remote(part, part, s5.at[0], t5.at[1 - delta, (member + j) % 4], sib).wait_recv()

    arrived((1,))

    def others():
        arrived((-1, 0))
        share.start()
        copies.append(share)

    wall[bin_] = solve(gath, steer_ref, bin_ % 2, others)
    for n, to in enumerate(bins):
        copy = remote(wall.at[bin_], wall.at[bin_], s6.at[n], t6.at[bin_], at_home(to, member))
        copy.start()
        copies.append(copy)

    share.wait_recv()
    sr[0:2] = sr[32:34]
    sr[34] = sr[2]
    for n in (0, 1, 15, 2, 14, 3, 13, 4, 12, 5, 11, 6, 10, 7, 9, 8):
        duo = (bin_ // 2 + 16 - n) % 16
        first = duo * 2
        waits = (first, first + 1) if n else (bin_ + 1 - 2 * (bin_ % 2),)
        for q in waits:
            remote(wall.at[q], wall.at[q], s6.at[0], t6.at[q], sib).wait_recv()
        beam_pair(first, wall, s, sr, table)

    slots[...] = (
        jnp.dot(select[...], table[...], preferred_element_type=F32)
        .astype(BF16)
        .reshape(16, 16, 256)
    )
    for j, q in enumerate(planes):
        copy = remote(slots.at[q], d1.at[zx], s7.at[j], t7.at[j], q * 8 + yc)
        copy.start()
        copies.append(copy)
    d1[zx] = slots[zx]
    for j, q in enumerate(froms):
        remote(slots.at[q], d1.at[q], s7.at[j], t7.at[j], sib).wait_recv()
    mid[...] = (
        jnp.dot(turn[...], d1[...].reshape(256, 256), preferred_element_type=F32)
        .astype(BF16)
        .reshape(8, 32, 256)
    )
    for j, q in enumerate(posts):
        copy = remote(mid.at[q], d2.at[yc], s8.at[j], t8.at[j], zx * 8 + q)
        copy.start()
        copies.append(copy)
    d2[yc] = mid[yc]
    for j, step in enumerate(POSTS):
        q = (yc + 8 - step) % 8
        remote(mid.at[q], d2.at[q], s8.at[j], t8.at[j], sib).wait_recv()
    rows = jnp.dot(back[...], d2[...].reshape(256, 256), preferred_element_type=F32)
    out_ref[...] = rows.astype(BF16)
    finish()


def program(raw, replica, det_bin, det_block, det_beam, owner):
    dma = pltpu.SemaphoreType.DMA
    vm = pltpu.VMEM
    rows = (1, 128)
    return pl.pallas_call(
        kernel,
        out_shape=jax.ShapeDtypeStruct((256, 256), BF16),
        in_specs=[HBM] * 8,
        out_specs=VMEM,
        scratch_shapes=[
            vm((2, 64, 32, 256), BF16),
            vm((64, 32, 128), BF16),
            vm((64, 32, 128), BF16),
            vm((64, 32, 128), BF16),
            vm((64, 32, 128), BF16),
            vm((64, 32, 384), BF16),
            vm((64, 32, 384), BF16),
            vm((512, 256), BF16),
            vm((512, 256), BF16),
            vm((35, 64, 512), BF16),
            vm((32, 64, 128), BF16),
            vm((35, 64, 128), BF16),
            vm((2, 32, 80, 128), F32),
            vm((32, 80, 128), F32),
            vm((32, 80, 128), F32),
            vm((3, 4, 80, 128), F32),
            vm((3, 4, 80, 128), F32),
            vm((8, 80, 128), F32),
            vm((15, 40, 128), F32),
            vm((3, 4, 40, 128), F32),
            vm((32, 16, 256), BF16),
            vm((512, 256), BF16),
            vm((256, 512), BF16),
            vm((256, 256), BF16),
            vm((256, 256), BF16),
            vm((16, 16, 256), BF16),
            vm((16, 16, 256), BF16),
            vm((8, 32, 256), BF16),
            vm((8, 32, 256), BF16),
            vm((2, 128), BF16),
            vm((512, 512), BF16),
            vm((8, 128), F32),
            vm(rows, jnp.int32), vm(rows, jnp.int32), vm(rows, jnp.int32), vm(rows, jnp.int32),
            dma((4,)), dma((7,)), dma((2, 4)), dma((2, 4)),
            dma((4,)), dma((4,)), dma((6,)), dma((6,)), dma((15,)), dma((15,)),
            dma((15,)), dma((15,)), dma((11,)), dma((3, 4)), dma((31,)), dma((32,)),
            dma((15,)), dma((15,)), dma((7,)), dma((7,)), dma(()), dma(()),
        ],
        compiler_params=pltpu.CompilerParams(
            collective_id=0, has_side_effects=True, vmem_limit_bytes=LIMIT
        ),
        name="stap",
    )(
        raw, replica, jnp.asarray(dft_matrix()), jnp.asarray(steer_rows()),
        det_bin, det_block, det_beam, owner,
    )


def on_device(raw, replica, det_bin, det_block, det_beam, det_owner):
    rows = [v.reshape(1, 128) for v in (det_bin, det_block, det_beam, det_owner)]
    return program(raw, replica, *rows).astype(F32)


def solution(mesh):
    in_specs = (
        P(None, None, None, "range"),
        P(),
        P("range"),
        P("range"),
        P("range"),
        P("range", None),
    )
    return jax.shard_map(
        on_device,
        mesh=mesh,
        in_specs=in_specs,
        out_specs=P("range", None),
        check_vma=False,
    )
```

```python
import math

import jax
import jax.numpy as jnp
import numpy as np
from jax import lax
from jax.experimental import pallas as pl
from jax.experimental.pallas import tpu as pltpu
from jax.sharding import PartitionSpec as P

C = 64
PULSES = 32
TAPS = 128
BEAMS = 8
F32 = jnp.float32
BF16 = jnp.bfloat16
MESH = pl.DeviceIdType.MESH
VMEM = pl.BlockSpec(memory_space=pltpu.VMEM)
HBM = pl.BlockSpec(memory_space=pltpu.HBM)
NT = (((1,), (1,)), ((), ()))
LIMIT = 63 * 1024 * 1024
FAR = (10, 9, 11, 6, 14, 2, 8, 5, 7, 13, 15, 1, 3, 4, 12)
POSTS = (4, 5, 3, 2, 6, 7, 1)


def dft_matrix():
    index = np.arange(PULSES)
    angle = 2.0 * math.pi / PULSES * (index[:, None] * index[None, :] % PULSES)
    scale = PULSES**-0.5
    real = np.cos(angle) * scale
    imag = -np.sin(angle) * scale
    eye = np.eye(8)
    kr = np.einsum("pd,ab->dabp", real, eye).reshape(256, 256)
    ki = np.einsum("pd,ab->dabp", imag, eye).reshape(256, 256)
    full = np.concatenate([np.concatenate([kr, -ki], 1), np.concatenate([ki, kr], 1)], 0)
    return full.astype(jnp.bfloat16)


def steer_rows():
    sines = -0.8 + 1.6 * np.arange(BEAMS, dtype=np.float32) / np.float32(BEAMS - 1)
    angle = (math.pi * np.arange(C, dtype=np.float32)[None, :] * sines[:, None]).astype(np.float32)
    return np.concatenate([np.cos(angle), -np.sin(angle)], 1).astype(np.float32)


def remote(src, dst, send, recv, to):
    return pltpu.make_async_remote_copy(
        src_ref=src, dst_ref=dst, send_sem=send, recv_sem=recv, device_id=(to,), device_id_type=MESH
    )


def build_toeplitz(rep_ref, keep, tza, tz):
    def band(v):
        wide = jnp.concatenate(
            [jnp.broadcast_to(v, (TAPS, TAPS)), jnp.zeros((TAPS, TAPS), F32)], axis=1
        )
        return pltpu.roll(wide, 0, 1, stride=1, stride_axis=0).T

    rep = rep_ref[...].astype(F32)
    tr = band(rep[0:1])
    ti = band(rep[1:2])
    full = jnp.concatenate(
        [jnp.concatenate([tr, -ti], axis=1), jnp.concatenate([ti, tr], axis=1)], axis=0
    )
    tz[...] = full.astype(BF16)
    row = lax.broadcasted_iota(jnp.int32, (512, 256), 0) % 256
    lane = lax.broadcasted_iota(jnp.int32, (512, 256), 1) % 128
    tza[...] = jnp.where((row >= 64) & (lane < 64), full * keep, full).astype(BF16)


def join(*parts):
    return jnp.concatenate(parts, axis=-1)


def window_inner(at, raw, ur, ui):
    for n, u in enumerate((ur, ui)):
        u[at, :, 128:256] = join(raw[n, at, :, 64:128], raw[n, at, :, 128:192])


def window_edges(at, raw, hl, hr, ur, ui):
    for n, u in enumerate((ur, ui)):
        lanes = slice(64 * n, 64 * n + 64)
        u[at, :, 0:128] = join(hl[at, :, lanes], raw[n, at, :, 0:64])
        u[at, :, 256:384] = join(raw[n, at, :, 192:256], hr[at, :, lanes])


def spectra_part(i, ur, ui, dft_ref, s, tza, tz):
    first = 16 * i
    for b in range(2):
        ys = []
        for n in range(2):
            at = pl.ds(first + 8 * n, 8)
            gates = slice(128 * b, 128 * b + 256)
            window = join(ur[at, :, gates].reshape(256, 256), ui[at, :, gates].reshape(256, 256))
            band = tz[...] if b else tza[...]
            ys.append(jnp.dot(window, band, preferred_element_type=F32).astype(BF16))
        ya, yb = ys
        y = jnp.concatenate(
            [join(ya[:, :128], yb[:, :128]), join(ya[:, 128:], yb[:, 128:])], axis=0
        )
        out = jnp.dot(dft_ref[...], y, preferred_element_type=F32)
        for p in range(2):
            h = out[256 * p : 256 * p + 256]
            v = jnp.concatenate(
                [h[:, :128].reshape(32, 8, 128), h[:, 128:].reshape(32, 8, 128)], axis=1
            )
            lanes = 256 * b + 128 * p
            s[2:34, first : first + 16, lanes : lanes + 128] = v.astype(BF16)


def snake(k):
    z = k // 4
    x = k % 4
    return z, x + z % 2 * (3 - 2 * x)


def home(q):
    z, x = snake(q // 2)
    return z * 32 + x * 8 + q % 2 * 2


def at_home(q, member):
    return home(q) + member // 2 * 4 + member % 2


def beam_pair(first, wall, s, sr, table):
    lhs = wall[pl.ds(first, 2)].reshape(32, 256)
    rhs = join(
        s[pl.ds(first + 1, 4)].reshape(256, 512), sr[pl.ds(first + 1, 4)].reshape(256, 128)
    )
    prod = jnp.dot(lhs, rhs, preferred_element_type=F32)
    top = jnp.concatenate([prod[0:8], prod[16:24]], axis=0)
    low = jnp.concatenate([prod[8:16], prod[24:32]], axis=0)
    half = lax.broadcasted_iota(jnp.int32, (16, 128), 1) < 64

    def flip(v):
        return pltpu.roll(v, 64, 1)

    parts = []
    for at in (0, 256):
        parts.append(flip(top[:, at : at + 128] + low[:, at + 128 : at + 256]))
        parts.append(flip(top[:, at + 128 : at + 256] - low[:, at : at + 128]))
    turn = flip(low[:, 512:])
    last = top[:, 512:] + jnp.where(half, turn, -turn)
    lanes = [
        jnp.where(half, parts[0], parts[2]),
        jnp.where(half, parts[1], parts[3]),
        jnp.where(half, parts[2], flip(last)),
        jnp.where(half, parts[3], last),
    ]
    for i in range(2):
        rows = pl.ds(pl.multiple_of(256 * i + first * 8, 16), 16)
        table[rows] = join(*lanes[2 * i : 2 * i + 2]).astype(BF16)


def store_products(p, places, two, one, zero):
    lane = lax.broadcasted_iota(jnp.int32, (32, 128), 1)
    row = lax.broadcasted_iota(jnp.int32, (32, 128), 0)
    swapped = pltpu.roll(zero, 64, 1)
    top = jnp.where(row >= lane, zero[:32], swapped[:32])
    bottom = jnp.where(row + 32 >= lane - 64, swapped[32:], zero[32:])
    packed = jnp.where(lane < 64, top, bottom)
    for h in range(2):
        pos = places[h]
        for q in range(2):
            a = 32 * h + 16 * q
            p[h, pos, 40 * q : 40 * q + 16] = two[a : a + 16]
            p[h, pos, 40 * q + 16 : 40 * q + 32] = one[a : a + 16]
            p[h, pos, 40 * q + 32 : 40 * q + 40] = packed[a // 2 : a // 2 + 8]


def cross_products(z, x, s, p):
    f = 2 * (4 * z + x + z % 2 * (3 - 2 * x))
    lhs = s[pl.ds(f, 4)].reshape(256, 512)
    rhs = []
    for n in range(2):
        v = s[f + 2 + n]
        rhs += [v, join(-v[:, 128:256], v[:, :128], -v[:, 384:], v[:, 256:384])]
    prod = lax.dot_general(lhs, jnp.concatenate(rhs, axis=0), NT, preferred_element_type=F32)
    first, second = (z * 8 + x * 2, x * 8 + z * 2), (z * 8 + x * 2 + 1, x * 8 + z * 2 + 1)
    store_products(p, first, prod[:64, :128], prod[64:128, :128], prod[128:192, :128])
    store_products(p, second, prod[64:128, 128:], prod[128:192, 128:], prod[192:, 128:])


def times_i(m):
    return jnp.concatenate([-m[:, 64:], m[:, :64]], axis=1)


def cdot(x, y):
    return jnp.dot(
        x, jnp.concatenate([y, times_i(y)], axis=0),
        preferred_element_type=F32, precision=lax.Precision.HIGHEST,
    )


def adjoint(m):
    t = m.T
    return jnp.concatenate([t[:64], -t[64:]], axis=1)


def lane_of(v, k):
    return jnp.broadcast_to(v[:, k : k + 1], (8, 128))


def row_of(v, r):
    return jnp.broadcast_to(v[r : r + 1], (8, 128))


def cmul(x, y):
    return (x[0] * y[0] - x[1] * y[1], x[0] * y[1] + x[1] * y[0])


def cmulc(x, y):
    return (x[0] * y[0] + x[1] * y[1], x[1] * y[0] - x[0] * y[1])


def cadd(x, y):
    return (x[0] + y[0], x[1] + y[1])


def csub(x, y):
    return (x[0] - y[0], x[1] - y[1])


def cscale(x, c):
    return (x * c[0], x * c[1])


def conj(x):
    return (x[0], -x[1])


def size2(x):
    return x[0] * x[0] + x[1] * x[1]


def rdot(x, y):
    return x[0] * y[0] + x[1] * y[1]


def cm(c, row):
    v, w = row
    return (c[0] * v + c[1] * w, c[0] * w - c[1] * v)


def hermitian_inverse(m):
    lane = lax.broadcasted_iota(jnp.int32, (8, 128), 1)
    sub = lax.broadcasted_iota(jnp.int32, (8, 128), 0)
    ms = [m[8 * t : 8 * t + 8] for t in range(8)]
    for k in range(0, 64, 4):
        t0, r0 = divmod(k, 8)
        w = ms[t0]
        wi = pltpu.roll(w, 64, 1)
        wi = jnp.where(lane < 64, -wi, wi)
        cr = [[lane_of(v, k + j) for v in ms] for j in range(4)]
        ci = [[lane_of(v, 64 + k + j) for v in ms] for j in range(4)]

        def entry(i, j):
            return (row_of(cr[j][t0], r0 + i), row_of(ci[j][t0], r0 + i))

        a, d, b = entry(0, 0)[0], entry(1, 1)[0], entry(0, 1)
        p, s, q = entry(2, 2)[0], entry(3, 3)[0], entry(2, 3)
        bb = [[entry(0, 2), entry(0, 3)], [entry(1, 2), entry(1, 3)]]
        det = 1.0 / (a * d - size2(b))
        ia, id_, ib = d * det, a * det, cscale(-det, b)
        ww = [
            [cadd(cscale(ia, bb[0][j]), cmul(ib, bb[1][j])) for j in range(2)],
            [cadd(cmul(conj(ib), bb[0][j]), cscale(id_, bb[1][j])) for j in range(2)],
        ]
        s00 = p - (rdot(bb[0][0], ww[0][0]) + rdot(bb[1][0], ww[1][0]))
        s11 = s - (rdot(bb[0][1], ww[0][1]) + rdot(bb[1][1], ww[1][1]))
        s01 = csub(q, cadd(cmulc(ww[0][1], bb[0][0]), cmulc(ww[1][1], bb[1][0])))
        dets = 1.0 / (s00 * s11 - size2(s01))
        j00, j11, j01 = s11 * dets, s00 * dets, cscale(-dets, s01)
        hit = ((lane >= k) & (lane < k + 4)) | ((lane >= 64 + k) & (lane < 68 + k))
        rows = []
        for j in range(4):
            real = jnp.where(hit, jnp.where(lane == k + j, 1.0, 0.0), row_of(w, r0 + j))
            imag = jnp.where(hit, jnp.where(lane == 64 + k + j, 1.0, 0.0), row_of(wi, r0 + j))
            rows.append((real, imag))
        t2 = csub(rows[2], cadd(cm(conj(ww[0][0]), rows[0]), cm(conj(ww[1][0]), rows[1])))
        t3 = csub(rows[3], cadd(cm(conj(ww[0][1]), rows[0]), cm(conj(ww[1][1]), rows[1])))
        x2 = cadd(cscale(j00, t2), cm(j01, t3))
        x3 = cadd(cscale(j11, t3), cm(conj(j01), t2))
        u0 = cadd(cscale(ia, rows[0]), cm(ib, rows[1]))
        u1 = cadd(cscale(id_, rows[1]), cm(conj(ib), rows[0]))
        x0 = csub(u0, cadd(cm(ww[0][0], x2), cm(ww[0][1], x3)))
        x1 = csub(u1, cadd(cm(ww[1][0], x2), cm(ww[1][1], x3)))
        g = [x0, x1, x2, x3]
        for t in range(8):
            terms = [cr[j][t] * g[j][0] + ci[j][t] * g[j][1] for j in range(4)]
            mt = jnp.where(hit, 0.0, ms[t]) - ((terms[0] + terms[1]) + (terms[2] + terms[3]))
            if t == t0:
                for j in range(4):
                    mt = jnp.where(sub == r0 + j, g[j][0], mt)
            ms[t] = mt
    return jnp.concatenate(ms, axis=0)


def solve(g_ref, steer_ref, parity, others):
    scale = 1.0 / 32768.0
    order = (0, 2, 1, 3)
    r64 = lax.broadcasted_iota(jnp.int32, (64, 64), 0)
    c64 = lax.broadcasted_iota(jnp.int32, (64, 64), 1)

    def block(g, rows):
        return jnp.concatenate([g_ref[g, m, rows] for m in order], axis=0) * scale

    def diagonal(g):
        pk = block(g, slice(32, 40))
        k = jnp.concatenate([pk[:, :64], pk[:, 64:]], axis=0)
        kt = k.T
        real = jnp.where(r64 >= c64, k, kt)
        imag = jnp.where(r64 < c64, k, jnp.where(r64 == c64, 0.0, -kt))
        return jnp.concatenate([real, imag], axis=1)

    p = hermitian_inverse(diagonal(0))
    others()
    a33 = diagonal(1)
    a22 = diagonal(2)
    a12 = block(2, slice(0, 16))
    a13 = block(1, slice(16, 32))
    a32 = block(2, slice(16, 32))
    v21 = cdot(adjoint(a12), p)
    v31 = cdot(adjoint(a13), p)
    s22 = a22 - cdot(v21, a12)
    s32 = a32 - cdot(v31, a12)
    s33 = a33 - cdot(v31, a13)
    q = hermitian_inverse(s22)
    v32 = cdot(s32, q)
    s33 = s33 - cdot(v32, adjoint(s32))
    r = hermitian_inverse(s33)
    t = steer_ref[...]
    y3 = cdot(t, r)
    y2 = -cdot(y3, v32)
    y1 = -cdot(y2, v21) - cdot(y3, v31)
    norm = lax.rsqrt(jnp.sum(t * y3, axis=1, keepdims=True))
    real = [(v[:, :64] * norm) for v in (y1, y3, y2)]
    imag = [(v[:, 64:] * -norm) for v in (y1, y3, y2)]
    rows = jnp.concatenate(
        [jnp.concatenate(real, axis=1), jnp.concatenate(imag, axis=1)], axis=0
    )
    zero = jnp.zeros((16, 64), F32)
    even = jnp.concatenate([rows, zero], axis=1)
    odd = jnp.concatenate([zero, rows], axis=1)
    return jnp.where(parity == 0, even, odd).astype(BF16)


def selection(bin_ref, block_ref, beam_ref, owner_ref, select, turn, back):
    s_iota = lax.broadcasted_iota(jnp.int32, (256, 128), 0)
    named = (s_iota // 2 == owner_ref[...]).astype(F32)
    before = (
        lax.broadcasted_iota(jnp.int32, (128, 128), 0)
        < lax.broadcasted_iota(jnp.int32, (128, 128), 1)
    ).astype(F32)
    earlier = jnp.dot(named.astype(BF16), before.astype(BF16), preferred_element_type=F32)
    pick = jnp.where(earlier == (s_iota % 2).astype(F32), named, 0.0).astype(BF16)
    wanted = block_ref[...] * 256 + bin_ref[...] * 8 + beam_ref[...]
    t_iota = lax.broadcasted_iota(jnp.int32, (512, 128), 0)
    holds = (t_iota == wanted).astype(F32).astype(BF16)
    select[...] = lax.dot_general(pick, holds, NT, preferred_element_type=F32).astype(BF16)
    o = lax.broadcasted_iota(jnp.int32, (256, 256), 0)
    i = lax.broadcasted_iota(jnp.int32, (256, 256), 1)
    turn[...] = (i == o % 32 // 2 * 16 + o // 32 * 2 + o % 2).astype(F32).astype(BF16)
    back[...] = (i == o % 16 // 2 * 32 + o // 16 * 2 + o % 2).astype(F32).astype(BF16)


def kernel(
    raw_ref, rep_in, dft_in, steer_in, bin_in, block_in, beam_in, owner_in,
    out_ref,
    raw, pkl, pkr, hl, hr, ur, ui, tza, tz, s, pks, sr, p, r1, a1, rp, rm, a2, r3, gath, wall, passed, table,
    select, turn, back, slots, d1, mid, d2,
    rep_ref, dft_ref, steer_ref, bin_ref, block_ref, beam_ref, owner_ref,
    ls, ms, hs, ht, s1, t1, s2, t2, s3, t3, s4, t4, s5, t5, s6, t6, s7, t7, s8, t8, s9, t9, s4b, t4b,
):
    me = lax.axis_index("range")
    core = me % 2
    y = me // 2 % 4
    x = me // 8 % 4
    z = me // 32
    zx = me // 8
    yc = me % 8
    bin_ = 2 * (4 * z + x + z % 2 * (3 - 2 * x)) + y % 2
    member = y // 2 * 2 + core
    sib = me + 1 - 2 * core
    sa = 32 - 24 * core
    sb = 8 + 24 * core
    a = me // sa % 4
    b = me // sb % 4
    left = (me + 127) % 128
    right = (me + 1) % 128

    def along(stride, coord, j):
        return me + ((coord + j) % 4 - coord) * stride

    near = []
    for delta in (1, -1, 0):
        for j in range(4):
            if delta or j:
                near.append((delta, j, at_home((bin_ + delta + 32) % 32, (member + j) % 4)))
    planes = [(z + j // 4) % 4 * 4 + (x + j % 4) % 4 for j in FAR]
    froms = [(z + 4 - j // 4) % 4 * 4 + (x + 4 - j % 4) % 4 for j in FAR]
    posts = [(yc + j) % 8 for j in POSTS]
    sheet = [
        ((b + j // 4) % 4, (y + j % 4) % 4)
        for j in FAR
    ]
    spots = [me + (q - b) * sb + (r - y) * 2 for q, r in sheet]
    partners = [left, right, sib, along(sa, a, 1), along(sa, a, 3)] + spots
    small = [
        pltpu.make_async_copy(src, dst, ms.at[n])
        for n, (src, dst) in enumerate(
            [
                (rep_in, rep_ref), (dft_in, dft_ref), (steer_in, steer_ref), (bin_in, bin_ref),
                (block_in, block_ref), (beam_in, beam_ref), (owner_in, owner_ref),
            ]
        )
    ]
    small[0].start()
    loads = []
    for i in range(4):
        at = pl.ds(16 * i, 16)
        copy = pltpu.make_async_copy(raw_ref.at[:, at], raw.at[:, at], ls.at[i])
        copy.start()
        loads.append(copy)
    for copy in small[1:]:
        copy.start()
    barrier = pltpu.get_barrier_semaphore()
    for to in partners:
        pl.semaphore_signal(barrier, inc=1, device_id=(to,), device_id_type=MESH)
    for i in range(4):
        at = pl.ds(16 * i, 16)
        loads[i].wait()
        pkl[at] = jnp.concatenate([raw[0, at, :, 0:64], raw[1, at, :, 0:64]], axis=-1)
        pkr[at] = jnp.concatenate([raw[0, at, :, 192:256], raw[1, at, :, 192:256]], axis=-1)
        window_inner(at, raw, ur, ui)
    pl.semaphore_wait(barrier, len(partners))
    copies = []

    def finish():
        for copy in copies:
            copy.wait_send()


    def to_left(i):
        at = pl.ds(16 * i, 16)
        return remote(pkl.at[at], hr.at[at], hs.at[0, i], ht.at[0, i], left)

    for i in range(4):
        at = pl.ds(16 * i, 16)
        copy = remote(pkr.at[at], hl.at[at], hs.at[1, i], ht.at[1, i], right)
        copy.start()
        copies.append(copy)

        @pl.when(me > 0)
        def _():
            to_left(i).start()

    @pl.when(me == 127)
    def _():
        hr[...] = jnp.zeros_like(hr)

    small[0].wait()
    build_toeplitz(rep_ref, jnp.where(me > 0, 1.0, 0.0).astype(F32), tza, tz)
    for copy in small[1:]:
        copy.wait()
    selection(bin_ref, block_ref, beam_ref, owner_ref, select, turn, back)
    for i in range(4):
        copies[i].wait_recv()

        @pl.when(me < 127)
        def _():
            to_left(i).wait_recv()

        window_edges(pl.ds(16 * i, 16), raw, hl, hr, ur, ui)
        spectra_part(i, ur, ui, dft_ref, s, tza, tz)

    @pl.when(me > 0)
    def _():
        for i in range(4):
            to_left(i).wait_send()

    s[0:2] = s[32:34]
    s[34] = s[2]
    pks[...] = join(s[2:34, :, 0:64], s[2:34, :, 128:192])
    share = remote(pks, sr.at[pl.ds(2, 32)], s9, t9, left)

    order = (2, 1, 3, 0)
    oa = me // sb % 4
    for j in order:
        q = (oa + j) % 4
        for u in range(4):
            cross_products(core * q + (1 - core) * u, core * u + (1 - core) * q, s, p)
        at = pl.ds(q * 8, 8)
        copy = remote(p.at[1 - core, at], r1.at[at], s1.at[j], t1.at[j], sib)
        copy.start()
        copies.append(copy)

    rings = []

    def ring(src, dst, n, to):
        copy = remote(src, dst, s2.at[n], t2.at[n], to)
        copy.start()
        copies.append(copy)
        rings.append(copy)

    ahead, behind = along(sa, a, 1), along(sa, a, 3)
    base = {j: (a + j) % 4 * 8 for j in range(4)}
    for j in order:
        at = pl.ds(base[j], 8)
        remote(p.at[core, at], r1.at[at], s1.at[j], t1.at[j], sib).wait_recv()
        a1[at] = p[core, at] + r1[at]
        if j == 2:
            ring(a1.at[pl.ds(base[2], 4)], rp.at[0], 0, ahead)
            ring(a1.at[pl.ds(base[2] + 4, 4)], rm.at[0], 1, behind)
        elif j == 1:
            ring(a1.at[pl.ds(base[1] + 4, 4)], rp.at[1], 2, ahead)
        elif j == 3:
            ring(a1.at[pl.ds(base[3], 4)], rm.at[1], 3, behind)
    rings[0].wait_recv()
    at = pl.ds(base[1], 4)
    a1[at] = a1[at] + rp[0]
    ring(a1.at[at], rp.at[2], 4, ahead)
    rings[1].wait_recv()
    at = pl.ds(base[3] + 4, 4)
    a1[at] = a1[at] + rm[0]
    ring(a1.at[at], rm.at[2], 5, behind)
    for n in (2, 3):
        rings[n].wait_recv()
    at = pl.ds(base[0] + 4, 4)
    a2[4:8] = a1[at] + rp[1]
    at = pl.ds(base[0], 4)
    a2[0:4] = a1[at] + rm[1]
    rings[4].wait_recv()
    a2[0:4] = a2[0:4] + rp[2]
    rings[5].wait_recv()
    a2[4:8] = a2[4:8] + rm[2]

    parts = ((pl.ds(32, 8), 32, 8, s3, t3), (pl.ds(0, 32), 0, 32, s4, t4))
    for rows, start, size, sends, lands in parts:
        for n, (q, r) in enumerate(sheet):
            at = pl.ds(pl.multiple_of(r // 2 * 40 + start, 8), size)
            copy = remote(
                a2.at[q * 2 + r % 2, at], r3.at[n, rows], sends.at[n], lands.at[n], spots[n]
            )
            copy.start()
            copies.append(copy)
    needs = {-1: pl.ds(0, 40), 0: pl.ds(16, 24), 1: pl.ds(32, 8)}

    def pass_on(deltas):
        for n, (delta, j, to) in enumerate(near):
            if delta in deltas:
                part = gath.at[1, member, needs[delta]]
                there = gath.at[1 - delta, member, needs[delta]]
                copy = remote(part, there, s5.at[n], t5.at[1 - delta, member], to)
                copy.start()
                copies.append(copy)

    for rows, start, size, sends, lands in parts:
        for n in range(15):
            remote(r3.at[n, rows], r3.at[n, rows], sends.at[n], lands.at[n], sib).wait_recv()
        at = pl.ds(pl.multiple_of(y // 2 * 40 + start, 8), size)
        terms = [a2[b * 2 + y % 2, at]] + [r3[n, rows] for n in range(15)]
        while len(terms) > 1:
            terms = [u + v for u, v in zip(terms[::2], terms[1::2])]
        gath[1, member, rows] = terms[0]
        pass_on((1,) if start else (-1, 0))

    def arrived(deltas):
        for delta, j, _ in near:
            if delta in deltas:
                part = gath.at[1 - delta, (member + j) % 4, needs[delta]]
                remote(part, part, s5.at[0], t5.at[1 - delta, (member + j) % 4], sib).wait_recv()

    arrived((1,))

    def others():
        arrived((-1, 0))
        share.start()
        copies.append(share)

    wall[bin_] = solve(gath, steer_ref, bin_ % 2, others)
    side = bin_ // 2 % 2
    for n, step in enumerate((4, 3, 5, 2, 6, 1, 7, 0)):
        for e in range(2):
            to = (bin_ // 4 + step) % 8 * 4 + core * 2 + e

            @pl.when(to != bin_)
            def _(n=n, e=e, to=to):
                remote(
                    wall.at[bin_], wall.at[bin_], s6.at[2 * n + e], t6.at[bin_],
                    at_home(to, member // 2 * 2 + side),
                ).start()

    share.wait_recv()
    sr[0:2] = sr[32:34]
    sr[34] = sr[2]
    for step in (0, 1, 7, 2, 6, 3, 5, 4):
        first = (bin_ // 4 + step) % 8 * 4 + core * 2
        at = pl.ds(first, 2)
        for e in range(2):

            @pl.when(first + e != bin_)
            def _(q=first + e):
                remote(wall.at[q], wall.at[q], s6.at[0], t6.at[q], sib).wait_recv()

        copy = remote(wall.at[at], passed.at[at], s4b.at[step], t4b.at[step], sib)
        copy.start()
        copies.append(copy)
        beam_pair(first, wall, s, sr, table)
    for step in (0, 1, 7, 2, 6, 3, 5, 4):
        first = (bin_ // 4 + step) % 8 * 4 + 2 - core * 2
        at = pl.ds(first, 2)
        remote(wall.at[at], passed.at[at], s4b.at[step], t4b.at[step], sib).wait_recv()
        beam_pair(first, passed, s, sr, table)
    for n, step in enumerate((4, 3, 5, 2, 6, 1, 7, 0)):
        for e in range(2):

            @pl.when((bin_ // 4 + step) % 8 * 4 + core * 2 + e != bin_)
            def _(n=n, e=e):
                remote(wall.at[bin_], wall.at[bin_], s6.at[2 * n + e], t6.at[bin_], sib).wait_send()

    slots[...] = (
        jnp.dot(select[...], table[...], preferred_element_type=F32)
        .astype(BF16)
        .reshape(16, 16, 256)
    )
    for j, q in enumerate(planes):
        copy = remote(slots.at[q], d1.at[zx], s7.at[j], t7.at[j], q * 8 + yc)
        copy.start()
        copies.append(copy)
    d1[zx] = slots[zx]
    for j, q in enumerate(froms):
        remote(slots.at[q], d1.at[q], s7.at[j], t7.at[j], sib).wait_recv()
    mid[...] = (
        jnp.dot(turn[...], d1[...].reshape(256, 256), preferred_element_type=F32)
        .astype(BF16)
        .reshape(8, 32, 256)
    )
    for j, q in enumerate(posts):
        copy = remote(mid.at[q], d2.at[yc], s8.at[j], t8.at[j], zx * 8 + q)
        copy.start()
        copies.append(copy)
    d2[yc] = mid[yc]
    for j, step in enumerate(POSTS):
        q = (yc + 8 - step) % 8
        remote(mid.at[q], d2.at[q], s8.at[j], t8.at[j], sib).wait_recv()
    rows = jnp.dot(back[...], d2[...].reshape(256, 256), preferred_element_type=F32)
    out_ref[...] = rows.astype(BF16)
    finish()


def program(raw, replica, det_bin, det_block, det_beam, owner):
    dma = pltpu.SemaphoreType.DMA
    vm = pltpu.VMEM
    rows = (1, 128)
    return pl.pallas_call(
        kernel,
        out_shape=jax.ShapeDtypeStruct((256, 256), BF16),
        in_specs=[HBM] * 8,
        out_specs=VMEM,
        scratch_shapes=[
            vm((2, 64, 32, 256), BF16),
            vm((64, 32, 128), BF16),
            vm((64, 32, 128), BF16),
            vm((64, 32, 128), BF16),
            vm((64, 32, 128), BF16),
            vm((64, 32, 384), BF16),
            vm((64, 32, 384), BF16),
            vm((512, 256), BF16),
            vm((512, 256), BF16),
            vm((35, 64, 512), BF16),
            vm((32, 64, 128), BF16),
            vm((35, 64, 128), BF16),
            vm((2, 32, 80, 128), F32),
            vm((32, 80, 128), F32),
            vm((32, 80, 128), F32),
            vm((3, 4, 80, 128), F32),
            vm((3, 4, 80, 128), F32),
            vm((8, 80, 128), F32),
            vm((15, 40, 128), F32),
            vm((3, 4, 40, 128), F32),
            vm((32, 16, 256), BF16),
            vm((32, 16, 256), BF16),
            vm((512, 256), BF16),
            vm((256, 512), BF16),
            vm((256, 256), BF16),
            vm((256, 256), BF16),
            vm((16, 16, 256), BF16),
            vm((16, 16, 256), BF16),
            vm((8, 32, 256), BF16),
            vm((8, 32, 256), BF16),
            vm((2, 128), BF16),
            vm((512, 512), BF16),
            vm((8, 128), F32),
            vm(rows, jnp.int32), vm(rows, jnp.int32), vm(rows, jnp.int32), vm(rows, jnp.int32),
            dma((4,)), dma((7,)), dma((2, 4)), dma((2, 4)),
            dma((4,)), dma((4,)), dma((6,)), dma((6,)), dma((15,)), dma((15,)),
            dma((15,)), dma((15,)), dma((11,)), dma((3, 4)), dma((31,)), dma((32,)),
            dma((15,)), dma((15,)), dma((7,)), dma((7,)), dma(()), dma(()), dma((8,)), dma((8,)),
        ],
        compiler_params=pltpu.CompilerParams(
            collective_id=0, has_side_effects=True, vmem_limit_bytes=LIMIT
        ),
        name="stap",
    )(
        raw, replica, jnp.asarray(dft_matrix()), jnp.asarray(steer_rows()),
        det_bin, det_block, det_beam, owner,
    )


def on_device(raw, replica, det_bin, det_block, det_beam, det_owner):
    rows = [v.reshape(1, 128) for v in (det_bin, det_block, det_beam, det_owner)]
    return program(raw, replica, *rows).astype(F32)


def solution(mesh):
    in_specs = (
        P(None, None, None, "range"),
        P(),
        P("range"),
        P("range"),
        P("range"),
        P("range", None),
    )
    return jax.shard_map(
        on_device,
        mesh=mesh,
        in_specs=in_specs,
        out_specs=P("range", None),
        check_vma=False,
    )
```

```python
import math

import jax
import jax.numpy as jnp
import numpy as np
from jax import lax
from jax.experimental import pallas as pl
from jax.experimental.pallas import tpu as pltpu
from jax.sharding import PartitionSpec as P

C = 64
PULSES = 32
TAPS = 128
BEAMS = 8
F32 = jnp.float32
BF16 = jnp.bfloat16
MESH = pl.DeviceIdType.MESH
VMEM = pl.BlockSpec(memory_space=pltpu.VMEM)
HBM = pl.BlockSpec(memory_space=pltpu.HBM)
NT = (((1,), (1,)), ((), ()))
LIMIT = 63 * 1024 * 1024
FAR = (10, 9, 11, 6, 14, 2, 8, 5, 7, 13, 15, 1, 3, 4, 12)
POSTS = (4, 5, 3, 2, 6, 7, 1)


def dft_matrix():
    index = np.arange(PULSES)
    angle = 2.0 * math.pi / PULSES * (index[:, None] * index[None, :] % PULSES)
    scale = PULSES**-0.5
    real = np.cos(angle) * scale
    imag = -np.sin(angle) * scale
    eye = np.eye(8)
    kr = np.einsum("pd,ab->dabp", real, eye).reshape(256, 256)
    ki = np.einsum("pd,ab->dabp", imag, eye).reshape(256, 256)
    full = np.concatenate([np.concatenate([kr, -ki], 1), np.concatenate([ki, kr], 1)], 0)
    return full.astype(jnp.bfloat16)


def steer_rows():
    sines = -0.8 + 1.6 * np.arange(BEAMS, dtype=np.float32) / np.float32(BEAMS - 1)
    angle = (math.pi * np.arange(C, dtype=np.float32)[None, :] * sines[:, None]).astype(np.float32)
    return np.concatenate([np.cos(angle), -np.sin(angle)], 1).astype(np.float32)


def remote(src, dst, send, recv, to):
    return pltpu.make_async_remote_copy(
        src_ref=src, dst_ref=dst, send_sem=send, recv_sem=recv, device_id=(to,), device_id_type=MESH
    )


def build_toeplitz(rep_ref, keep, tza, tz):
    def band(v):
        wide = jnp.concatenate(
            [jnp.broadcast_to(v, (TAPS, TAPS)), jnp.zeros((TAPS, TAPS), F32)], axis=1
        )
        return pltpu.roll(wide, 0, 1, stride=1, stride_axis=0).T

    rep = rep_ref[...].astype(F32)
    tr = band(rep[0:1])
    ti = band(rep[1:2])
    full = jnp.concatenate(
        [jnp.concatenate([tr, -ti], axis=1), jnp.concatenate([ti, tr], axis=1)], axis=0
    )
    tz[...] = full.astype(BF16)
    row = lax.broadcasted_iota(jnp.int32, (512, 256), 0) % 256
    lane = lax.broadcasted_iota(jnp.int32, (512, 256), 1) % 128
    tza[...] = jnp.where((row >= 64) & (lane < 64), full * keep, full).astype(BF16)


def join(*parts):
    return jnp.concatenate(parts, axis=-1)


def window_inner(at, raw, ur, ui):
    for n, u in enumerate((ur, ui)):
        u[at, :, 128:256] = join(raw[n, at, :, 64:128], raw[n, at, :, 128:192])


def window_edges(at, raw, hl, hr, ur, ui):
    for n, u in enumerate((ur, ui)):
        lanes = slice(64 * n, 64 * n + 64)
        u[at, :, 0:128] = join(hl[at, :, lanes], raw[n, at, :, 0:64])
        u[at, :, 256:384] = join(raw[n, at, :, 192:256], hr[at, :, lanes])


def spectra_part(i, ur, ui, dft_ref, s, tza, tz):
    first = 16 * i
    for b in range(2):
        ys = []
        for n in range(2):
            at = pl.ds(first + 8 * n, 8)
            gates = slice(128 * b, 128 * b + 256)
            window = join(ur[at, :, gates].reshape(256, 256), ui[at, :, gates].reshape(256, 256))
            band = tz[...] if b else tza[...]
            ys.append(jnp.dot(window, band, preferred_element_type=F32).astype(BF16))
        ya, yb = ys
        y = jnp.concatenate(
            [join(ya[:, :128], yb[:, :128]), join(ya[:, 128:], yb[:, 128:])], axis=0
        )
        out = jnp.dot(dft_ref[...], y, preferred_element_type=F32)
        for p in range(2):
            h = out[256 * p : 256 * p + 256]
            v = jnp.concatenate(
                [h[:, :128].reshape(32, 8, 128), h[:, 128:].reshape(32, 8, 128)], axis=1
            )
            lanes = 256 * b + 128 * p
            s[2:34, first : first + 16, lanes : lanes + 128] = v.astype(BF16)


def snake(k):
    z = k // 4
    x = k % 4
    return z, x + z % 2 * (3 - 2 * x)


def home(q):
    z, x = snake(q // 2)
    return z * 32 + x * 8 + q % 2 * 2


def at_home(q, member):
    return home(q) + member // 2 * 4 + member % 2


def beam_pair(first, wall, s, sr, table):
    lhs = wall[pl.ds(first, 2)].reshape(32, 256)
    rhs = join(
        s[pl.ds(first + 1, 4)].reshape(256, 512), sr[pl.ds(first + 1, 4)].reshape(256, 128)
    )
    prod = jnp.dot(lhs, rhs, preferred_element_type=F32)
    top = jnp.concatenate([prod[0:8], prod[16:24]], axis=0)
    low = jnp.concatenate([prod[8:16], prod[24:32]], axis=0)
    half = lax.broadcasted_iota(jnp.int32, (16, 128), 1) < 64

    def flip(v):
        return pltpu.roll(v, 64, 1)

    parts = []
    for at in (0, 256):
        parts.append(flip(top[:, at : at + 128] + low[:, at + 128 : at + 256]))
        parts.append(flip(top[:, at + 128 : at + 256] - low[:, at : at + 128]))
    turn = flip(low[:, 512:])
    last = top[:, 512:] + jnp.where(half, turn, -turn)
    lanes = [
        jnp.where(half, parts[0], parts[2]),
        jnp.where(half, parts[1], parts[3]),
        jnp.where(half, parts[2], flip(last)),
        jnp.where(half, parts[3], last),
    ]
    for i in range(2):
        rows = pl.ds(pl.multiple_of(256 * i + first * 8, 16), 16)
        table[rows] = join(*lanes[2 * i : 2 * i + 2]).astype(BF16)


def store_products(p, places, two, one, zero):
    lane = lax.broadcasted_iota(jnp.int32, (32, 128), 1)
    row = lax.broadcasted_iota(jnp.int32, (32, 128), 0)
    swapped = pltpu.roll(zero, 64, 1)
    top = jnp.where(row >= lane, zero[:32], swapped[:32])
    bottom = jnp.where(row + 32 >= lane - 64, swapped[32:], zero[32:])
    packed = jnp.where(lane < 64, top, bottom)
    for h in range(2):
        pos = places[h]
        for q in range(2):
            a = 32 * h + 16 * q
            p[h, pos, 40 * q : 40 * q + 16] = two[a : a + 16]
            p[h, pos, 40 * q + 16 : 40 * q + 32] = one[a : a + 16]
            p[h, pos, 40 * q + 32 : 40 * q + 40] = packed[a // 2 : a // 2 + 8]


def cross_products(z, x, s, p):
    f = 2 * (4 * z + x + z % 2 * (3 - 2 * x))
    lhs = s[pl.ds(f, 4)].reshape(256, 512)
    rhs = []
    for n in range(2):
        v = s[f + 2 + n]
        rhs += [v, join(-v[:, 128:256], v[:, :128], -v[:, 384:], v[:, 256:384])]
    prod = lax.dot_general(lhs, jnp.concatenate(rhs, axis=0), NT, preferred_element_type=F32)
    first, second = (z * 8 + x * 2, x * 8 + z * 2), (z * 8 + x * 2 + 1, x * 8 + z * 2 + 1)
    store_products(p, first, prod[:64, :128], prod[64:128, :128], prod[128:192, :128])
    store_products(p, second, prod[64:128, 128:], prod[128:192, 128:], prod[192:, 128:])


def times_i(m):
    return jnp.concatenate([-m[:, 64:], m[:, :64]], axis=1)


def cdot(x, y):
    return jnp.dot(
        x, jnp.concatenate([y, times_i(y)], axis=0),
        preferred_element_type=F32, precision=lax.Precision.HIGHEST,
    )


def adjoint(m):
    t = m.T
    return jnp.concatenate([t[:64], -t[64:]], axis=1)


def lane_of(v, k):
    return jnp.broadcast_to(v[:, k : k + 1], (8, 128))


def row_of(v, r):
    return jnp.broadcast_to(v[r : r + 1], (8, 128))


def cmul(x, y):
    return (x[0] * y[0] - x[1] * y[1], x[0] * y[1] + x[1] * y[0])


def cmulc(x, y):
    return (x[0] * y[0] + x[1] * y[1], x[1] * y[0] - x[0] * y[1])


def cadd(x, y):
    return (x[0] + y[0], x[1] + y[1])


def csub(x, y):
    return (x[0] - y[0], x[1] - y[1])


def cscale(x, c):
    return (x * c[0], x * c[1])


def conj(x):
    return (x[0], -x[1])


def size2(x):
    return x[0] * x[0] + x[1] * x[1]


def rdot(x, y):
    return x[0] * y[0] + x[1] * y[1]


def cm(c, row):
    v, w = row
    return (c[0] * v + c[1] * w, c[0] * w - c[1] * v)


def hermitian_inverse(m):
    lane = lax.broadcasted_iota(jnp.int32, (8, 128), 1)
    sub = lax.broadcasted_iota(jnp.int32, (8, 128), 0)
    ms = [m[8 * t : 8 * t + 8] for t in range(8)]
    for k in range(0, 64, 4):
        t0, r0 = divmod(k, 8)
        w = ms[t0]
        wi = pltpu.roll(w, 64, 1)
        wi = jnp.where(lane < 64, -wi, wi)
        cr = [[lane_of(v, k + j) for v in ms] for j in range(4)]
        ci = [[lane_of(v, 64 + k + j) for v in ms] for j in range(4)]

        def entry(i, j):
            return (row_of(cr[j][t0], r0 + i), row_of(ci[j][t0], r0 + i))

        a, d, b = entry(0, 0)[0], entry(1, 1)[0], entry(0, 1)
        p, s, q = entry(2, 2)[0], entry(3, 3)[0], entry(2, 3)
        bb = [[entry(0, 2), entry(0, 3)], [entry(1, 2), entry(1, 3)]]
        det = 1.0 / (a * d - size2(b))
        ia, id_, ib = d * det, a * det, cscale(-det, b)
        ww = [
            [cadd(cscale(ia, bb[0][j]), cmul(ib, bb[1][j])) for j in range(2)],
            [cadd(cmul(conj(ib), bb[0][j]), cscale(id_, bb[1][j])) for j in range(2)],
        ]
        s00 = p - (rdot(bb[0][0], ww[0][0]) + rdot(bb[1][0], ww[1][0]))
        s11 = s - (rdot(bb[0][1], ww[0][1]) + rdot(bb[1][1], ww[1][1]))
        s01 = csub(q, cadd(cmulc(ww[0][1], bb[0][0]), cmulc(ww[1][1], bb[1][0])))
        dets = 1.0 / (s00 * s11 - size2(s01))
        j00, j11, j01 = s11 * dets, s00 * dets, cscale(-dets, s01)
        hit = ((lane >= k) & (lane < k + 4)) | ((lane >= 64 + k) & (lane < 68 + k))
        rows = []
        for j in range(4):
            real = jnp.where(hit, jnp.where(lane == k + j, 1.0, 0.0), row_of(w, r0 + j))
            imag = jnp.where(hit, jnp.where(lane == 64 + k + j, 1.0, 0.0), row_of(wi, r0 + j))
            rows.append((real, imag))
        t2 = csub(rows[2], cadd(cm(conj(ww[0][0]), rows[0]), cm(conj(ww[1][0]), rows[1])))
        t3 = csub(rows[3], cadd(cm(conj(ww[0][1]), rows[0]), cm(conj(ww[1][1]), rows[1])))
        x2 = cadd(cscale(j00, t2), cm(j01, t3))
        x3 = cadd(cscale(j11, t3), cm(conj(j01), t2))
        u0 = cadd(cscale(ia, rows[0]), cm(ib, rows[1]))
        u1 = cadd(cscale(id_, rows[1]), cm(conj(ib), rows[0]))
        x0 = csub(u0, cadd(cm(ww[0][0], x2), cm(ww[0][1], x3)))
        x1 = csub(u1, cadd(cm(ww[1][0], x2), cm(ww[1][1], x3)))
        g = [x0, x1, x2, x3]
        for t in range(8):
            terms = [cr[j][t] * g[j][0] + ci[j][t] * g[j][1] for j in range(4)]
            mt = jnp.where(hit, 0.0, ms[t]) - ((terms[0] + terms[1]) + (terms[2] + terms[3]))
            if t == t0:
                for j in range(4):
                    mt = jnp.where(sub == r0 + j, g[j][0], mt)
            ms[t] = mt
    return jnp.concatenate(ms, axis=0)


def solve(g_ref, steer_ref, parity, others):
    scale = 1.0 / 32768.0
    order = (0, 2, 1, 3)
    r64 = lax.broadcasted_iota(jnp.int32, (64, 64), 0)
    c64 = lax.broadcasted_iota(jnp.int32, (64, 64), 1)

    def block(g, rows):
        return jnp.concatenate([g_ref[g, m, rows] for m in order], axis=0) * scale

    def diagonal(g):
        pk = block(g, slice(32, 40))
        k = jnp.concatenate([pk[:, :64], pk[:, 64:]], axis=0)
        kt = k.T
        real = jnp.where(r64 >= c64, k, kt)
        imag = jnp.where(r64 < c64, k, jnp.where(r64 == c64, 0.0, -kt))
        return jnp.concatenate([real, imag], axis=1)

    p = hermitian_inverse(diagonal(0))
    others()
    a33 = diagonal(1)
    a22 = diagonal(2)
    a12 = block(2, slice(0, 16))
    a13 = block(1, slice(16, 32))
    a32 = block(2, slice(16, 32))
    v21 = cdot(adjoint(a12), p)
    v31 = cdot(adjoint(a13), p)
    s22 = a22 - cdot(v21, a12)
    s32 = a32 - cdot(v31, a12)
    s33 = a33 - cdot(v31, a13)
    q = hermitian_inverse(s22)
    v32 = cdot(s32, q)
    s33 = s33 - cdot(v32, adjoint(s32))
    r = hermitian_inverse(s33)
    t = steer_ref[...]
    y3 = cdot(t, r)
    y2 = -cdot(y3, v32)
    y1 = -cdot(y2, v21) - cdot(y3, v31)
    norm = lax.rsqrt(jnp.sum(t * y3, axis=1, keepdims=True))
    real = [(v[:, :64] * norm) for v in (y1, y3, y2)]
    imag = [(v[:, 64:] * -norm) for v in (y1, y3, y2)]
    rows = jnp.concatenate(
        [jnp.concatenate(real, axis=1), jnp.concatenate(imag, axis=1)], axis=0
    )
    zero = jnp.zeros((16, 64), F32)
    even = jnp.concatenate([rows, zero], axis=1)
    odd = jnp.concatenate([zero, rows], axis=1)
    return jnp.where(parity == 0, even, odd).astype(BF16)


def selection(bin_ref, block_ref, beam_ref, owner_ref, select, turn, back):
    s_iota = lax.broadcasted_iota(jnp.int32, (256, 128), 0)
    named = (s_iota // 2 == owner_ref[...]).astype(F32)
    before = (
        lax.broadcasted_iota(jnp.int32, (128, 128), 0)
        < lax.broadcasted_iota(jnp.int32, (128, 128), 1)
    ).astype(F32)
    earlier = jnp.dot(named.astype(BF16), before.astype(BF16), preferred_element_type=F32)
    pick = jnp.where(earlier == (s_iota % 2).astype(F32), named, 0.0).astype(BF16)
    wanted = block_ref[...] * 256 + bin_ref[...] * 8 + beam_ref[...]
    t_iota = lax.broadcasted_iota(jnp.int32, (512, 128), 0)
    holds = (t_iota == wanted).astype(F32).astype(BF16)
    select[...] = lax.dot_general(pick, holds, NT, preferred_element_type=F32).astype(BF16)
    o = lax.broadcasted_iota(jnp.int32, (256, 256), 0)
    i = lax.broadcasted_iota(jnp.int32, (256, 256), 1)
    turn[...] = (i == o % 32 // 2 * 16 + o // 32 * 2 + o % 2).astype(F32).astype(BF16)
    back[...] = (i == o % 16 // 2 * 32 + o // 16 * 2 + o % 2).astype(F32).astype(BF16)


def kernel(
    raw_ref, rep_in, dft_in, steer_in, bin_in, block_in, beam_in, owner_in,
    out_ref,
    raw, pkl, pkr, hl, hr, ur, ui, tza, tz, s, pks, sr, p, r1, a1, rp, rm, a2, r3, gath, wall, passed, table,
    select, turn, back, slots, d1, mid, d2,
    rep_ref, dft_ref, steer_ref, bin_ref, block_ref, beam_ref, owner_ref,
    ls, ms, hs, ht, s1, t1, s2, t2, s3, t3, s4, t4, s5, t5, s6, t6, s7, t7, s8, t8, s9, t9, s4b, t4b,
):
    me = lax.axis_index("range")
    core = me % 2
    y = me // 2 % 4
    x = me // 8 % 4
    z = me // 32
    zx = me // 8
    yc = me % 8
    bin_ = 2 * (4 * z + x + z % 2 * (3 - 2 * x)) + y % 2
    member = y // 2 * 2 + core
    sib = me + 1 - 2 * core
    sa = 32 - 24 * core
    sb = 8 + 24 * core
    a = me // sa % 4
    b = me // sb % 4
    left = (me + 127) % 128
    right = (me + 1) % 128

    def along(stride, coord, j):
        return me + ((coord + j) % 4 - coord) * stride

    near = []
    for delta in (1, -1, 0):
        for j in range(4):
            if delta or j:
                near.append((delta, j, at_home((bin_ + delta + 32) % 32, (member + j) % 4)))
    planes = [(z + j // 4) % 4 * 4 + (x + j % 4) % 4 for j in FAR]
    froms = [(z + 4 - j // 4) % 4 * 4 + (x + 4 - j % 4) % 4 for j in FAR]
    posts = [(yc + j) % 8 for j in POSTS]
    sheet = [
        ((b + j // 4) % 4, (y + j % 4) % 4)
        for j in FAR
    ]
    spots = [me + (q - b) * sb + (r - y) * 2 for q, r in sheet]
    partners = [left, right, sib, along(sa, a, 1), along(sa, a, 3)] + spots
    small = [
        pltpu.make_async_copy(src, dst, ms.at[n])
        for n, (src, dst) in enumerate(
            [
                (rep_in, rep_ref), (dft_in, dft_ref), (steer_in, steer_ref), (bin_in, bin_ref),
                (block_in, block_ref), (beam_in, beam_ref), (owner_in, owner_ref),
            ]
        )
    ]
    small[0].start()
    loads = []
    for i in range(4):
        at = pl.ds(16 * i, 16)
        copy = pltpu.make_async_copy(raw_ref.at[:, at], raw.at[:, at], ls.at[i])
        copy.start()
        loads.append(copy)
    for copy in small[1:]:
        copy.start()
    barrier = pltpu.get_barrier_semaphore()
    for to in partners:
        pl.semaphore_signal(barrier, inc=1, device_id=(to,), device_id_type=MESH)
    for i in range(4):
        at = pl.ds(16 * i, 16)
        loads[i].wait()
        pkl[at] = jnp.concatenate([raw[0, at, :, 0:64], raw[1, at, :, 0:64]], axis=-1)
        pkr[at] = jnp.concatenate([raw[0, at, :, 192:256], raw[1, at, :, 192:256]], axis=-1)
        window_inner(at, raw, ur, ui)
    pl.semaphore_wait(barrier, len(partners))
    copies = []

    def finish():
        for copy in copies:
            copy.wait_send()


    def to_left(i):
        at = pl.ds(16 * i, 16)
        return remote(pkl.at[at], hr.at[at], hs.at[0, i], ht.at[0, i], left)

    for i in range(4):
        at = pl.ds(16 * i, 16)
        copy = remote(pkr.at[at], hl.at[at], hs.at[1, i], ht.at[1, i], right)
        copy.start()
        copies.append(copy)

        @pl.when(me > 0)
        def _():
            to_left(i).start()

    @pl.when(me == 127)
    def _():
        hr[...] = jnp.zeros_like(hr)

    small[0].wait()
    build_toeplitz(rep_ref, jnp.where(me > 0, 1.0, 0.0).astype(F32), tza, tz)
    for copy in small[1:]:
        copy.wait()
    selection(bin_ref, block_ref, beam_ref, owner_ref, select, turn, back)
    for i in range(4):
        copies[i].wait_recv()

        @pl.when(me < 127)
        def _():
            to_left(i).wait_recv()

        window_edges(pl.ds(16 * i, 16), raw, hl, hr, ur, ui)
        spectra_part(i, ur, ui, dft_ref, s, tza, tz)

    @pl.when(me > 0)
    def _():
        for i in range(4):
            to_left(i).wait_send()

    s[0:2] = s[32:34]
    s[34] = s[2]
    pks[...] = join(s[2:34, :, 0:64], s[2:34, :, 128:192])
    share = remote(pks, sr.at[pl.ds(2, 32)], s9, t9, left)

    order = (2, 1, 3, 0)
    oa = me // sb % 4
    for j in order:
        q = (oa + j) % 4
        for u in range(4):
            cross_products(core * q + (1 - core) * u, core * u + (1 - core) * q, s, p)
        at = pl.ds(q * 8, 8)
        copy = remote(p.at[1 - core, at], r1.at[at], s1.at[j], t1.at[j], sib)
        copy.start()
        copies.append(copy)

    rings = []

    def ring(src, dst, n, to):
        copy = remote(src, dst, s2.at[n], t2.at[n], to)
        copy.start()
        copies.append(copy)
        rings.append(copy)

    ahead, behind = along(sa, a, 1), along(sa, a, 3)
    base = {j: (a + j) % 4 * 8 for j in range(4)}
    for j in order:
        at = pl.ds(base[j], 8)
        remote(p.at[core, at], r1.at[at], s1.at[j], t1.at[j], sib).wait_recv()
        a1[at] = p[core, at] + r1[at]
        if j == 2:
            ring(a1.at[pl.ds(base[2], 4)], rp.at[0], 0, ahead)
            ring(a1.at[pl.ds(base[2] + 4, 4)], rm.at[0], 1, behind)
        elif j == 1:
            ring(a1.at[pl.ds(base[1] + 4, 4)], rp.at[1], 2, ahead)
        elif j == 3:
            ring(a1.at[pl.ds(base[3], 4)], rm.at[1], 3, behind)
    rings[0].wait_recv()
    at = pl.ds(base[1], 4)
    a1[at] = a1[at] + rp[0]
    ring(a1.at[at], rp.at[2], 4, ahead)
    rings[1].wait_recv()
    at = pl.ds(base[3] + 4, 4)
    a1[at] = a1[at] + rm[0]
    ring(a1.at[at], rm.at[2], 5, behind)
    for n in (2, 3):
        rings[n].wait_recv()
    at = pl.ds(base[0] + 4, 4)
    a2[4:8] = a1[at] + rp[1]
    at = pl.ds(base[0], 4)
    a2[0:4] = a1[at] + rm[1]
    rings[4].wait_recv()
    a2[0:4] = a2[0:4] + rp[2]
    rings[5].wait_recv()
    a2[4:8] = a2[4:8] + rm[2]

    parts = ((pl.ds(32, 8), 32, 8, s3, t3), (pl.ds(0, 32), 0, 32, s4, t4))
    for rows, start, size, sends, lands in parts:
        for n, (q, r) in enumerate(sheet):
            at = pl.ds(pl.multiple_of(r // 2 * 40 + start, 8), size)
            copy = remote(
                a2.at[q * 2 + r % 2, at], r3.at[n, rows], sends.at[n], lands.at[n], spots[n]
            )
            copy.start()
            copies.append(copy)
    needs = {-1: pl.ds(0, 40), 0: pl.ds(16, 24), 1: pl.ds(32, 8)}

    def pass_on(deltas):
        for n, (delta, j, to) in enumerate(near):
            if delta in deltas:
                part = gath.at[1, member, needs[delta]]
                there = gath.at[1 - delta, member, needs[delta]]
                copy = remote(part, there, s5.at[n], t5.at[1 - delta, member], to)
                copy.start()
                copies.append(copy)

    for rows, start, size, sends, lands in parts:
        for n in range(15):
            remote(r3.at[n, rows], r3.at[n, rows], sends.at[n], lands.at[n], sib).wait_recv()
        at = pl.ds(pl.multiple_of(y // 2 * 40 + start, 8), size)
        terms = [a2[b * 2 + y % 2, at]] + [r3[n, rows] for n in range(15)]
        while len(terms) > 1:
            terms = [u + v for u, v in zip(terms[::2], terms[1::2])]
        gath[1, member, rows] = terms[0]
        pass_on((1,) if start else (-1, 0))

    def arrived(deltas):
        for delta, j, _ in near:
            if delta in deltas:
                part = gath.at[1 - delta, (member + j) % 4, needs[delta]]
                remote(part, part, s5.at[0], t5.at[1 - delta, (member + j) % 4], sib).wait_recv()

    arrived((1,))

    def others():
        arrived((-1, 0))
        share.start()
        copies.append(share)

    wall[bin_] = solve(gath, steer_ref, bin_ % 2, others)
    share.wait_recv()
    sr[0:2] = sr[32:34]
    sr[34] = sr[2]
    side = bin_ // 2 % 2
    for n, step in enumerate((4, 3, 5, 2, 6, 1, 7, 0)):
        for e in range(2):
            to = (bin_ // 4 + step) % 8 * 4 + core * 2 + e

            @pl.when(to != bin_)
            def _(n=n, e=e, to=to):
                remote(
                    wall.at[bin_], wall.at[bin_], s6.at[2 * n + e], t6.at[bin_],
                    at_home(to, member // 2 * 2 + side),
                ).start()

    for step in (0, 1, 7, 2, 6, 3, 5, 4):
        first = (bin_ // 4 + step) % 8 * 4 + core * 2
        at = pl.ds(first, 2)
        for e in range(2):

            @pl.when(first + e != bin_)
            def _(q=first + e):
                remote(wall.at[q], wall.at[q], s6.at[0], t6.at[q], sib).wait_recv()

        copy = remote(wall.at[at], passed.at[at], s4b.at[step], t4b.at[step], sib)
        copy.start()
        copies.append(copy)
        beam_pair(first, wall, s, sr, table)
    for step in (0, 1, 7, 2, 6, 3, 5, 4):
        first = (bin_ // 4 + step) % 8 * 4 + 2 - core * 2
        at = pl.ds(first, 2)
        remote(wall.at[at], passed.at[at], s4b.at[step], t4b.at[step], sib).wait_recv()
        beam_pair(first, passed, s, sr, table)
    for n, step in enumerate((4, 3, 5, 2, 6, 1, 7, 0)):
        for e in range(2):

            @pl.when((bin_ // 4 + step) % 8 * 4 + core * 2 + e != bin_)
            def _(n=n, e=e):
                remote(wall.at[bin_], wall.at[bin_], s6.at[2 * n + e], t6.at[bin_], sib).wait_send()

    slots[...] = (
        jnp.dot(select[...], table[...], preferred_element_type=F32)
        .astype(BF16)
        .reshape(16, 16, 256)
    )
    for j, q in enumerate(planes):
        copy = remote(slots.at[q], d1.at[zx], s7.at[j], t7.at[j], q * 8 + yc)
        copy.start()
        copies.append(copy)
    d1[zx] = slots[zx]
    for j, q in enumerate(froms):
        remote(slots.at[q], d1.at[q], s7.at[j], t7.at[j], sib).wait_recv()
    mid[...] = (
        jnp.dot(turn[...], d1[...].reshape(256, 256), preferred_element_type=F32)
        .astype(BF16)
        .reshape(8, 32, 256)
    )
    for j, q in enumerate(posts):
        copy = remote(mid.at[q], d2.at[yc], s8.at[j], t8.at[j], zx * 8 + q)
        copy.start()
        copies.append(copy)
    d2[yc] = mid[yc]
    for j, step in enumerate(POSTS):
        q = (yc + 8 - step) % 8
        remote(mid.at[q], d2.at[q], s8.at[j], t8.at[j], sib).wait_recv()
    rows = jnp.dot(back[...], d2[...].reshape(256, 256), preferred_element_type=F32)
    out_ref[...] = rows.astype(BF16)
    finish()


def program(raw, replica, det_bin, det_block, det_beam, owner):
    dma = pltpu.SemaphoreType.DMA
    vm = pltpu.VMEM
    rows = (1, 128)
    return pl.pallas_call(
        kernel,
        out_shape=jax.ShapeDtypeStruct((256, 256), BF16),
        in_specs=[HBM] * 8,
        out_specs=VMEM,
        scratch_shapes=[
            vm((2, 64, 32, 256), BF16),
            vm((64, 32, 128), BF16),
            vm((64, 32, 128), BF16),
            vm((64, 32, 128), BF16),
            vm((64, 32, 128), BF16),
            vm((64, 32, 384), BF16),
            vm((64, 32, 384), BF16),
            vm((512, 256), BF16),
            vm((512, 256), BF16),
            vm((35, 64, 512), BF16),
            vm((32, 64, 128), BF16),
            vm((35, 64, 128), BF16),
            vm((2, 32, 80, 128), F32),
            vm((32, 80, 128), F32),
            vm((32, 80, 128), F32),
            vm((3, 4, 80, 128), F32),
            vm((3, 4, 80, 128), F32),
            vm((8, 80, 128), F32),
            vm((15, 40, 128), F32),
            vm((3, 4, 40, 128), F32),
            vm((32, 16, 256), BF16),
            vm((32, 16, 256), BF16),
            vm((512, 256), BF16),
            vm((256, 512), BF16),
            vm((256, 256), BF16),
            vm((256, 256), BF16),
            vm((16, 16, 256), BF16),
            vm((16, 16, 256), BF16),
            vm((8, 32, 256), BF16),
            vm((8, 32, 256), BF16),
            vm((2, 128), BF16),
            vm((512, 512), BF16),
            vm((8, 128), F32),
            vm(rows, jnp.int32), vm(rows, jnp.int32), vm(rows, jnp.int32), vm(rows, jnp.int32),
            dma((4,)), dma((7,)), dma((2, 4)), dma((2, 4)),
            dma((4,)), dma((4,)), dma((6,)), dma((6,)), dma((15,)), dma((15,)),
            dma((15,)), dma((15,)), dma((11,)), dma((3, 4)), dma((31,)), dma((32,)),
            dma((15,)), dma((15,)), dma((7,)), dma((7,)), dma(()), dma(()), dma((8,)), dma((8,)),
        ],
        compiler_params=pltpu.CompilerParams(
            collective_id=0, has_side_effects=True, vmem_limit_bytes=LIMIT
        ),
        name="stap",
    )(
        raw, replica, jnp.asarray(dft_matrix()), jnp.asarray(steer_rows()),
        det_bin, det_block, det_beam, owner,
    )


def on_device(raw, replica, det_bin, det_block, det_beam, det_owner):
    rows = [v.reshape(1, 128) for v in (det_bin, det_block, det_beam, det_owner)]
    return program(raw, replica, *rows).astype(F32)


def solution(mesh):
    in_specs = (
        P(None, None, None, "range"),
        P(),
        P("range"),
        P("range"),
        P("range"),
        P("range", None),
    )
    return jax.shard_map(
        on_device,
        mesh=mesh,
        in_specs=in_specs,
        out_specs=P("range", None),
        check_vma=False,
    )
```
